32 devices in a mesh: fsdp: 8 (over y, x, core), ctx: 4 (over z).
Axes of the slice: x: 2, y: 2, z: 4, core: 2. Of those that a mesh axis runs over, the one named last changes fastest.
Arguments:
- tokens: bfloat16 [8, 512, 1024], P('fsdp', 'ctx'), may hold values from -6 to 6
- segment_ids: int32 [8, 512], P('fsdp'), may hold values from 0 to 2, as said below
- group_order: int32 [4], replicated, may hold values from 0 to 3, each once
- ln1_gain: bfloat16 [2, 1024], P(None, ('fsdp', 'ctx')), may hold values from 0.5 to 1.5
- ln1_bias: bfloat16 [2, 1024], P(None, ('fsdp', 'ctx')), may hold values from -2 to 2
- qkv_weight: bfloat16 [2, 1024, 3072], P(None, ('fsdp', 'ctx')), may hold values from -0.1875 to 0.1875
- qv_bias: bfloat16 [2, 2048], P(None, ('fsdp', 'ctx')), may hold values from -3 to 3
- out_weight: bfloat16 [2, 1024, 1024], P(None, ('fsdp', 'ctx')), may hold values from -0.5 to 0.5
- out_bias: bfloat16 [2, 1024], P(None, ('fsdp', 'ctx')), may hold values from -2 to 2
- ln2_gain: bfloat16 [2, 1024], P(None, ('fsdp', 'ctx')), may hold values from 0.5 to 1.5
- ln2_bias: bfloat16 [2, 1024], P(None, ('fsdp', 'ctx')), may hold values from -2 to 2
- up_weight: bfloat16 [2, 1024, 4096], P(None, ('fsdp', 'ctx')), may hold values from -0.1875 to 0.1875
- up_bias: bfloat16 [2, 4096], P(None, ('fsdp', 'ctx')), may hold values from -3 to 3
- down_weight: bfloat16 [2, 4096, 1024], P(None, ('fsdp', 'ctx')), may hold values from -0.09375 to 0.09375
- down_bias: bfloat16 [2, 1024], P(None, ('fsdp', 'ctx')), may hold values from -2 to 2
- cotangent: bfloat16 [8, 512, 1024], P('fsdp', 'ctx'), may hold values from -6 to 6
Outputs:
- output: bfloat16 [8, 512, 1024], P('fsdp', 'ctx')
- tokens_grad: float32 [8, 512, 1024], P('fsdp', 'ctx')
- grad_ln1_gain: float32 [2, 1024], P(None, ('fsdp', 'ctx'))
- grad_ln1_bias: float32 [2, 1024], P(None, ('fsdp', 'ctx'))
- grad_qkv_weight: float32 [2, 1024, 3072], P(None, ('fsdp', 'ctx'))
- grad_qv_bias: float32 [2, 2048], P(None, ('fsdp', 'ctx'))
- grad_out_weight: float32 [2, 1024, 1024], P(None, ('fsdp', 'ctx'))
- grad_out_bias: float32 [2, 1024], P(None, ('fsdp', 'ctx'))
- grad_ln2_gain: float32 [2, 1024], P(None, ('fsdp', 'ctx'))
- grad_ln2_bias: float32 [2, 1024], P(None, ('fsdp', 'ctx'))
- grad_up_weight: float32 [2, 1024, 4096], P(None, ('fsdp', 'ctx'))
- grad_up_bias: float32 [2, 4096], P(None, ('fsdp', 'ctx'))
- grad_down_weight: float32 [2, 4096, 1024], P(None, ('fsdp', 'ctx'))
- grad_down_bias: float32 [2, 1024], P(None, ('fsdp', 'ctx'))
The draws below stay inside these ranges and needn't reach their ends.
Inputs may be any that keep to these rules, and one draw needn't show every extreme that they name: `segment_ids`: in each stream the ids never fall with position; document 0 ends before position 64, document 2 begins after position 448 and is never empty. A permutation; index c of ctx holds the position blocks group_order[c] and 7 - group_order[c].
All inputs are finite; a program needn't handle non-finite values.
Results may differ from the reference program's by a relative error of at most 0.02.
Values may be sent and summed in bfloat16 or wider, within the bound.
No kernel may reach another device: no remote copies, remote signals or barrier semaphores. Data moves between devices by JAX's collectives and lax.ppermute only.
A program may use at most 320 MiB of HBM per device.

```python
import jax
import jax.numpy as jnp
from jax import lax

D = 1024
HEADS = 16
HEAD_DIM = 64
FF = 4096
GROUP = 128
LAYERS = 2
STREAM = 512
STREAMS = 8
N_CTX = 4


def draw_segment_ids(key, part):
    key = jax.random.fold_in(key, 7)
    first_key, last_key = jax.random.split(key)
    opening = jax.random.randint(first_key, (STREAMS,), 1, GROUP // 2)
    closing = jax.random.randint(last_key, (STREAMS,), 1, GROUP // 2)
    position = jnp.arange(STREAM, dtype=jnp.int32)
    lower_part = (position[None, :] >= opening[:, None]).astype(jnp.int32)
    upper_part = (position[None, :] >= STREAM - closing[:, None]).astype(jnp.int32)
    return lower_part + upper_part


def shard_levels(stream_key, shape, cuts, low, high):
    def one(axis_at, parts):
        draws = jax.random.uniform(jax.random.fold_in(jax.random.fold_in(stream_key, 6), axis_at), (parts,), jnp.float32, low / len(cuts), high / len(cuts))
        return jnp.repeat(jnp.exp(draws), shape[axis_at] // parts).reshape((-1,) + (1,) * (len(shape) - axis_at - 1))

    loudness = one(*cuts[0])
    for cut in cuts[1:]:
        loudness = loudness * one(*cut)
    return loudness


def normal_values(stream_key, shape, scale, most, cuts=(), held_as=jnp.bfloat16):
    values = jax.random.normal(stream_key, shape, jnp.float32) * scale
    if len(cuts) > 0:
        values = shard_levels(stream_key, shape, cuts, -0.22, 0.18) * values
    return jnp.clip(values, min=-most, max=most).astype(held_as)


def setup_inputs(seed: int = 0) -> dict:
    streams_of = jax.random.split(jax.random.key(seed), 17)
    tokens = normal_values(streams_of[0], (STREAMS, STREAM, D), 1.0, 6.0, ((0, 8), (1, 4)))
    segment_ids = draw_segment_ids(jax.random.fold_in(streams_of[16], 71), 0)
    group_order = jax.random.permutation(streams_of[2], N_CTX).astype(jnp.int32)
    ln1_gain = jnp.clip(1.0 + 0.1 * jax.random.normal(streams_of[3], (LAYERS, D), jnp.float32), 0.5, 1.5).astype(jnp.bfloat16)
    ln1_bias = normal_values(streams_of[4], (LAYERS, D), 0.3, 2.0, ((1, 32),))
    qkv_weight = normal_values(streams_of[5], (LAYERS, D, 3 * D), D ** -0.5, 0.1875, ((1, 32),))
    qv_bias = normal_values(streams_of[6], (LAYERS, 2 * D), 0.5, 3.0, ((1, 32),))
    out_weight = normal_values(streams_of[7], (LAYERS, D, D), (D // 8) ** -0.5, 0.5, ((1, 32),))
    out_bias = normal_values(streams_of[8], (LAYERS, D), 0.3, 2.0, ((1, 32),))
    ln2_gain = jnp.clip(1.0 + 0.1 * jax.random.normal(streams_of[9], (LAYERS, D), jnp.float32), 0.5, 1.5).astype(jnp.bfloat16)
    ln2_bias = normal_values(streams_of[10], (LAYERS, D), 0.3, 2.0, ((1, 32),))
    up_weight = normal_values(streams_of[11], (LAYERS, D, FF), D ** -0.5, 0.1875, ((1, 32),))
    up_bias = normal_values(streams_of[12], (LAYERS, FF), 0.5, 3.0, ((1, 32),))
    down_weight = normal_values(streams_of[13], (LAYERS, FF, D), FF ** -0.5, 0.09375, ((1, 32),))
    down_bias = normal_values(streams_of[14], (LAYERS, D), 0.3, 2.0, ((1, 32),))
    cotangent = normal_values(streams_of[15], (STREAMS, STREAM, D), 1.0, 6.0, ((0, 8), (1, 4)))
    return dict(tokens=tokens, segment_ids=segment_ids, group_order=group_order, ln1_gain=ln1_gain, ln1_bias=ln1_bias, qkv_weight=qkv_weight, qv_bias=qv_bias, out_weight=out_weight, out_bias=out_bias, ln2_gain=ln2_gain, ln2_bias=ln2_bias, up_weight=up_weight, up_bias=up_bias, down_weight=down_weight, down_bias=down_bias, cotangent=cotangent)


EPSILON = 1e-05
PRECISE = lax.Precision.HIGHEST

@jax.custom_vjp
def low(v):
    return lax.optimization_barrier(v.astype(jnp.bfloat16)).astype(jnp.float32)

@jax.custom_vjp
def low_back(v):
    return v

def low_keep(v):
    return (low(v), None)

def low_pass(kept, grad):
    return (grad,)

def back_keep(v):
    return (v, None)

def back_low(kept, grad):
    return (low(grad),)
low.defvjp(low_keep, low_pass)
low_back.defvjp(back_keep, back_low)

def norm_rows(values, gain, shift):
    row_mean = lax.optimization_barrier(jnp.mean(values, axis=-1, keepdims=True))
    centred = values - row_mean
    row_var = lax.optimization_barrier(jnp.mean(centred * centred, axis=-1, keepdims=True))
    return centred * lax.rsqrt(row_var + EPSILON) * gain + shift

def head_slopes():
    head_index = jnp.arange(HEADS, dtype=jnp.float32)
    return jnp.exp2(-8.0 * (head_index + 1.0) / HEADS)

def layout_places(group_order):
    rows = jnp.arange(STREAM, dtype=jnp.int32)
    half = GROUP // 2
    owner = rows // GROUP
    within = rows % GROUP
    lead = jnp.take(group_order, owner).astype(jnp.int32)
    block = jnp.where(within < half, lead, 2 * N_CTX - 1 - lead)
    return (block * half + within % half).astype(jnp.int32)

def attend(queries, key_rows, value_rows, segments, places):
    length = queries.shape[0]
    query_h = queries.reshape(length, HEADS, HEAD_DIM)
    key_h = key_rows.reshape(length, HEADS, HEAD_DIM)
    value_h = value_rows.reshape(length, HEADS, HEAD_DIM)
    scores = jnp.einsum('qhd,khd->hqk', query_h, key_h, precision=PRECISE) * HEAD_DIM ** (-0.5)
    row_seg = jnp.take(segments, places)
    distance = places[:, None] - places[None, :]
    allowed = (distance >= 0) & (row_seg[:, None] == row_seg[None, :])
    scores = scores - head_slopes()[:, None, None] * distance.astype(jnp.float32)[None]
    scores = low_back(scores)
    scores = jnp.where(allowed[None], scores, -1e+30)
    weights = low(jax.nn.softmax(scores, axis=-1))
    mixed = jnp.einsum('hqk,khd->qhd', weights, value_h, precision=PRECISE)
    return mixed.reshape(length, HEADS * HEAD_DIM)

def project(values, matrix):
    return jnp.einsum('nsd,de->nse', values, matrix, precision=PRECISE)

def forward(segment_ids, places, tokens, ln1_gain, ln1_bias, qkv_weight, qv_bias, out_weight, out_bias, ln2_gain, ln2_bias, up_weight, up_bias, down_weight, down_bias):
    residual = tokens
    checked = jax.checkpoint(attend)
    for layer_no in range(ln1_gain.shape[0]):
        normed = low(norm_rows(residual, ln1_gain[layer_no], ln1_bias[layer_no]))
        bias_full = jnp.concatenate([qv_bias[layer_no][:D], jnp.zeros((D,), jnp.float32), qv_bias[layer_no][D:]])
        qkv = low(low_back(project(normed, qkv_weight[layer_no]) + bias_full))
        attended = lax.map(lambda stream_item: checked(stream_item[0], stream_item[1], stream_item[2], stream_item[3], places), (qkv[:, :, :D], qkv[:, :, D:2 * D], qkv[:, :, 2 * D:], segment_ids))
        attended = low(low_back(attended))
        residual = residual + low_back(project(attended, out_weight[layer_no]) + out_bias[layer_no])
        normed_two = low(norm_rows(residual, ln2_gain[layer_no], ln2_bias[layer_no]))
        pre_act = low_back(project(normed_two, up_weight[layer_no]) + up_bias[layer_no])
        hidden = low(jax.nn.gelu(pre_act, approximate=True))
        residual = residual + low_back(project(hidden, down_weight[layer_no]) + down_bias[layer_no])
    return residual

def reference(tokens, segment_ids, group_order, ln1_gain, ln1_bias, qkv_weight, qv_bias, out_weight, out_bias, ln2_gain, ln2_bias, up_weight, up_bias, down_weight, down_bias, cotangent):
    params = [ln1_gain, ln1_bias, qkv_weight, qv_bias, out_weight, out_bias, ln2_gain, ln2_bias, up_weight, up_bias, down_weight, down_bias]
    floats = [param.astype(jnp.float32) for param in params]
    places = layout_places(group_order)

    def wrapped(token_vals, *param_vals):
        return forward(segment_ids, places, token_vals, *param_vals)
    result, pullback = jax.vjp(wrapped, tokens.astype(jnp.float32), *floats)
    grads = pullback(cotangent.astype(jnp.float32))
    return (result.astype(jnp.bfloat16), grads[0], grads[1], grads[2], grads[3], grads[4], grads[5], grads[6], grads[7], grads[8], grads[9], grads[10], grads[11], grads[12])
```

```python
import jax
import jax.numpy as jnp
from jax import lax
from jax.sharding import Mesh, PartitionSpec as P

HEADS = 16
EPSILON = 1e-05
BF = jnp.bfloat16
F32 = jnp.float32
AXES = ("y", "x", "core", "zh", "zl")


def here(axis):
    return lax.axis_index(axis)


def swap(value, axis):
    return lax.ppermute(value, axis, [(0, 1), (1, 0)])


def ordered(mine, other, axis):
    first = here(axis) == 0
    return jnp.stack([jnp.where(first, mine, other), jnp.where(first, other, mine)])


def pick(value, axis):
    return lax.dynamic_index_in_dim(value, here(axis), 0, keepdims=False)


def pick_other(value, axis):
    return lax.dynamic_index_in_dim(value, 1 - here(axis), 0, keepdims=False)


def trade(value, axis):
    if lax.axis_size(axis) == 2:
        return ordered(pick(value, axis), swap(pick_other(value, axis), axis), axis)
    return lax.all_to_all(value, axis, 0, 0, tiled=True)


def collect(value, axis):
    if lax.axis_size(axis) == 2:
        return ordered(value, swap(value, axis), axis)
    return lax.all_gather(value, axis, axis=0, tiled=False)


def reduce_to(value, axis):
    if lax.axis_size(axis) == 2:
        return pick(value, axis) + swap(pick_other(value, axis), axis)
    return lax.psum_scatter(value, axis, scatter_dimension=0, tiled=False)


def flipped(value, axis, dim):
    return jnp.where(here(axis) == 0, value, jnp.flip(value, dim))


def gather_shards(shard):
    if lax.axis_size("y") != 2:
        return lax.all_gather(shard, ("y", "x", "zh"), axis=0, tiled=False)
    far = swap(shard, "zh")
    near_x = swap(shard, "x")
    far_y = swap(far, "y")
    near_y = swap(shard, "y")
    near_xy = swap(near_x, "y")
    far_x = swap(far, "x")
    far_yx = swap(far_y, "x")
    rel = jnp.stack([shard, far, near_x, far_x, near_y, far_y, near_xy, far_yx])
    rel = rel.reshape((2, 2, 2) + shard.shape)
    rel = flipped(flipped(flipped(rel, "y", 0), "x", 1), "zh", 2)
    return rel.reshape((8,) + shard.shape)


def scatter_shards(grads):
    shape = grads.shape[1:]
    if lax.axis_size("y") != 2:
        return lax.psum_scatter(
            grads, ("y", "x", "zh"), scatter_dimension=0, tiled=False
        )
    rel = grads.reshape((2, 2, 2) + shape)
    rel = flipped(flipped(flipped(rel, "y", 0), "x", 1), "zh", 2)
    near, far = rel[:, :, 0], rel[:, :, 1]
    far = far[:, 0] + swap(far[:, 1].astype(BF), "x").astype(F32)
    near = near[0] + swap(near[1].astype(BF), "y").astype(F32)
    far = far[0] + swap(far[1].astype(BF), "y").astype(F32)
    near = near[0] + swap(near[1].astype(BF), "x").astype(F32)
    return near + swap(far.astype(BF), "zh").astype(F32)


def corner_turn(value):
    return lax.ppermute(value, ("core", "zh"), [(0, 0), (1, 2), (2, 1), (3, 3)])


def norm_rows(values, gain, shift):
    row_mean = jnp.mean(values, axis=-1, keepdims=True)
    centred = values - row_mean
    row_var = jnp.mean(centred * centred, axis=-1, keepdims=True)
    return centred * lax.rsqrt(row_var + EPSILON) * gain + shift


def gelu_tanh(values):
    return jax.nn.gelu(values, approximate=True)


def dot(left, right):
    return jnp.dot(left, right, preferred_element_type=F32)


def dot_t(left, matrix):
    return lax.dot_general(
        left, matrix, (((1,), (1,)), ((), ())), preferred_element_type=F32
    )


def outer_sum(left, right):
    return jnp.einsum("td,te->de", left, right, preferred_element_type=F32)


def body(
    tokens,
    segment_ids,
    group_order,
    ln1_gain,
    ln1_bias,
    qkv_weight,
    qv_bias,
    out_weight,
    out_bias,
    ln2_gain,
    ln2_bias,
    up_weight,
    up_bias,
    down_weight,
    down_bias,
    cotangent,
):
    ny, nx, nc, nzh, nzl = (lax.axis_size(a) for a in AXES)
    chips = ny * nx
    span = chips // nzl
    layers, width = ln1_gain.shape[0], tokens.shape[2]
    hidden = up_weight.shape[2]
    group = tokens.shape[1]
    ctx_count = nzh * nzl
    rank_width = width // (nc * nzl)
    rank_hidden = hidden // (nc * nzl)
    head_size = width // HEADS
    rank_heads = rank_width // head_size
    quarter = width // (chips * nc)
    unit = width // (chips * nc * nzh)
    core_rows = nzl * group
    rows = nc * core_rows
    scale = head_size ** (-0.5)

    def inner(value):
        shape = value.shape
        value = value.reshape(shape[:-1] + (chips, 2, 2, unit))
        return jnp.swapaxes(value, -3, -2).reshape(shape)

    small = (ln1_gain, ln1_bias, out_bias, ln2_gain, ln2_bias, down_bias)
    small_all = small + (qv_bias, up_bias)
    packed = jnp.concatenate([v.reshape(-1) for v in small_all])
    for axis in reversed(AXES):
        packed = collect(packed, axis)
    vectors = []
    at = 0
    for v in small_all:
        size = v.shape[0] * v.shape[1]
        part = packed[..., at : at + size].reshape((ny, nx, nc, nzh, nzl) + v.shape)
        part = jnp.moveaxis(part, 5, 0)
        vectors.append(part.reshape(layers, -1).astype(F32))
        at += size
    vec = [inner(v) for v in vectors[:6]]
    full_qv, full_up = vectors[6], vectors[7]

    def rank_columns(value):
        shape = value.shape[:-1]
        value = value.reshape(shape + (nzl, span, nc, quarter))
        value = lax.dynamic_index_in_dim(value, here("zl"), len(shape), keepdims=False)
        value = lax.dynamic_index_in_dim(value, here("core"), len(shape) + 1, keepdims=False)
        return value.reshape(shape + (rank_width,))

    q_bias = rank_columns(full_qv[:, :width])
    v_bias = rank_columns(full_qv[:, width:])
    qkv_bias = jnp.concatenate([q_bias, jnp.zeros_like(q_bias), v_bias], axis=1)
    up_b = full_up.reshape(layers, chips, nc, nzh, nzl, -1)
    up_b = lax.dynamic_index_in_dim(up_b, here("zl"), 4, keepdims=False)
    up_b = lax.dynamic_index_in_dim(up_b, here("core"), 2, keepdims=False)
    up_b = up_b.reshape(layers, rank_hidden)

    def to_ranks(value):
        value = trade(value, "core")
        return jnp.swapaxes(trade(jnp.swapaxes(value, 0, 1), "zl"), 0, 1)

    def fetch(layer):
        w = qkv_weight[layer]
        n = w.shape[0]
        w = w.reshape(n, 3, nzl, span, nc, quarter)
        w = jnp.transpose(w, (4, 2, 0, 1, 3, 5)).reshape(nc, nzl, n, 3 * rank_width)
        w_qkv = gather_shards(to_ranks(w).reshape(-1, 3 * rank_width))
        w = gather_shards(inner(out_weight[layer]))
        w = trade(w.reshape(nzl, span, nzh, n, width), "zl")
        w_out = jnp.transpose(w, (1, 2, 0, 3, 4)).reshape(rank_width, width)
        w = up_weight[layer].reshape(n, chips, nc, nzh, nzl, -1)
        w = jnp.transpose(w, (2, 4, 0, 1, 3, 5)).reshape(nc, nzl, n, rank_hidden)
        w_up = gather_shards(to_ranks(w).reshape(-1, rank_hidden))
        w_down = gather_shards(inner(down_weight[layer]))
        return (
            w_qkv.reshape(width, 3 * rank_width),
            w_out,
            w_up.reshape(width, rank_hidden),
            w_down.reshape(rank_hidden, width),
        )

    def from_ranks(value):
        value = jnp.swapaxes(trade(jnp.swapaxes(value, 0, 1), "zl"), 0, 1)
        return trade(value, "core")

    def send(grads):
        g_qkv, g_out, g_up, g_down = grads
        n = width // (chips * 2 * ctx_count)
        g = scatter_shards(g_qkv.reshape(chips * nzh, -1, 3 * rank_width))
        g = from_ranks(g.astype(BF).reshape(nc, nzl, n, 3 * rank_width)).astype(F32)
        g = g.reshape(nc, nzl, n, 3, span, quarter)
        d_qkv = jnp.transpose(g, (2, 3, 1, 4, 0, 5)).reshape(n, 3 * width)
        g = g_out.astype(BF).reshape(span, nzh, nzl, n, width)
        g = trade(jnp.transpose(g, (2, 0, 1, 3, 4)), "zl").astype(F32)
        d_out = inner(scatter_shards(g.reshape(chips * nzh, n, width)))
        g = scatter_shards(g_up.reshape(chips * nzh, -1, rank_hidden))
        g = from_ranks(g.astype(BF).reshape(nc, nzl, n, rank_hidden)).astype(F32)
        g = g.reshape(nc, nzl, n, chips, nzh, -1)
        d_up = jnp.transpose(g, (2, 3, 0, 4, 1, 5)).reshape(n, hidden)
        d_down = inner(scatter_shards(g_down.reshape(chips * nzh, -1, width)))
        return d_qkv, d_out, d_up, d_down

    def own_columns(value, mine):
        value = inner(value).reshape(ny, nx, nc, nzh, nzl, -1)
        keep = jnp.arange(nzl)[:, None] == here("zl")
        return jnp.where(keep, value, 0.0)

    def send_small(sums):
        g1, b1, gqv, bo, g2, b2, bu, bd = sums
        parts = [own_columns(v, None) for v in (g1, b1, bo, g2, b2, bd)]

        def placed(value):
            value = value.reshape(1, span, 1, quarter)
            keep = (jnp.arange(nzl)[:, None, None, None] == here("zl")) & (
                jnp.arange(nc)[None, None, :, None] == here("core")
            )
            return jnp.where(keep, value, 0.0).reshape(width)

        qv = jnp.concatenate([placed(gqv[0]), placed(gqv[1])])
        parts.append(qv.reshape(ny, nx, nc, nzh, nzl, -1))
        up = bu.reshape(ny, nx, 1, nzh, 1, -1)
        keep = (jnp.arange(nzl)[:, None] == here("zl")) & (
            jnp.arange(nc)[:, None, None, None] == here("core")
        )
        parts.append(jnp.where(keep, up, 0.0))
        value = jnp.concatenate(parts, axis=-1)
        for axis in AXES:
            value = reduce_to(value, axis)
        sizes = [p.shape[-1] for p in parts]
        cut, at = [], 0
        for s in sizes:
            cut.append(value[at : at + s])
            at += s
        g1, b1, bo, g2, b2, bd, qv, up = cut
        return g1, b1, qv, bo, g2, b2, up, bd

    def place(value):
        return collect(inner(corner_turn(value)), "zl").reshape(core_rows, width)

    def both_cores(value):
        return collect(value, "core").reshape(rows, -1)

    def total(partial):
        part = partial.reshape(nc, core_rows, width)
        part = pick(part, "core") + swap(pick_other(part, "core").astype(BF), "core").astype(F32)
        if nzl == 2:
            return part + swap(part.astype(BF), "zl").astype(F32)
        return lax.psum(part, "zl")

    seg = collect(segment_ids[0], "core")
    seg = lax.dynamic_index_in_dim(seg, here("zh"), 0, keepdims=False)
    half = group // 2
    block = jnp.stack([group_order, 2 * ctx_count - 1 - group_order], axis=1)
    pos = (block[:, :, None] * half + jnp.arange(half, dtype=jnp.int32)).reshape(rows)
    row_seg = jnp.take(seg, pos)
    distance = pos[:, None] - pos[None, :]
    allowed = (distance >= 0) & (row_seg[:, None] == row_seg[None, :])
    distance = distance.astype(F32)
    head_no = jnp.arange(rank_heads)
    head_no = (
        (here("zl") * span + head_no // (quarter // head_size)) * nc + here("core")
    ) * (quarter // head_size) + head_no % (quarter // head_size)
    slopes = jnp.exp2(-8.0 * (head_no.astype(F32) + 1.0) / HEADS)

    def scores_of(q, k):
        s = jnp.einsum("qhd,khd->hqk", q, k, preferred_element_type=F32) * scale
        return s - slopes[:, None, None] * distance[None]

    def split(qkv):
        return [
            v.reshape(rows, rank_heads, head_size) for v in jnp.split(qkv, 3, axis=1)
        ]

    weights = [fetch(layer) for layer in range(layers)]
    x = place(tokens[0]).astype(F32)
    kept = []
    for layer in range(layers):
        w_qkv, w_out, w_up, w_down = weights[layer]
        g1, b1, bo, g2, b2, bd = (v[layer] for v in vec)
        h1 = both_cores(norm_rows(x, g1, b1).astype(BF))
        qkv = (dot(h1, w_qkv) + qkv_bias[layer]).astype(BF)
        q, k, v = split(qkv)
        s = jnp.where(allowed, scores_of(q, k), -1e30)
        top = jnp.max(s, axis=-1, keepdims=True)
        p = jnp.where(allowed, jnp.exp(s - top), 0.0)
        den = jnp.sum(p, axis=-1, keepdims=True)
        p = p / den
        o = jnp.einsum("hqk,khd->qhd", p.astype(BF), v, preferred_element_type=F32)
        log_total = top + jnp.log(den)
        o = o.reshape(rows, rank_width).astype(BF)
        x1 = x + total(dot(o, w_out)) + bo
        h2 = both_cores(norm_rows(x1, g2, b2).astype(BF))
        u = dot(h2, w_up) + up_b[layer]
        a = gelu_tanh(u).astype(BF)
        x2 = x1 + total(dot(a, w_down)) + bd
        kept.append((x, h1, qkv, log_total, o, x1, h2, u, a))
        x = x2

    def leave(value):
        mine = lax.dynamic_index_in_dim(
            value.reshape(nzl, group, width), here("zl"), 0, keepdims=False
        )
        return corner_turn(inner(mine))[None]

    final_rows = leave(x.astype(BF))

    gx = place(cotangent[0]).astype(F32)
    result = [None] * layers
    for layer in reversed(range(layers)):
        w_qkv, w_out, w_up, w_down = weights[layer]
        g1, b1, bo, g2, b2, bd = (v[layer] for v in vec)
        x, h1, qkv, log_total, o, x1, h2, u, a = kept[layer]
        gy2_mine = gx.astype(BF)
        gy2 = both_cores(gy2_mine)
        d_down = outer_sum(a, gy2)
        d_bd = jnp.sum(gy2_mine.astype(F32), axis=0)
        _, gelu_back = jax.vjp(gelu_tanh, u)
        gu = gelu_back(dot_t(gy2, w_down))[0].astype(BF)
        d_up = outer_sum(h2, gu)
        d_bu = jnp.sum(gu.astype(F32), axis=0)
        _, back = jax.vjp(norm_rows, x1, g2, b2)
        gn, d_g2, d_b2 = back(total(dot_t(gu, w_up)))
        gm = gx + gn
        gy1_mine = gm.astype(BF)
        gy1 = both_cores(gy1_mine)
        d_out = outer_sum(o, gy1)
        d_bo = jnp.sum(gy1_mine.astype(F32), axis=0)
        go_f = dot_t(gy1, w_out)
        go = go_f.astype(BF).reshape(rows, rank_heads, head_size)
        q, k, v = split(qkv)
        p = jnp.where(allowed, jnp.exp(scores_of(q, k) - log_total), 0.0)
        dp = jnp.einsum("qhd,khd->hqk", go, v, preferred_element_type=F32)
        ds = (p * (dp - jnp.sum(dp * p, axis=-1, keepdims=True))).astype(BF)
        gq = scale * jnp.einsum("hqk,khd->qhd", ds, k, preferred_element_type=F32)
        gk = scale * jnp.einsum("hqk,qhd->khd", ds, q, preferred_element_type=F32)
        gv = jnp.einsum("hqk,qhd->khd", p.astype(BF), go, preferred_element_type=F32)
        gqkv = jnp.concatenate(
            [g.reshape(rows, rank_width) for g in (gq, gk, gv)], axis=1
        ).astype(BF)
        d_qkv = outer_sum(h1, gqkv)
        sums = jnp.sum(gqkv.astype(F32), axis=0)
        _, back = jax.vjp(norm_rows, x, g1, b1)
        gn, d_g1, d_b1 = back(total(dot_t(gqkv, w_qkv)))
        gx = gm + gn
        d_qv = (sums[:rank_width], sums[2 * rank_width :])
        big = send((d_qkv, d_out, d_up, d_down))
        tiny = send_small((d_g1, d_b1, d_qv, d_bo, d_g2, d_b2, d_bu, d_bd))
        result[layer] = (
            tiny[0], tiny[1], big[0], tiny[2], big[1], tiny[3],
            tiny[4], tiny[5], big[2], tiny[6], big[3], tiny[7],
        )
    stacked = [jnp.stack([result[layer][i] for layer in range(layers)]) for i in range(12)]
    return (final_rows, leave(gx)) + tuple(stacked)


def solution(mesh):
    fsdp, ctx = mesh.shape["fsdp"], mesh.shape["ctx"]
    fine = Mesh(mesh.devices.reshape(fsdp // 4, 2, 2, 2, ctx // 2), AXES)
    stream, place = ("y", "x", "core"), ("zh", "zl")
    rows = P(stream, place, None)
    flat, deep = P(None, AXES), P(None, AXES, None)
    params = (flat, flat, deep, flat, deep, flat, flat, flat, deep, flat, deep, flat)
    in_specs = (rows, P(stream, None), P()) + params + (rows,)
    out_specs = (rows, rows) + params
    return jax.shard_map(body, mesh=fine, in_specs=in_specs, out_specs=out_specs, check_vma=False)
```

```python
import jax
import jax.numpy as jnp
from jax import lax
from jax.experimental import pallas as pl
from jax.experimental.pallas import tpu as pltpu
from jax.sharding import Mesh, PartitionSpec as P

HEADS = 16
EPSILON = 1e-05
BF = jnp.bfloat16
F32 = jnp.float32
AXES = ("y", "x", "core", "zh", "zl")


def here(axis):
    return lax.axis_index(axis)


def swap(value, axis):
    return lax.ppermute(value, axis, [(0, 1), (1, 0)])


def ordered(mine, other, axis):
    first = here(axis) == 0
    return jnp.stack([jnp.where(first, mine, other), jnp.where(first, other, mine)])


def pick(value, axis):
    return lax.dynamic_index_in_dim(value, here(axis), 0, keepdims=False)


def pick_other(value, axis):
    return lax.dynamic_index_in_dim(value, 1 - here(axis), 0, keepdims=False)


def trade(value, axis):
    if lax.axis_size(axis) == 2:
        return ordered(pick(value, axis), swap(pick_other(value, axis), axis), axis)
    return lax.all_to_all(value, axis, 0, 0, tiled=True)


def collect(value, axis):
    if lax.axis_size(axis) == 2:
        return ordered(value, swap(value, axis), axis)
    return lax.all_gather(value, axis, axis=0, tiled=False)


def reduce_to(value, axis):
    if lax.axis_size(axis) == 2:
        return pick(value, axis) + swap(pick_other(value, axis), axis)
    return lax.psum_scatter(value, axis, scatter_dimension=0, tiled=False)


def flipped(value, axis, dim):
    return jnp.where(here(axis) == 0, value, jnp.flip(value, dim))


def gather_shards(shard):
    if lax.axis_size("y") != 2:
        return lax.all_gather(shard, ("y", "x", "zh"), axis=0, tiled=False)
    far = swap(shard, "zh")
    near_x = swap(shard, "x")
    far_y = swap(far, "y")
    near_y = swap(shard, "y")
    near_xy = swap(near_x, "y")
    far_x = swap(far, "x")
    far_yx = swap(far_y, "x")
    rel = jnp.stack([shard, far, near_x, far_x, near_y, far_y, near_xy, far_yx])
    rel = rel.reshape((2, 2, 2) + shard.shape)
    rel = flipped(flipped(flipped(rel, "y", 0), "x", 1), "zh", 2)
    return rel.reshape((8,) + shard.shape)


def scatter_shards(grads):
    shape = grads.shape[1:]
    if lax.axis_size("y") != 2:
        return lax.psum_scatter(
            grads, ("y", "x", "zh"), scatter_dimension=0, tiled=False
        )
    rel = grads.reshape((2, 2, 2) + shape)
    rel = flipped(flipped(flipped(rel, "y", 0), "x", 1), "zh", 2)
    near, far = rel[:, :, 0], rel[:, :, 1]
    far = far[:, 0] + swap(far[:, 1].astype(BF), "x").astype(F32)
    near = near[0] + swap(near[1].astype(BF), "y").astype(F32)
    far = far[0] + swap(far[1].astype(BF), "y").astype(F32)
    near = near[0] + swap(near[1].astype(BF), "x").astype(F32)
    return near + swap(far.astype(BF), "zh").astype(F32)


def corner_turn(value):
    return lax.ppermute(value, ("core", "zh"), [(0, 0), (1, 2), (2, 1), (3, 3)])


def norm_rows(values, gain, shift):
    row_mean = jnp.mean(values, axis=-1, keepdims=True)
    centred = values - row_mean
    row_var = jnp.mean(centred * centred, axis=-1, keepdims=True)
    return centred * lax.rsqrt(row_var + EPSILON) * gain + shift


def gelu_tanh(values):
    return jax.nn.gelu(values, approximate=True)


def dot(left, right):
    return jnp.dot(left, right, preferred_element_type=F32)


def dot_t(left, matrix):
    return lax.dot_general(
        left, matrix, (((1,), (1,)), ((), ())), preferred_element_type=F32
    )


def outer_sum(left, right):
    return jnp.einsum("td,te->de", left, right, preferred_element_type=F32)


def wide_body(
    tokens,
    segment_ids,
    group_order,
    ln1_gain,
    ln1_bias,
    qkv_weight,
    qv_bias,
    out_weight,
    out_bias,
    ln2_gain,
    ln2_bias,
    up_weight,
    up_bias,
    down_weight,
    down_bias,
    cotangent,
):
    ny, nx, nc, nzh, nzl = (lax.axis_size(a) for a in AXES)
    chips = ny * nx
    span = chips // nzl
    layers, width = ln1_gain.shape[0], tokens.shape[2]
    hidden = up_weight.shape[2]
    group = tokens.shape[1]
    ctx_count = nzh * nzl
    rank_width = width // (nc * nzl)
    rank_hidden = hidden // (nc * nzl)
    head_size = width // HEADS
    rank_heads = rank_width // head_size
    quarter = width // (chips * nc)
    unit = width // (chips * nc * nzh)
    core_rows = nzl * group
    rows = nc * core_rows
    scale = head_size ** (-0.5)

    def inner(value):
        shape = value.shape
        value = value.reshape(shape[:-1] + (chips, 2, 2, unit))
        return jnp.swapaxes(value, -3, -2).reshape(shape)

    small = (ln1_gain, ln1_bias, out_bias, ln2_gain, ln2_bias, down_bias)
    small_all = small + (qv_bias, up_bias)
    packed = jnp.concatenate([v.reshape(-1) for v in small_all])
    for axis in reversed(AXES):
        packed = collect(packed, axis)
    vectors = []
    at = 0
    for v in small_all:
        size = v.shape[0] * v.shape[1]
        part = packed[..., at : at + size].reshape((ny, nx, nc, nzh, nzl) + v.shape)
        part = jnp.moveaxis(part, 5, 0)
        vectors.append(part.reshape(layers, -1).astype(F32))
        at += size
    vec = [inner(v) for v in vectors[:6]]
    full_qv, full_up = vectors[6], vectors[7]

    def rank_columns(value):
        shape = value.shape[:-1]
        value = value.reshape(shape + (nzl, span, nc, quarter))
        value = lax.dynamic_index_in_dim(value, here("zl"), len(shape), keepdims=False)
        value = lax.dynamic_index_in_dim(value, here("core"), len(shape) + 1, keepdims=False)
        return value.reshape(shape + (rank_width,))

    q_bias = rank_columns(full_qv[:, :width])
    v_bias = rank_columns(full_qv[:, width:])
    qkv_bias = jnp.concatenate([q_bias, jnp.zeros_like(q_bias), v_bias], axis=1)
    up_b = full_up.reshape(layers, chips, nc, nzh, nzl, -1)
    up_b = lax.dynamic_index_in_dim(up_b, here("zl"), 4, keepdims=False)
    up_b = lax.dynamic_index_in_dim(up_b, here("core"), 2, keepdims=False)
    up_b = up_b.reshape(layers, rank_hidden)

    def to_ranks(value):
        value = trade(value, "core")
        return jnp.swapaxes(trade(jnp.swapaxes(value, 0, 1), "zl"), 0, 1)

    def fetch(layer):
        w = qkv_weight[layer]
        n = w.shape[0]
        w = w.reshape(n, 3, nzl, span, nc, quarter)
        w = jnp.transpose(w, (4, 2, 0, 1, 3, 5)).reshape(nc, nzl, n, 3 * rank_width)
        w_qkv = gather_shards(to_ranks(w).reshape(-1, 3 * rank_width))
        w = gather_shards(inner(out_weight[layer]))
        w = trade(w.reshape(nzl, span, nzh, n, width), "zl")
        w_out = jnp.transpose(w, (1, 2, 0, 3, 4)).reshape(rank_width, width)
        w = up_weight[layer].reshape(n, chips, nc, nzh, nzl, -1)
        w = jnp.transpose(w, (2, 4, 0, 1, 3, 5)).reshape(nc, nzl, n, rank_hidden)
        w_up = gather_shards(to_ranks(w).reshape(-1, rank_hidden))
        w_down = gather_shards(inner(down_weight[layer]))
        return (
            w_qkv.reshape(width, 3 * rank_width),
            w_out,
            w_up.reshape(width, rank_hidden),
            w_down.reshape(rank_hidden, width),
        )

    def from_ranks(value):
        value = jnp.swapaxes(trade(jnp.swapaxes(value, 0, 1), "zl"), 0, 1)
        return trade(value, "core")

    def send(grads):
        g_qkv, g_out, g_up, g_down = grads
        n = width // (chips * 2 * ctx_count)
        g = scatter_shards(g_qkv.reshape(chips * nzh, -1, 3 * rank_width))
        g = from_ranks(g.astype(BF).reshape(nc, nzl, n, 3 * rank_width)).astype(F32)
        g = g.reshape(nc, nzl, n, 3, span, quarter)
        d_qkv = jnp.transpose(g, (2, 3, 1, 4, 0, 5)).reshape(n, 3 * width)
        g = g_out.astype(BF).reshape(span, nzh, nzl, n, width)
        g = trade(jnp.transpose(g, (2, 0, 1, 3, 4)), "zl").astype(F32)
        d_out = inner(scatter_shards(g.reshape(chips * nzh, n, width)))
        g = scatter_shards(g_up.reshape(chips * nzh, -1, rank_hidden))
        g = from_ranks(g.astype(BF).reshape(nc, nzl, n, rank_hidden)).astype(F32)
        g = g.reshape(nc, nzl, n, chips, nzh, -1)
        d_up = jnp.transpose(g, (2, 3, 0, 4, 1, 5)).reshape(n, hidden)
        d_down = inner(scatter_shards(g_down.reshape(chips * nzh, -1, width)))
        return d_qkv, d_out, d_up, d_down

    def own_columns(value, mine):
        value = inner(value).reshape(ny, nx, nc, nzh, nzl, -1)
        keep = jnp.arange(nzl)[:, None] == here("zl")
        return jnp.where(keep, value, 0.0)

    def send_small(sums):
        g1, b1, gqv, bo, g2, b2, bu, bd = sums
        parts = [own_columns(v, None) for v in (g1, b1, bo, g2, b2, bd)]

        def placed(value):
            value = value.reshape(1, span, 1, quarter)
            keep = (jnp.arange(nzl)[:, None, None, None] == here("zl")) & (
                jnp.arange(nc)[None, None, :, None] == here("core")
            )
            return jnp.where(keep, value, 0.0).reshape(width)

        qv = jnp.concatenate([placed(gqv[0]), placed(gqv[1])])
        parts.append(qv.reshape(ny, nx, nc, nzh, nzl, -1))
        up = bu.reshape(ny, nx, 1, nzh, 1, -1)
        keep = (jnp.arange(nzl)[:, None] == here("zl")) & (
            jnp.arange(nc)[:, None, None, None] == here("core")
        )
        parts.append(jnp.where(keep, up, 0.0))
        value = jnp.concatenate(parts, axis=-1)
        for axis in AXES:
            value = reduce_to(value, axis)
        sizes = [p.shape[-1] for p in parts]
        cut, at = [], 0
        for s in sizes:
            cut.append(value[at : at + s])
            at += s
        g1, b1, bo, g2, b2, bd, qv, up = cut
        return g1, b1, qv, bo, g2, b2, up, bd

    def place(value):
        return collect(inner(corner_turn(value)), "zl").reshape(core_rows, width)

    def both_cores(value):
        return collect(value, "core").reshape(rows, -1)

    def total(partial):
        part = partial.reshape(nc, core_rows, width)
        part = pick(part, "core") + swap(pick_other(part, "core").astype(BF), "core").astype(F32)
        if nzl == 2:
            return part + swap(part.astype(BF), "zl").astype(F32)
        return lax.psum(part, "zl")

    seg = collect(segment_ids[0], "core")
    seg = lax.dynamic_index_in_dim(seg, here("zh"), 0, keepdims=False)
    half = group // 2
    block = jnp.stack([group_order, 2 * ctx_count - 1 - group_order], axis=1)
    pos = (block[:, :, None] * half + jnp.arange(half, dtype=jnp.int32)).reshape(rows)
    row_seg = jnp.take(seg, pos)
    distance = pos[:, None] - pos[None, :]
    allowed = (distance >= 0) & (row_seg[:, None] == row_seg[None, :])
    distance = distance.astype(F32)
    head_no = jnp.arange(rank_heads)
    head_no = (
        (here("zl") * span + head_no // (quarter // head_size)) * nc + here("core")
    ) * (quarter // head_size) + head_no % (quarter // head_size)
    slopes = jnp.exp2(-8.0 * (head_no.astype(F32) + 1.0) / HEADS)

    def scores_of(q, k):
        s = jnp.einsum("qhd,khd->hqk", q, k, preferred_element_type=F32) * scale
        return s - slopes[:, None, None] * distance[None]

    def split(qkv):
        return [
            v.reshape(rows, rank_heads, head_size) for v in jnp.split(qkv, 3, axis=1)
        ]

    weights = [fetch(layer) for layer in range(layers)]
    x = place(tokens[0]).astype(F32)
    kept = []
    for layer in range(layers):
        w_qkv, w_out, w_up, w_down = weights[layer]
        g1, b1, bo, g2, b2, bd = (v[layer] for v in vec)
        h1 = both_cores(norm_rows(x, g1, b1).astype(BF))
        qkv = (dot(h1, w_qkv) + qkv_bias[layer]).astype(BF)
        q, k, v = split(qkv)
        s = jnp.where(allowed, scores_of(q, k), -1e30)
        top = jnp.max(s, axis=-1, keepdims=True)
        p = jnp.where(allowed, jnp.exp(s - top), 0.0)
        den = jnp.sum(p, axis=-1, keepdims=True)
        p = p / den
        o = jnp.einsum("hqk,khd->qhd", p.astype(BF), v, preferred_element_type=F32)
        log_total = top + jnp.log(den)
        o = o.reshape(rows, rank_width).astype(BF)
        x1 = x + total(dot(o, w_out)) + bo
        h2 = both_cores(norm_rows(x1, g2, b2).astype(BF))
        u = dot(h2, w_up) + up_b[layer]
        a = gelu_tanh(u).astype(BF)
        x2 = x1 + total(dot(a, w_down)) + bd
        kept.append((x, h1, qkv, log_total, o, x1, h2, u, a))
        x = x2

    def leave(value):
        mine = lax.dynamic_index_in_dim(
            value.reshape(nzl, group, width), here("zl"), 0, keepdims=False
        )
        return corner_turn(inner(mine))[None]

    final_rows = leave(x.astype(BF))

    gx = place(cotangent[0]).astype(F32)
    result = [None] * layers
    for layer in reversed(range(layers)):
        w_qkv, w_out, w_up, w_down = weights[layer]
        g1, b1, bo, g2, b2, bd = (v[layer] for v in vec)
        x, h1, qkv, log_total, o, x1, h2, u, a = kept[layer]
        gy2_mine = gx.astype(BF)
        gy2 = both_cores(gy2_mine)
        d_down = outer_sum(a, gy2)
        d_bd = jnp.sum(gy2_mine.astype(F32), axis=0)
        _, gelu_back = jax.vjp(gelu_tanh, u)
        gu = gelu_back(dot_t(gy2, w_down))[0].astype(BF)
        d_up = outer_sum(h2, gu)
        d_bu = jnp.sum(gu.astype(F32), axis=0)
        _, back = jax.vjp(norm_rows, x1, g2, b2)
        gn, d_g2, d_b2 = back(total(dot_t(gu, w_up)))
        gm = gx + gn
        gy1_mine = gm.astype(BF)
        gy1 = both_cores(gy1_mine)
        d_out = outer_sum(o, gy1)
        d_bo = jnp.sum(gy1_mine.astype(F32), axis=0)
        go_f = dot_t(gy1, w_out)
        go = go_f.astype(BF).reshape(rows, rank_heads, head_size)
        q, k, v = split(qkv)
        p = jnp.where(allowed, jnp.exp(scores_of(q, k) - log_total), 0.0)
        dp = jnp.einsum("qhd,khd->hqk", go, v, preferred_element_type=F32)
        ds = (p * (dp - jnp.sum(dp * p, axis=-1, keepdims=True))).astype(BF)
        gq = scale * jnp.einsum("hqk,khd->qhd", ds, k, preferred_element_type=F32)
        gk = scale * jnp.einsum("hqk,qhd->khd", ds, q, preferred_element_type=F32)
        gv = jnp.einsum("hqk,qhd->khd", p.astype(BF), go, preferred_element_type=F32)
        gqkv = jnp.concatenate(
            [g.reshape(rows, rank_width) for g in (gq, gk, gv)], axis=1
        ).astype(BF)
        d_qkv = outer_sum(h1, gqkv)
        sums = jnp.sum(gqkv.astype(F32), axis=0)
        _, back = jax.vjp(norm_rows, x, g1, b1)
        gn, d_g1, d_b1 = back(total(dot_t(gqkv, w_qkv)))
        gx = gm + gn
        d_qv = (sums[:rank_width], sums[2 * rank_width :])
        big = send((d_qkv, d_out, d_up, d_down))
        tiny = send_small((d_g1, d_b1, d_qv, d_bo, d_g2, d_b2, d_bu, d_bd))
        result[layer] = (
            tiny[0], tiny[1], big[0], tiny[2], big[1], tiny[3],
            tiny[4], tiny[5], big[2], tiny[6], big[3], tiny[7],
        )
    stacked = [jnp.stack([result[layer][i] for layer in range(layers)]) for i in range(12)]
    return (final_rows, leave(gx)) + tuple(stacked)


def bit(axis, flip):
    place = lax.axis_index(axis)
    return 1 - place if flip else place


def slot_places():
    for slot in range(8):
        yield slot, bit("y", slot & 4), bit("x", slot & 2), bit("zh", slot & 1)


def slot_blocks():
    return [(r, (y * 2 + x) * 2 + zh) for r, y, x, zh in slot_places()]


def at(block, size):
    return pl.ds(pl.multiple_of(block * size, size), size)


def run(kernel, outs, *ins, limit=40, flops=0):
    smem = pl.BlockSpec(memory_space=pltpu.SMEM)
    vmem = pl.BlockSpec(memory_space=pltpu.VMEM)
    scratch = getattr(kernel, "scratch", [])
    moved = sum(v.size * v.dtype.itemsize for v in list(ins) + list(outs))
    return pl.pallas_call(
        kernel,
        out_shape=tuple(outs),
        in_specs=[smem if v.size == 4 else vmem for v in ins],
        out_specs=tuple(vmem for _ in outs),
        scratch_shapes=scratch,
        compiler_params=pltpu.CompilerParams(vmem_limit_bytes=limit << 20),
        cost_estimate=pl.CostEstimate(flops=flops, bytes_accessed=moved, transcendentals=0),
    )(*ins)


def shape(*sizes, dtype=BF):
    return jax.ShapeDtypeStruct(sizes, dtype)


def with_scratch(kernel, *scratch):
    kernel.scratch = list(scratch)
    return kernel


def inner_columns(value):
    low = lax.broadcasted_iota(jnp.int32, (value.shape[0], 128), 1) < 64
    parts = []
    for i in range(0, value.shape[1], 256):
        a, b = value[:, i : i + 128], value[:, i + 128 : i + 256]
        parts.append(jnp.where(low, a, pltpu.roll(b, 64, 1)))
        parts.append(jnp.where(low, pltpu.roll(a, 64, 1), b))
    return jnp.concatenate(parts, axis=1)


def spread(value):
    n = value.shape[1]
    if n == 128:
        return value.astype(F32)
    hit = lax.broadcasted_iota(jnp.int32, (n, 128), 1) % n == lax.broadcasted_iota(
        jnp.int32, (n, 128), 0
    )
    return dot(value.astype(F32), hit.astype(F32))


RANKS = ((0, 0), (1, 0), (0, 1), (1, 1))


def qkv_blocks(core, zl):
    return [
        (s * 8 + zl * 4 + x * 2 + core, s * 2 + x) for s in range(3) for x in range(2)
    ]


def up_blocks(core, zl):
    return [
        (chip * 8 + core * 4 + zh * 2 + zl, chip * 2 + zh)
        for chip in range(4)
        for zh in range(2)
    ]


def prepare(g1, b1, bo, g2, b2, bd, qv, up, w_qkv, w_out, w_up, w_down, *outs):
    first, rest = outs[0:4], outs[4:8]
    out_a, out_b, down = outs[8:11]
    rows = [spread(v[...]) for v in (g1, b1, bo, g2, b2, bd, qv, up)]
    small = jnp.concatenate([v[l : l + 1] for l in range(2) for v in rows], axis=0)
    for i, (dc, dl) in enumerate(RANKS):
        core, zl = bit("core", dc), bit("zl", dl)
        for src, dst in qkv_blocks(core, zl):
            first[i][0:32, dst * 128 : dst * 128 + 128] = w_qkv[0, :, at(src, 128)]
            rest[i][:, 1024 + dst * 128 : 1152 + dst * 128] = w_qkv[1, :, at(src, 128)]
        for src, dst in up_blocks(core, zl):
            rest[i][:, dst * 128 : dst * 128 + 128] = w_up[0, :, at(src, 128)]
            rest[i][:, 1792 + dst * 128 : 1920 + dst * 128] = w_up[1, :, at(src, 128)]
        first[i][32:48, 0:128] = small.astype(BF)
        first[i][32:48, 128:768] = jnp.zeros((16, 640), BF)
    low_zl = lax.axis_index("zl") == 0
    for l in range(2):
        w = inner_columns(w_out[l].astype(F32)).astype(BF)
        out_a[l * 32 : l * 32 + 32] = jnp.where(low_zl, w[:, :512], w[:, 512:])
        out_b[l * 32 : l * 32 + 32] = jnp.where(low_zl, w[:, 512:], w[:, :512])
        down[l] = inner_columns(w_down[l].astype(F32)).astype(BF)


def put_out(piece, layer, out_a, out_b):
    for ref, flip in ((out_a, 0), (out_b, 1)):
        zl_from = bit("y", flip)
        for h in range(2):
            piece[pl.ds(pl.multiple_of(h * 64 + zl_from * 32, 32), 32), 768:1024] = ref[
                layer * 32 : layer * 32 + 32, h * 256 : h * 256 + 256
            ]


def pack_first(m0, m1, m2, m3, out_a, out_b, piece):
    lane = lax.broadcasted_iota(jnp.int32, (16, 128), 1)
    kind = lax.broadcasted_iota(jnp.int32, (16, 128), 0) % 8
    one = jnp.zeros((16, 128), F32)
    two = jnp.zeros((16, 128), F32)
    for i, m in enumerate((m0, m1, m2, m3)):
        core, zl = bit("core", RANKS[i][0]), bit("zl", RANKS[i][1])
        piece[at(core * 2 + zl, 32), 0:768] = m[0:32, :]
        s = m[32:48, 0:128].astype(F32)
        mine = (kind < 6) & (lane // 32 == core * 2 + zl)
        pair = (kind == 6) & (lane // 64 == zl)
        if i == 0:
            mine = mine | (kind == 7)
        one = one + jnp.where(mine | (pair & (core == 0)), s, 0.0)
        two = two + jnp.where(pair & (core == 1), s, 0.0)
    put_out(piece, 0, out_a, out_b)
    piece[128:144, 0:128] = one.astype(BF)
    piece[128:144, 128:256] = two.astype(BF)
    piece[128:144, 256:1024] = jnp.zeros((16, 768), BF)


def pack_rest(m0, m1, m2, m3, out_a, out_b, down, mlp_0, att_1, mlp_1):
    for i, m in enumerate((m0, m1, m2, m3)):
        spot = at(bit("core", RANKS[i][0]) * 2 + bit("zl", RANKS[i][1]), 32)
        mlp_0[spot, :] = m[:, 0:1024]
        att_1[spot, 0:768] = m[:, 1024:1792]
        mlp_1[spot, :] = m[:, 1792:2816]
    put_out(att_1, 1, out_a, out_b)
    mlp_0[128:256, :] = down[0]
    mlp_1[128:256, :] = down[1]


def gather_slots(piece):
    far = swap(piece, "zh")
    near_x = swap(piece, "x")
    near_y = swap(piece, "y")
    far_y = swap(far, "y")
    far_x = swap(far, "x")
    near_xy = swap(near_x, "y")
    far_yx = swap(far_y, "x")
    return (piece, far, near_x, far_x, near_y, far_y, near_xy, far_yx)


def load_rows(pieces, scratch, row, columns):
    for r, block in slot_blocks():
        scratch[at(block, 128), :] = pieces[r][row : row + 128, 0:columns]


def load_out(pieces, scratch):
    for r, y, x, zh in slot_places():
        for h in range(2):
            scratch[at(x * 2 + zh, 64), at(y * 2 + h, 256)] = pieces[r][
                h * 64 : h * 64 + 64, 768:1024
            ]


def normal(x):
    centred = x - jnp.mean(x, axis=-1, keepdims=True)
    inv = lax.rsqrt(jnp.mean(centred * centred, axis=-1, keepdims=True) + EPSILON)
    return centred * inv, inv


def load_stream(blocks, scratch):
    for i, (dc, dl) in enumerate(RANKS):
        spot = at(bit("core", dc) * 2 + bit("zl", dl), 128)
        scratch[spot, :] = inner_columns(blocks[i][0].astype(F32)).astype(scratch.dtype)


def load_cores(mine, other, scratch):
    scratch[at(bit("core", 0), 256), :] = mine[...]
    scratch[at(bit("core", 1), 256), :] = other[...]


def split_product(left, right, keep, send):
    mine, other = at(bit("core", 0), 256), at(bit("core", 1), 256)
    send[...] = right(left[other, :]).astype(BF)
    keep[...] = right(left[mine, :])


def row_positions(order, dim):
    shape_ = (512, 1) if dim == 0 else (1, 512)
    row = lax.broadcasted_iota(jnp.int32, shape_, dim)
    start = jnp.zeros(shape_, jnp.int32)
    for c in range(4):
        lead = order[c]
        start = jnp.where(row // 64 == 2 * c, lead, start)
        start = jnp.where(row // 64 == 2 * c + 1, 7 - lead, start)
    return start * 64 + row % 64


def masked_distance(seg_a, seg_b, order, dist):
    same = lax.axis_index("core") == lax.axis_index("zh")
    seg = jnp.where(same, seg_a[...], seg_b[...])
    ends = [jnp.sum((seg < d).astype(jnp.int32), axis=1, keepdims=True) for d in (1, 2)]

    def doc(pos):
        return (pos >= ends[0]).astype(jnp.int32) + (pos >= ends[1]).astype(jnp.int32)

    rows, cols = row_positions(order, 0), row_positions(order, 1)
    gap = rows - cols
    fine = (gap >= 0) & (doc(rows) == doc(cols))
    dist[...] = jnp.where(fine, gap.astype(F32), 1e32)


def slope_of(pair, half):
    core, zl = lax.axis_index("core"), lax.axis_index("zl")
    value = jnp.float32(0.0)
    for c in range(2):
        for z in range(2):
            head = 8 * z + 4 * pair + 2 * c + half
            value = jnp.where((core == c) & (zl == z), jnp.float32(2.0 ** (-8.0 * (head + 1) / HEADS)), value)
    return value


def attend(qkv, dist, probs, o):
    low = lax.broadcasted_iota(jnp.int32, (128, 128), 1) < 64
    for pair in range(2):
        k = qkv[:, 256 + pair * 128 : 384 + pair * 128]
        v = qkv[:, 512 + pair * 128 : 640 + pair * 128]

        def rows(step, carry):
            spot = at(step, 128)
            q = qkv[spot, pair * 128 : pair * 128 + 128]
            d = dist[spot, :]
            found = []
            for half in range(2):
                qh = jnp.where(low == (half == 0), q, jnp.zeros_like(q))
                s = dot_t(qh, k) * 0.125 - slope_of(pair, half) * d
                p = jnp.exp(s - jnp.max(s, axis=1, keepdims=True))
                p = (p / jnp.sum(p, axis=1, keepdims=True)).astype(BF)
                probs[pair * 2 + half, spot, :] = p
                found.append(dot(p, v))
            o[spot, pair * 128 : pair * 128 + 128] = jnp.where(low, *found).astype(BF)
            return carry

        lax.fori_loop(0, 4, rows, 0)


def attention_part(h1, vec, layer, pieces, seg_a, seg_b, order, outs, scratch):
    qkv, probs, o, keep, send = outs
    wq, wo, dist = scratch
    load_rows(pieces, wq, 0, 768)
    load_out(pieces, wo)
    masked_distance(seg_a, seg_b, order, dist)
    qkv[...] = (dot(h1[...], wq[...]) + vec[layer * 8 + 6 : layer * 8 + 7, 0:768]).astype(BF)
    attend(qkv, dist, probs, o)
    split_product(o, lambda rows: dot(rows, wo[...]), keep, send)


def first_attention(t0, t1, t2, t3, *refs):
    pieces, (seg_a, seg_b, order), refs = refs[:8], refs[8:11], refs[11:]
    vec, h1, outs, scratch = refs[0], refs[1], refs[2:7], refs[7:]
    q_one, q_two, scratch = scratch[0], scratch[1], scratch[2:]
    for r, block in slot_blocks():
        vec[:, at(block, 128)] = pieces[r][128:144, 0:128].astype(F32)
        q_two[:, at(block, 128)] = pieces[r][128:144, 128:256].astype(F32)
    q_one[...] = vec[...]
    core, zl = lax.axis_index("core"), lax.axis_index("zl")
    for l in range(2):
        row = slice(l * 8 + 6, l * 8 + 7)
        for base, y in ((0, 0), (512, 1)):
            block = (y * 2 + zl) * 2 + core
            vec[row, base : base + 128] = q_one[row, at(block, 128)]
            vec[row, base + 128 : base + 256] = q_two[row, at(block, 128)]
        vec[row, 256:512] = jnp.zeros((1, 256), F32)
    load_stream((t0, t1, t2, t3), h1)
    for i in range(4):
        spot = slice(i * 128, i * 128 + 128)
        z, _ = normal(h1[spot, :].astype(F32))
        h1[spot, :] = (z * vec[0:1, :] + vec[1:2, :]).astype(BF)
    attention_part(h1, vec, 0, pieces, seg_a, seg_b, order, outs, scratch)


def next_attention(mine, other, *refs):
    pieces, (vec, seg_a, seg_b, order), refs = refs[:8], refs[8:12], refs[12:]
    h1, outs, scratch = refs[0], refs[1:6], refs[6:]
    load_cores(mine, other, h1)
    attention_part(h1, vec, 1, pieces, seg_a, seg_b, order, outs, scratch)


def add_parts(keep, came, out):
    out[...] = (keep[...] + came[...].astype(F32)).astype(BF)


def norm_stage(bias_row, gain_row):
    def kernel(x, part, came, vec, x_out, h):
        for i in range(2):
            spot = slice(i * 128, i * 128 + 128)
            v = x[spot, :] + part[spot, :].astype(F32) + came[spot, :].astype(F32)
            v = v + vec[bias_row : bias_row + 1, :]
            x_out[spot, :] = v
            z, _ = normal(v)
            h[spot, :] = (z * vec[gain_row : gain_row + 1] + vec[gain_row + 1 : gain_row + 2]).astype(BF)

    return kernel


def first_norm_stage(t0, t2, part, came, vec, x_out, h, x0):
    x0[at(bit("zl", 0), 128), :] = inner_columns(t0[0].astype(F32))
    x0[at(bit("zl", 1), 128), :] = inner_columns(t2[0].astype(F32))
    norm_stage(2, 3)(x0, part, came, vec, x_out, h)


def mlp_stage(layer):
    def kernel(mine, other, *refs):
        pieces, vec, refs = refs[:8], refs[8], refs[9:]
        h2, u, a, keep, send, w = refs
        load_cores(mine, other, h2)
        load_rows(pieces, w, 0, 1024)
        for i in range(4):
            spot = slice(i * 128, i * 128 + 128)
            z = dot(h2[spot, :], w[...]) + vec[layer * 8 + 7 : layer * 8 + 8, :]
            u[spot, :] = z
            a[spot, :] = gelu_tanh(z).astype(BF)
        load_rows(pieces, w, 128, 1024)
        split_product(a, lambda rows: dot(rows, w[...]), keep, send)

    return with_scratch(kernel, pltpu.VMEM((1024, 1024), BF))


def finish_rows(x, part, came, vec, out):
    spot = at(bit("zl", 0), 128)
    v = x[spot, :] + part[spot, :].astype(F32) + came[spot, :].astype(F32) + vec[13:14, :]
    out[0] = inner_columns(v).astype(BF)


def gelu_slope(u):
    c = 0.7978845608028654
    t = jnp.tanh(c * (u + 0.044715 * u * u * u))
    return 0.5 * (1.0 + t) + 0.5 * u * (1.0 - t * t) * (c * (1.0 + 3 * 0.044715 * u * u))


def mlp_back_part(gy2, u, pieces, gu, keep, send, w):
    load_rows(pieces, w, 128, 1024)
    for i in range(4):
        spot = slice(i * 128, i * 128 + 128)
        gu[spot, :] = (dot_t(gy2[spot, :], w[...]) * gelu_slope(u[spot, :])).astype(BF)
    load_rows(pieces, w, 0, 1024)
    split_product(gu, lambda rows: dot_t(rows, w[...]), keep, send)


def first_mlp_back(c0, c1, c2, c3, u, *refs):
    pieces, refs = refs[:8], refs[8:]
    load_stream((c0, c1, c2, c3), refs[0])
    mlp_back_part(refs[0], u, pieces, *refs[1:])


def next_mlp_back(mine, other, u, *refs):
    pieces, refs = refs[:8], refs[8:]
    load_cores(mine, other, refs[0])
    mlp_back_part(refs[0], u, pieces, *refs[1:])


def turned_dot(left, right):
    return lax.dot_general(left, right, (((0,), (0,)), ((), ())), preferred_element_type=F32)


def slot_spots(near_send, near_0, near_1, far_send, far_0, far_1):
    return (
        near_0, far_0, near_1, far_send.at[0], near_send.at[0], far_1, near_send.at[1], far_send.at[1],
    )


def mlp_grads(h2, a, gy2, gu, *outs):
    spots = slot_spots(*outs)
    for r, block in slot_blocks():
        spots[r][0:128, :] = turned_dot(h2[:, at(block, 128)], gu[...]).astype(BF)
        spots[r][128:256, :] = turned_dot(a[:, at(block, 128)], gy2[...]).astype(BF)


def norm_back(gx, part, came, x, gain, gm, gy, sums):
    totals = [jnp.zeros((1, x.shape[1]), F32) for _ in range(4)]
    for i in range(2):
        spot = slice(i * 128, i * 128 + 128)
        dh = part[spot, :].astype(F32) + came[spot, :].astype(F32)
        z, inv = normal(x[spot, :])
        dz = dh * gain
        mean_a = jnp.mean(dz, axis=-1, keepdims=True)
        mean_b = jnp.mean(dz * z, axis=-1, keepdims=True)
        up = gx[spot, :]
        g = up + inv * (dz - mean_a - z * mean_b)
        gm[spot, :] = g
        rounded = g.astype(BF)
        gy[spot, :] = rounded
        new = (dh * z, dh, rounded.astype(F32), up.astype(BF).astype(F32))
        totals = [t + jnp.sum(v, axis=0, keepdims=True) for t, v in zip(totals, new)]
    sums[...] = jnp.concatenate(totals + [jnp.zeros((4, x.shape[1]), F32)], axis=0)


def norm_back_stage(gain_row):
    def kernel(gx, part, came, x, vec, gm, gy, sums):
        norm_back(gx, part, came, x, vec[gain_row : gain_row + 1, :], gm, gy, sums)

    return kernel


def first_norm_back(c0, c2, part, came, x, vec, gm, gy, sums, gx):
    gx[at(bit("zl", 0), 128), :] = inner_columns(c0[0].astype(F32))
    gx[at(bit("zl", 1), 128), :] = inner_columns(c2[0].astype(F32))
    norm_back(gx, part, came, x, vec[11:12, :], gm, gy, sums)


def last_norm_back(gx, part, came, t0, t2, vec, grad, sums, x, gm, gy):
    x[at(bit("zl", 0), 128), :] = inner_columns(t0[0].astype(F32))
    x[at(bit("zl", 1), 128), :] = inner_columns(t2[0].astype(F32))
    norm_back(gx, part, came, x, vec[0:1, :], gm, gy, sums)
    grad[0] = inner_columns(gm[at(bit("zl", 0), 128), :]).astype(BF)


def attention_back(mine, other, qkv, probs, *refs):
    pieces, refs = refs[:8], refs[8:]
    gy1, gqkv, keep, send, wq, wo, go, gk, gv = refs
    load_cores(mine, other, gy1)
    load_rows(pieces, wq, 0, 768)
    load_out(pieces, wo)
    go[...] = dot_t(gy1[...], wo[...]).astype(BF)
    low = lax.broadcasted_iota(jnp.int32, (128, 128), 1) < 64
    low_all = lax.broadcasted_iota(jnp.int32, (512, 128), 1) < 64
    for pair in range(2):
        k = qkv[:, 256 + pair * 128 : 384 + pair * 128]
        v = qkv[:, 512 + pair * 128 : 640 + pair * 128]
        gk[...] = jnp.zeros_like(gk)
        gv[...] = jnp.zeros_like(gv)

        def rows(step, carry):
            spot = at(step, 128)
            q = qkv[spot, pair * 128 : pair * 128 + 128]
            g = go[spot, pair * 128 : pair * 128 + 128]
            gq = []
            for half in range(2):
                lanes = low == (half == 0)
                gh = jnp.where(lanes, g, jnp.zeros_like(g))
                qh = jnp.where(lanes, q, jnp.zeros_like(q))
                p = probs[pair * 2 + half, spot, :]
                pf = p.astype(F32)
                dp = dot_t(gh, v)
                ds = (pf * (dp - jnp.sum(dp * pf, axis=1, keepdims=True))).astype(BF)
                gq.append(dot(ds, k))
                gk[...] += turned_dot(ds, qh)
                gv[...] += turned_dot(p, gh)
            gqkv[spot, pair * 128 : pair * 128 + 128] = (0.125 * jnp.where(low, *gq)).astype(BF)
            return carry

        lax.fori_loop(0, 4, rows, 0)
        gqkv[:, 256 + pair * 128 : 384 + pair * 128] = (0.125 * gk[...]).astype(BF)
        gqkv[:, 512 + pair * 128 : 640 + pair * 128] = gv[...].astype(BF)
    split_product(gqkv, lambda rows: dot_t(rows, wq[...]), keep, send)


def attention_grads(h1, o, gy1, gqkv, *outs):
    spots, d_out = slot_spots(*outs[:6]), outs[6]
    d_out[...] = turned_dot(o[...], gy1[...]).astype(BF)
    for (r, block), (_, y, x, zh) in zip(slot_blocks(), slot_places()):
        spots[r][0:128, 0:768] = turned_dot(h1[:, at(block, 128)], gqkv[...]).astype(BF)
        for h in range(2):
            spots[r][h * 64 : h * 64 + 64, 768:1024] = d_out[at(x * 2 + zh, 64), at(y * 2 + h, 256)]


def last_attention_grads(h1, o, gy1, gqkv, g1, e1, e0, gu1, gu0, gq1, *outs):
    attention_grads(h1, o, gy1, gqkv, *outs[:7])
    spots, (ups, wide) = slot_spots(*outs[:6]), outs[7:]
    none = jnp.zeros((2, 1024), F32)
    parts = [g1[0:2, :], e1[2:3, :], e1[0:2, :], e1[3:4, :], none, none]
    wide[...] = jnp.concatenate(parts + [e0[2:3, :], e0[0:2, :], e0[3:4, :], none], axis=0)
    sums = [jnp.sum(v[...].astype(F32), axis=0, keepdims=True) for v in (gu1, gu0)]
    ups[...] = jnp.concatenate(sums + [jnp.zeros((14, 1024), F32)], axis=0)
    q = [jnp.sum(v[...].astype(F32), axis=0, keepdims=True) for v in (gq1, gqkv)]
    q = jnp.concatenate(q + [jnp.zeros((14, 768), F32)], axis=0)
    core, zl = lax.axis_index("core"), lax.axis_index("zl")
    for r, block in slot_blocks():
        rows = slice(128, 144)
        spots[r][rows, 0:128] = wide[:, at(block, 128)].astype(BF)
        spots[r][rows, 128:256] = ups[:, at(block, 128)].astype(BF)
        mine = jnp.where(block == 4 + zl * 2 + core, q[:, 512:768], jnp.zeros((16, 256), F32))
        mine = jnp.where(block == zl * 2 + core, q[:, 0:256], mine)
        spots[r][rows, 256:512] = mine.astype(BF)
        spots[r][rows, 512:1024] = jnp.zeros((16, 512), BF)


def scatter_slots(near_send, near_0, near_1, far_send, far_0, far_1):
    near = swap(near_send, "y")
    far = swap(far_send, "x")
    near_2 = swap((near_1.astype(F32) + near[1].astype(F32)).astype(BF), "x")
    far_2 = swap((far_1.astype(F32) + far[1].astype(F32)).astype(BF), "y")
    far_all = far_0.astype(F32) + far[0].astype(F32) + far_2.astype(F32)
    far_3 = swap(far_all.astype(BF), "zh")
    return near_0, near, near_2, far_3


def summed(parts, rows, columns):
    near_0, near, near_2, far_3 = parts
    value = near_0[rows, columns].astype(F32) + near[0, rows, columns].astype(F32)
    return value + near_2[rows, columns].astype(F32) + far_3[rows, columns].astype(F32)


def own_out(parts, flip):
    row = bit("y", flip) * 32
    halves = []
    for h in range(2):
        spot = pl.ds(pl.multiple_of(h * 64 + row, 32), 32)
        halves.append(summed(parts, spot, slice(768, 1024)))
    return jnp.concatenate(halves, axis=1)


def unpack_rest(*refs):
    mlp_1, att_1, mlp_0 = refs[0:4], refs[4:8], refs[8:12]
    mine, sends, a, b, down = refs[12], refs[13:16], refs[16], refs[17], refs[18]
    for i, (dc, dl) in enumerate(RANKS):
        rows = at(bit("core", dc) * 2 + bit("zl", dl), 32)
        to = mine if i == 0 else sends[i - 1]
        for parts, start, width in ((mlp_0, 0, 1024), (att_1, 1024, 768), (mlp_1, 1792, 1024)):
            value = summed(parts, rows, slice(0, width))
            to[:, start : start + width] = value.astype(to.dtype)
    a[...] = own_out(att_1, 0).astype(BF)
    b[...] = own_out(att_1, 1).astype(BF)
    for l, parts in ((0, mlp_0), (1, mlp_1)):
        down[l] = inner_columns(summed(parts, slice(128, 256), slice(0, 1024)))


def unpack_last(near_0, near, near_2, far_3, a1, b1, mine, *refs):
    parts = (near_0, near, near_2, far_3)
    sends, (a, b) = refs[0:3], refs[3:5]
    for i, (dc, dl) in enumerate(RANKS):
        rows = at(bit("core", dc) * 2 + bit("zl", dl), 32)
        to = mine if i == 0 else sends[i - 1]
        to[0:32, :] = summed(parts, rows, slice(0, 768)).astype(to.dtype)
        to[32:48, :] = summed(parts, slice(128, 144), slice(0, 768)).astype(to.dtype)
    a[0:32, :] = own_out(parts, 0).astype(BF)
    b[0:32, :] = own_out(parts, 1).astype(BF)
    a[32:64, :] = a1[...]
    b[32:64, :] = b1[...]


def finish(rest, r1, r2, r3, last, l1, l2, l3, a, b, total, *outs):
    g1, b1, w_qkv, qv, w_out, bo, g2, b2, w_up, up, bd = outs
    for i, (rm, lm) in enumerate(((rest, last), (r1, l1), (r2, l2), (r3, l3))):
        core, zl = bit("core", RANKS[i][0]), bit("zl", RANKS[i][1])
        for src, dst in qkv_blocks(core, zl):
            w_qkv[0, :, at(src, 128)] = lm[0:32, dst * 128 : dst * 128 + 128].astype(F32)
            w_qkv[1, :, at(src, 128)] = rm[:, 1024 + dst * 128 : 1152 + dst * 128].astype(F32)
        for src, dst in up_blocks(core, zl):
            w_up[0, :, at(src, 128)] = rm[:, dst * 128 : dst * 128 + 128].astype(F32)
            w_up[1, :, at(src, 128)] = rm[:, 1792 + dst * 128 : 1920 + dst * 128].astype(F32)
    low_zl = lax.axis_index("zl") == 0
    for l in range(2):
        va, vb = a[l * 32 : l * 32 + 32].astype(F32), b[l * 32 : l * 32 + 32].astype(F32)
        w = jnp.concatenate([jnp.where(low_zl, va, vb), jnp.where(low_zl, vb, va)], axis=1)
        w_out[l] = inner_columns(w)
    spot = lax.axis_index("core") * 2 + lax.axis_index("zl")

    def chunk(value, size):
        found = jnp.zeros((value.shape[0], size), F32)
        for j in range(4):
            found = jnp.where(spot == j, value[:, j * size : j * size + size], found)
        return found

    wide = chunk(last[32:48, 0:128] + l1[32:48, 0:128].astype(F32), 32)
    block = (lax.axis_index("y") * 2 + lax.axis_index("x")) * 2 + lax.axis_index("zh")
    late = chunk(total[:, at(block, 128)], 32)
    for row, ref in ((2, bo), (3, g2), (4, b2), (5, bd)):
        ref[...] = jnp.concatenate([wide[row + 8 : row + 9], wide[row : row + 1]], axis=0)
    g1[...] = jnp.concatenate([late[0:1], wide[0:1]], axis=0)
    b1[...] = jnp.concatenate([late[1:2], wide[1:2]], axis=0)
    up[...] = jnp.concatenate([last[33:34, 128:256], last[32:33, 128:256]], axis=0)
    both = last[32:48, 256:512]
    for m in (l1, l2, l3):
        both = both + m[32:48, 256:512].astype(F32)
    both = chunk(both, 64)
    qv[...] = jnp.concatenate([both[1:2], both[0:1]], axis=0)


def corner(value):
    return lax.ppermute(value, ("core", "zh"), [(0, 0), (1, 2), (2, 1), (3, 3)])


def to_partners(messages):
    one, two, three = messages
    return (
        swap(one, "core"),
        swap(two, "zl"),
        lax.ppermute(three, ("core", "zl"), [(0, 3), (3, 0), (1, 2), (2, 1)]),
    )


def stream_blocks(block):
    block = corner(block)
    by_zl = swap(block, "zl")
    return (block, swap(block, "core"), by_zl, swap(by_zl, "core"))


def narrow_body(
    tokens, segment_ids, group_order, ln1_gain, ln1_bias, qkv_weight, qv_bias, out_weight, out_bias,
    ln2_gain, ln2_bias, up_weight, up_bias, down_weight, down_bias, cotangent,
):
    ready = run(
        prepare,
        [shape(48, 768)] * 4 + [shape(32, 2816)] * 4 + [shape(64, 512)] * 2 + [shape(2, 128, 1024)],
        ln1_gain, ln1_bias, out_bias, ln2_gain, ln2_bias, down_bias, qv_bias, up_bias,
        qkv_weight, out_weight, up_weight, down_weight,
    )
    first = (ready[0],) + to_partners(ready[1:4])
    out_a = lax.ppermute(ready[8], ("y", "zl"), [(0, 0), (1, 2), (2, 1), (3, 3)])
    out_b = lax.ppermute(ready[9], ("y", "zl"), [(0, 2), (1, 0), (2, 3), (3, 1)])
    (att_0,) = run(pack_first, [shape(144, 1024)], *first, out_a, out_b)
    att_0 = gather_slots(att_0)
    blocks = stream_blocks(tokens)
    rest = (ready[4],) + to_partners(ready[5:8])
    mlp_0, att_1, mlp_1 = run(
        pack_rest, [shape(256, 1024), shape(128, 1024), shape(256, 1024)],
        *rest, out_a, out_b, ready[10],
    )
    mlp_0, att_1, mlp_1 = gather_slots(mlp_0), gather_slots(att_1), gather_slots(mlp_1)
    cots = stream_blocks(cotangent)
    segments = (segment_ids, swap(segment_ids, "core"), group_order)

    def share(keep, send):
        (part,) = run(add_parts, [shape(256, 1024)], keep, swap(send, "core"))
        return part, swap(part, "zl")

    def with_other(value):
        return value, swap(value, "core")

    attention_outs = [
        shape(512, 1024), shape(512, 768), shape(4, 512, 512), shape(512, 256),
        shape(256, 1024, dtype=F32), shape(256, 1024),
    ]
    weights_scratch = [pltpu.VMEM((1024, 768), BF), pltpu.VMEM((256, 1024), BF)]
    dist = pltpu.VMEM((512, 512), F32)
    vec_scratch = [pltpu.VMEM((16, 1024), F32)] * 2
    rows_out = [shape(256, 1024, dtype=F32), shape(256, 1024)]
    mlp_outs = [
        shape(512, 1024), shape(512, 1024, dtype=F32), shape(512, 1024),
        shape(256, 1024, dtype=F32), shape(256, 1024),
    ]
    wide = pltpu.VMEM((1024, 1024), BF)

    vec, h1_0, qkv_0, probs_0, o_0, keep, send = run(
        with_scratch(first_attention, *vec_scratch, *weights_scratch, dist),
        [shape(16, 1024, dtype=F32)] + attention_outs, *blocks, *att_0, *segments,
    )
    x1_0, h = run(
        with_scratch(first_norm_stage, pltpu.VMEM((256, 1024), F32)),
        rows_out, blocks[0], blocks[2], *share(keep, send), vec,
    )
    h2_0, u_0, a_0, keep, send = run(mlp_stage(0), mlp_outs, *with_other(h), *mlp_0, vec)
    x2_0, h = run(norm_stage(5, 8), rows_out, x1_0, *share(keep, send), vec)
    h1_1, qkv_1, probs_1, o_1, keep, send = run(
        with_scratch(next_attention, *weights_scratch, dist),
        attention_outs, *with_other(h), *att_1, vec, *segments,
    )
    x1_1, h = run(norm_stage(10, 11), rows_out, x2_0, *share(keep, send), vec)
    h2_1, u_1, a_1, keep, send = run(mlp_stage(1), mlp_outs, *with_other(h), *mlp_1, vec)
    (final,) = run(finish_rows, [shape(1, 128, 1024)], x1_1, *share(keep, send), vec)
    output = corner(final)

    mlp_back_outs = [
        shape(512, 1024), shape(512, 1024), shape(256, 1024, dtype=F32), shape(256, 1024),
    ]
    norm_outs = rows_out + [shape(8, 1024, dtype=F32)]
    attention_back_outs = [
        shape(512, 1024), shape(512, 768), shape(256, 1024, dtype=F32), shape(256, 1024),
    ]
    attention_back_scratch = weights_scratch + [
        pltpu.VMEM((512, 256), BF), pltpu.VMEM((512, 128), F32), pltpu.VMEM((512, 128), F32),
    ]

    def grad_outs(rows):
        near = [shape(2, rows, 1024), shape(rows, 1024), shape(rows, 1024)]
        return near + near

    out_scratch = pltpu.VMEM((256, 1024), BF)

    gy2, gu_1, keep, send = run(
        with_scratch(first_mlp_back, wide), mlp_back_outs, *cots, u_1, *mlp_1
    )
    mlp_sums_1 = scatter_slots(*run(mlp_grads, grad_outs(256), h2_1, a_1, gy2, gu_1))
    gm, gy, e1 = run(
        with_scratch(first_norm_back, pltpu.VMEM((256, 1024), F32)),
        norm_outs, cots[0], cots[2], *share(keep, send), x1_1, vec,
    )
    gy1, gqkv_1, keep, send = run(
        with_scratch(attention_back, *attention_back_scratch),
        attention_back_outs, *with_other(gy), qkv_1, probs_1, *att_1,
    )
    att_sums_1 = scatter_slots(
        *run(with_scratch(attention_grads, out_scratch), grad_outs(128), h1_1, o_1, gy1, gqkv_1)
    )
    gx, gy, g1 = run(norm_back_stage(8), norm_outs, gm, *share(keep, send), x2_0, vec)
    gy2, gu_0, keep, send = run(
        with_scratch(next_mlp_back, wide), mlp_back_outs, *with_other(gy), u_0, *mlp_0
    )
    mlp_sums_0 = scatter_slots(*run(mlp_grads, grad_outs(256), h2_0, a_0, gy2, gu_0))
    gm, gy, e0 = run(norm_back_stage(3), norm_outs, gx, *share(keep, send), x1_0, vec)
    gy1, gqkv_0, keep, send = run(
        with_scratch(attention_back, *attention_back_scratch),
        attention_back_outs, *with_other(gy), qkv_0, probs_0, *att_0,
    )
    att_sums_0 = scatter_slots(
        *run(
            with_scratch(
                last_attention_grads, out_scratch, *vec_scratch
            ),
            grad_outs(144), h1_0, o_0, gy1, gqkv_0, g1, e1, e0, gu_1, gu_0, gqkv_1,
        )
    )
    grad, late = run(
        with_scratch(last_norm_back, *[pltpu.VMEM((256, 1024), F32)] * 2, pltpu.VMEM((256, 1024), BF)),
        [shape(1, 128, 1024), shape(8, 1024, dtype=F32)],
        gm, *share(keep, send), blocks[0], blocks[2], vec,
    )
    tokens_grad = corner(grad).astype(F32)
    for axis in ("core", "zh", "x", "y"):
        late = late + swap(late, axis)

    rest = run(
        unpack_rest,
        [shape(32, 2816, dtype=F32)] + [shape(32, 2816)] * 3 + [shape(32, 512)] * 2
        + [shape(2, 128, 1024, dtype=F32)],
        *mlp_sums_1, *att_sums_1, *mlp_sums_0,
    )
    last = run(
        unpack_last,
        [shape(48, 768, dtype=F32)] + [shape(48, 768)] * 3 + [shape(64, 512)] * 2,
        *att_sums_0, rest[4], rest[5],
    )
    back_a = lax.ppermute(last[4], ("y", "zl"), [(0, 0), (1, 2), (2, 1), (3, 3)])
    back_b = lax.ppermute(last[5], ("y", "zl"), [(0, 1), (1, 3), (2, 0), (3, 2)])
    sizes = (
        (2, 32), (2, 32), (2, 32, 3072), (2, 64), (2, 32, 1024), (2, 32), (2, 32), (2, 32),
        (2, 32, 4096), (2, 128), (2, 32),
    )
    g = run(
        finish, [shape(*s, dtype=F32) for s in sizes],
        rest[0], *to_partners(rest[1:4]), last[0], *to_partners(last[1:4]), back_a, back_b, late,
    )
    return (output, tokens_grad) + tuple(g[:10]) + (rest[6], g[10])


def solution(mesh):
    fsdp, ctx = mesh.shape["fsdp"], mesh.shape["ctx"]
    fine = Mesh(mesh.devices.reshape(fsdp // 4, 2, 2, 2, ctx // 2), AXES)
    body = narrow_body if fine.devices.shape == (2, 2, 2, 2, 2) else wide_body
    stream, place = ("y", "x", "core"), ("zh", "zl")
    rows = P(stream, place, None)
    flat, deep = P(None, AXES), P(None, AXES, None)
    params = (flat, flat, deep, flat, deep, flat, flat, flat, deep, flat, deep, flat)
    in_specs = (rows, P(stream, None), P()) + params + (rows,)
    out_specs = (rows, rows) + params
    return jax.shard_map(body, mesh=fine, in_specs=in_specs, out_specs=out_specs, check_vma=False)
```

```python
import jax
import jax.numpy as jnp
from jax import lax
from jax.experimental import pallas as pl
from jax.experimental.pallas import tpu as pltpu
from jax.sharding import Mesh, PartitionSpec as P

HEADS = 16
EPSILON = 1e-05
BF = jnp.bfloat16
F32 = jnp.float32
AXES = ("y", "x", "core", "zh", "zl")


def here(axis):
    return lax.axis_index(axis)


def swap(value, axis):
    return lax.ppermute(value, axis, [(0, 1), (1, 0)])


def ordered(mine, other, axis):
    first = here(axis) == 0
    return jnp.stack([jnp.where(first, mine, other), jnp.where(first, other, mine)])


def pick(value, axis):
    return lax.dynamic_index_in_dim(value, here(axis), 0, keepdims=False)


def pick_other(value, axis):
    return lax.dynamic_index_in_dim(value, 1 - here(axis), 0, keepdims=False)


def trade(value, axis):
    if lax.axis_size(axis) == 2:
        return ordered(pick(value, axis), swap(pick_other(value, axis), axis), axis)
    return lax.all_to_all(value, axis, 0, 0, tiled=True)


def collect(value, axis):
    if lax.axis_size(axis) == 2:
        return ordered(value, swap(value, axis), axis)
    return lax.all_gather(value, axis, axis=0, tiled=False)


def reduce_to(value, axis):
    if lax.axis_size(axis) == 2:
        return pick(value, axis) + swap(pick_other(value, axis), axis)
    return lax.psum_scatter(value, axis, scatter_dimension=0, tiled=False)


def flipped(value, axis, dim):
    return jnp.where(here(axis) == 0, value, jnp.flip(value, dim))


def gather_shards(shard):
    if lax.axis_size("y") != 2:
        return lax.all_gather(shard, ("y", "x", "zh"), axis=0, tiled=False)
    far = swap(shard, "zh")
    near_x = swap(shard, "x")
    far_y = swap(far, "y")
    near_y = swap(shard, "y")
    near_xy = swap(near_x, "y")
    far_x = swap(far, "x")
    far_yx = swap(far_y, "x")
    rel = jnp.stack([shard, far, near_x, far_x, near_y, far_y, near_xy, far_yx])
    rel = rel.reshape((2, 2, 2) + shard.shape)
    rel = flipped(flipped(flipped(rel, "y", 0), "x", 1), "zh", 2)
    return rel.reshape((8,) + shard.shape)


def scatter_shards(grads):
    shape = grads.shape[1:]
    if lax.axis_size("y") != 2:
        return lax.psum_scatter(
            grads, ("y", "x", "zh"), scatter_dimension=0, tiled=False
        )
    rel = grads.reshape((2, 2, 2) + shape)
    rel = flipped(flipped(flipped(rel, "y", 0), "x", 1), "zh", 2)
    near, far = rel[:, :, 0], rel[:, :, 1]
    far = far[:, 0] + swap(far[:, 1].astype(BF), "x").astype(F32)
    near = near[0] + swap(near[1].astype(BF), "y").astype(F32)
    far = far[0] + swap(far[1].astype(BF), "y").astype(F32)
    near = near[0] + swap(near[1].astype(BF), "x").astype(F32)
    return near + swap(far.astype(BF), "zh").astype(F32)


def corner_turn(value):
    return lax.ppermute(value, ("core", "zh"), [(0, 0), (1, 2), (2, 1), (3, 3)])


def norm_rows(values, gain, shift):
    row_mean = jnp.mean(values, axis=-1, keepdims=True)
    centred = values - row_mean
    row_var = jnp.mean(centred * centred, axis=-1, keepdims=True)
    return centred * lax.rsqrt(row_var + EPSILON) * gain + shift


def gelu_tanh(values):
    return jax.nn.gelu(values, approximate=True)


def dot(left, right):
    return jnp.dot(left, right, preferred_element_type=F32)


def dot_t(left, matrix):
    return lax.dot_general(
        left, matrix, (((1,), (1,)), ((), ())), preferred_element_type=F32
    )


def outer_sum(left, right):
    return jnp.einsum("td,te->de", left, right, preferred_element_type=F32)


def wide_body(
    tokens,
    segment_ids,
    group_order,
    ln1_gain,
    ln1_bias,
    qkv_weight,
    qv_bias,
    out_weight,
    out_bias,
    ln2_gain,
    ln2_bias,
    up_weight,
    up_bias,
    down_weight,
    down_bias,
    cotangent,
):
    ny, nx, nc, nzh, nzl = (lax.axis_size(a) for a in AXES)
    chips = ny * nx
    span = chips // nzl
    layers, width = ln1_gain.shape[0], tokens.shape[2]
    hidden = up_weight.shape[2]
    group = tokens.shape[1]
    ctx_count = nzh * nzl
    rank_width = width // (nc * nzl)
    rank_hidden = hidden // (nc * nzl)
    head_size = width // HEADS
    rank_heads = rank_width // head_size
    quarter = width // (chips * nc)
    unit = width // (chips * nc * nzh)
    core_rows = nzl * group
    rows = nc * core_rows
    scale = head_size ** (-0.5)

    def inner(value):
        shape = value.shape
        value = value.reshape(shape[:-1] + (chips, 2, 2, unit))
        return jnp.swapaxes(value, -3, -2).reshape(shape)

    small = (ln1_gain, ln1_bias, out_bias, ln2_gain, ln2_bias, down_bias)
    small_all = small + (qv_bias, up_bias)
    packed = jnp.concatenate([v.reshape(-1) for v in small_all])
    for axis in reversed(AXES):
        packed = collect(packed, axis)
    vectors = []
    at = 0
    for v in small_all:
        size = v.shape[0] * v.shape[1]
        part = packed[..., at : at + size].reshape((ny, nx, nc, nzh, nzl) + v.shape)
        part = jnp.moveaxis(part, 5, 0)
        vectors.append(part.reshape(layers, -1).astype(F32))
        at += size
    vec = [inner(v) for v in vectors[:6]]
    full_qv, full_up = vectors[6], vectors[7]

    def rank_columns(value):
        shape = value.shape[:-1]
        value = value.reshape(shape + (nzl, span, nc, quarter))
        value = lax.dynamic_index_in_dim(value, here("zl"), len(shape), keepdims=False)
        value = lax.dynamic_index_in_dim(value, here("core"), len(shape) + 1, keepdims=False)
        return value.reshape(shape + (rank_width,))

    q_bias = rank_columns(full_qv[:, :width])
    v_bias = rank_columns(full_qv[:, width:])
    qkv_bias = jnp.concatenate([q_bias, jnp.zeros_like(q_bias), v_bias], axis=1)
    up_b = full_up.reshape(layers, chips, nc, nzh, nzl, -1)
    up_b = lax.dynamic_index_in_dim(up_b, here("zl"), 4, keepdims=False)
    up_b = lax.dynamic_index_in_dim(up_b, here("core"), 2, keepdims=False)
    up_b = up_b.reshape(layers, rank_hidden)

    def to_ranks(value):
        value = trade(value, "core")
        return jnp.swapaxes(trade(jnp.swapaxes(value, 0, 1), "zl"), 0, 1)

    def fetch(layer):
        w = qkv_weight[layer]
        n = w.shape[0]
        w = w.reshape(n, 3, nzl, span, nc, quarter)
        w = jnp.transpose(w, (4, 2, 0, 1, 3, 5)).reshape(nc, nzl, n, 3 * rank_width)
        w_qkv = gather_shards(to_ranks(w).reshape(-1, 3 * rank_width))
        w = gather_shards(inner(out_weight[layer]))
        w = trade(w.reshape(nzl, span, nzh, n, width), "zl")
        w_out = jnp.transpose(w, (1, 2, 0, 3, 4)).reshape(rank_width, width)
        w = up_weight[layer].reshape(n, chips, nc, nzh, nzl, -1)
        w = jnp.transpose(w, (2, 4, 0, 1, 3, 5)).reshape(nc, nzl, n, rank_hidden)
        w_up = gather_shards(to_ranks(w).reshape(-1, rank_hidden))
        w_down = gather_shards(inner(down_weight[layer]))
        return (
            w_qkv.reshape(width, 3 * rank_width),
            w_out,
            w_up.reshape(width, rank_hidden),
            w_down.reshape(rank_hidden, width),
        )

    def from_ranks(value):
        value = jnp.swapaxes(trade(jnp.swapaxes(value, 0, 1), "zl"), 0, 1)
        return trade(value, "core")

    def send(grads):
        g_qkv, g_out, g_up, g_down = grads
        n = width // (chips * 2 * ctx_count)
        g = scatter_shards(g_qkv.reshape(chips * nzh, -1, 3 * rank_width))
        g = from_ranks(g.astype(BF).reshape(nc, nzl, n, 3 * rank_width)).astype(F32)
        g = g.reshape(nc, nzl, n, 3, span, quarter)
        d_qkv = jnp.transpose(g, (2, 3, 1, 4, 0, 5)).reshape(n, 3 * width)
        g = g_out.astype(BF).reshape(span, nzh, nzl, n, width)
        g = trade(jnp.transpose(g, (2, 0, 1, 3, 4)), "zl").astype(F32)
        d_out = inner(scatter_shards(g.reshape(chips * nzh, n, width)))
        g = scatter_shards(g_up.reshape(chips * nzh, -1, rank_hidden))
        g = from_ranks(g.astype(BF).reshape(nc, nzl, n, rank_hidden)).astype(F32)
        g = g.reshape(nc, nzl, n, chips, nzh, -1)
        d_up = jnp.transpose(g, (2, 3, 0, 4, 1, 5)).reshape(n, hidden)
        d_down = inner(scatter_shards(g_down.reshape(chips * nzh, -1, width)))
        return d_qkv, d_out, d_up, d_down

    def own_columns(value, mine):
        value = inner(value).reshape(ny, nx, nc, nzh, nzl, -1)
        keep = jnp.arange(nzl)[:, None] == here("zl")
        return jnp.where(keep, value, 0.0)

    def send_small(sums):
        g1, b1, gqv, bo, g2, b2, bu, bd = sums
        parts = [own_columns(v, None) for v in (g1, b1, bo, g2, b2, bd)]

        def placed(value):
            value = value.reshape(1, span, 1, quarter)
            keep = (jnp.arange(nzl)[:, None, None, None] == here("zl")) & (
                jnp.arange(nc)[None, None, :, None] == here("core")
            )
            return jnp.where(keep, value, 0.0).reshape(width)

        qv = jnp.concatenate([placed(gqv[0]), placed(gqv[1])])
        parts.append(qv.reshape(ny, nx, nc, nzh, nzl, -1))
        up = bu.reshape(ny, nx, 1, nzh, 1, -1)
        keep = (jnp.arange(nzl)[:, None] == here("zl")) & (
            jnp.arange(nc)[:, None, None, None] == here("core")
        )
        parts.append(jnp.where(keep, up, 0.0))
        value = jnp.concatenate(parts, axis=-1)
        for axis in AXES:
            value = reduce_to(value, axis)
        sizes = [p.shape[-1] for p in parts]
        cut, at = [], 0
        for s in sizes:
            cut.append(value[at : at + s])
            at += s
        g1, b1, bo, g2, b2, bd, qv, up = cut
        return g1, b1, qv, bo, g2, b2, up, bd

    def place(value):
        return collect(inner(corner_turn(value)), "zl").reshape(core_rows, width)

    def both_cores(value):
        return collect(value, "core").reshape(rows, -1)

    def total(partial):
        part = partial.reshape(nc, core_rows, width)
        part = pick(part, "core") + swap(pick_other(part, "core").astype(BF), "core").astype(F32)
        if nzl == 2:
            return part + swap(part.astype(BF), "zl").astype(F32)
        return lax.psum(part, "zl")

    seg = collect(segment_ids[0], "core")
    seg = lax.dynamic_index_in_dim(seg, here("zh"), 0, keepdims=False)
    half = group // 2
    block = jnp.stack([group_order, 2 * ctx_count - 1 - group_order], axis=1)
    pos = (block[:, :, None] * half + jnp.arange(half, dtype=jnp.int32)).reshape(rows)
    row_seg = jnp.take(seg, pos)
    distance = pos[:, None] - pos[None, :]
    allowed = (distance >= 0) & (row_seg[:, None] == row_seg[None, :])
    distance = distance.astype(F32)
    head_no = jnp.arange(rank_heads)
    head_no = (
        (here("zl") * span + head_no // (quarter // head_size)) * nc + here("core")
    ) * (quarter // head_size) + head_no % (quarter // head_size)
    slopes = jnp.exp2(-8.0 * (head_no.astype(F32) + 1.0) / HEADS)

    def scores_of(q, k):
        s = jnp.einsum("qhd,khd->hqk", q, k, preferred_element_type=F32) * scale
        return s - slopes[:, None, None] * distance[None]

    def split(qkv):
        return [
            v.reshape(rows, rank_heads, head_size) for v in jnp.split(qkv, 3, axis=1)
        ]

    weights = [fetch(layer) for layer in range(layers)]
    x = place(tokens[0]).astype(F32)
    kept = []
    for layer in range(layers):
        w_qkv, w_out, w_up, w_down = weights[layer]
        g1, b1, bo, g2, b2, bd = (v[layer] for v in vec)
        h1 = both_cores(norm_rows(x, g1, b1).astype(BF))
        qkv = (dot(h1, w_qkv) + qkv_bias[layer]).astype(BF)
        q, k, v = split(qkv)
        s = jnp.where(allowed, scores_of(q, k), -1e30)
        top = jnp.max(s, axis=-1, keepdims=True)
        p = jnp.where(allowed, jnp.exp(s - top), 0.0)
        den = jnp.sum(p, axis=-1, keepdims=True)
        p = p / den
        o = jnp.einsum("hqk,khd->qhd", p.astype(BF), v, preferred_element_type=F32)
        log_total = top + jnp.log(den)
        o = o.reshape(rows, rank_width).astype(BF)
        x1 = x + total(dot(o, w_out)) + bo
        h2 = both_cores(norm_rows(x1, g2, b2).astype(BF))
        u = dot(h2, w_up) + up_b[layer]
        a = gelu_tanh(u).astype(BF)
        x2 = x1 + total(dot(a, w_down)) + bd
        kept.append((x, h1, qkv, log_total, o, x1, h2, u, a))
        x = x2

    def leave(value):
        mine = lax.dynamic_index_in_dim(
            value.reshape(nzl, group, width), here("zl"), 0, keepdims=False
        )
        return corner_turn(inner(mine))[None]

    final_rows = leave(x.astype(BF))

    gx = place(cotangent[0]).astype(F32)
    result = [None] * layers
    for layer in reversed(range(layers)):
        w_qkv, w_out, w_up, w_down = weights[layer]
        g1, b1, bo, g2, b2, bd = (v[layer] for v in vec)
        x, h1, qkv, log_total, o, x1, h2, u, a = kept[layer]
        gy2_mine = gx.astype(BF)
        gy2 = both_cores(gy2_mine)
        d_down = outer_sum(a, gy2)
        d_bd = jnp.sum(gy2_mine.astype(F32), axis=0)
        _, gelu_back = jax.vjp(gelu_tanh, u)
        gu = gelu_back(dot_t(gy2, w_down))[0].astype(BF)
        d_up = outer_sum(h2, gu)
        d_bu = jnp.sum(gu.astype(F32), axis=0)
        _, back = jax.vjp(norm_rows, x1, g2, b2)
        gn, d_g2, d_b2 = back(total(dot_t(gu, w_up)))
        gm = gx + gn
        gy1_mine = gm.astype(BF)
        gy1 = both_cores(gy1_mine)
        d_out = outer_sum(o, gy1)
        d_bo = jnp.sum(gy1_mine.astype(F32), axis=0)
        go_f = dot_t(gy1, w_out)
        go = go_f.astype(BF).reshape(rows, rank_heads, head_size)
        q, k, v = split(qkv)
        p = jnp.where(allowed, jnp.exp(scores_of(q, k) - log_total), 0.0)
        dp = jnp.einsum("qhd,khd->hqk", go, v, preferred_element_type=F32)
        ds = (p * (dp - jnp.sum(dp * p, axis=-1, keepdims=True))).astype(BF)
        gq = scale * jnp.einsum("hqk,khd->qhd", ds, k, preferred_element_type=F32)
        gk = scale * jnp.einsum("hqk,qhd->khd", ds, q, preferred_element_type=F32)
        gv = jnp.einsum("hqk,qhd->khd", p.astype(BF), go, preferred_element_type=F32)
        gqkv = jnp.concatenate(
            [g.reshape(rows, rank_width) for g in (gq, gk, gv)], axis=1
        ).astype(BF)
        d_qkv = outer_sum(h1, gqkv)
        sums = jnp.sum(gqkv.astype(F32), axis=0)
        _, back = jax.vjp(norm_rows, x, g1, b1)
        gn, d_g1, d_b1 = back(total(dot_t(gqkv, w_qkv)))
        gx = gm + gn
        d_qv = (sums[:rank_width], sums[2 * rank_width :])
        big = send((d_qkv, d_out, d_up, d_down))
        tiny = send_small((d_g1, d_b1, d_qv, d_bo, d_g2, d_b2, d_bu, d_bd))
        result[layer] = (
            tiny[0], tiny[1], big[0], tiny[2], big[1], tiny[3],
            tiny[4], tiny[5], big[2], tiny[6], big[3], tiny[7],
        )
    stacked = [jnp.stack([result[layer][i] for layer in range(layers)]) for i in range(12)]
    return (final_rows, leave(gx)) + tuple(stacked)


def bit(axis, flip):
    place = lax.axis_index(axis)
    return 1 - place if flip else place


def slot_places():
    for slot in range(8):
        yield slot, bit("y", slot & 4), bit("x", slot & 2), bit("zh", slot & 1)


class View:
    def __init__(self, ref, row):
        self.ref, self.row = ref, row

    def _spot(self, spot):
        rows, columns = spot if isinstance(spot, tuple) else (spot, slice(None))
        if isinstance(rows, slice):
            return slice(rows.start + self.row, rows.stop + self.row), columns
        return pl.ds(rows.start + self.row, rows.size), columns

    def __getitem__(self, spot):
        return self.ref[self._spot(spot)]

    def __setitem__(self, spot, value):
        self.ref[self._spot(spot)] = value


class Rows:
    def __init__(self, refs):
        self.refs, self.size = refs, refs[0].shape[0]

    def _span(self, spot):
        rows = spot[0] if isinstance(spot, tuple) else spot
        if rows is Ellipsis:
            return 0, len(self.refs)
        return rows.start // self.size, rows.stop // self.size

    def __getitem__(self, spot):
        first, last = self._span(spot)
        return jnp.concatenate([r[...] for r in self.refs[first:last]], axis=0)

    def __setitem__(self, spot, value):
        first, last = self._span(spot)
        for i in range(first, last):
            self.refs[i][...] = value[(i - first) * self.size : (i - first + 1) * self.size]

    def block(self, which):
        low, high = self[slice(0, 128), :], self[slice(128, 256), :]
        return jnp.where(which == 0, low, high)


class Joined:
    def __init__(self, low, high, cut):
        self.low, self.high, self.cut = low, high, cut

    def __getitem__(self, spot):
        rows, columns = spot
        parts = []
        if rows.start < self.cut:
            parts.append(self.low[rows.start : min(rows.stop, self.cut), columns])
        if rows.stop > self.cut:
            parts.append(self.high[max(rows.start, self.cut) - self.cut : rows.stop - self.cut, columns])
        return parts[0] if len(parts) == 1 else jnp.concatenate(parts, axis=0)


def eight_slots(own, far, near_x, near_y, by_x, by_y, both, rows):
    cut = 128 if rows == 256 else 64
    across = Joined(View(by_y, rows), View(by_x, rows), cut)
    return own, far, near_x, by_x, near_y, by_y, across, both


def att_0_slots(refs):
    return eight_slots(*refs, 144)


def mlp_0_slots(refs):
    own, far_up, far_down, *refs = refs
    return eight_slots(own, Joined(far_up, far_down, 128), *refs, 256)


def att_1_slots(refs):
    own, far, by_x_1, by_y_1, by_x, by_y, both = refs
    return eight_slots(own, View(far, 0), View(by_x_1, 256), View(by_y_1, 256), by_x, by_y, both, 128)


def mlp_1_slots(refs):
    own, own_down, far, far_down, by_x_1, by_y_1, by_x, by_y, both = refs
    own, far = Joined(View(own, 128), own_down, 128), Joined(View(far, 128), far_down, 128)
    return eight_slots(own, far, View(by_x_1, 192), View(by_y_1, 192), by_x, by_y, both, 256)


def second_message(far, near_x, near_y, to_x, to_y, rows):
    cut = 128 if rows == 256 else 64
    to_x[0:rows, :] = far[0:rows, :]
    to_y[0:rows, :] = far[0:rows, :]
    to_y[rows : rows + cut, :] = near_x[0:cut, :]
    to_x[rows : 2 * rows - cut, :] = near_y[cut:rows, :]


def att_0_message(far, near_x, near_y, to_x, to_y):
    second_message(far, near_x, near_y, to_x, to_y, 144)


def mlp_0_message(far_up, far_down, near_x, near_y, to_x, to_y, to_both):
    far = Joined(far_up, far_down, 128)
    to_both[...] = far[0:256, :]
    second_message(far, near_x, near_y, to_x, to_y, 256)


def att_1_message(far, near_x, near_y, own, own_down, to_x, to_y, to_both):
    to_both[...] = far[0:128, :]
    second_message(far, View(near_x, 256), View(near_y, 256), to_x, to_y, 128)
    for to in (to_x, to_y):
        to[192:320, :] = own[128:256, :]
        to[320:448, :] = own_down[...]


def mlp_1_message(far, far_down, near_x, near_y, to_x, to_y, to_both):
    far = Joined(View(far, 128), far_down, 128)
    to_both[...] = far[0:256, :]
    second_message(far, View(near_x, 192), View(near_y, 192), to_x, to_y, 256)


def slot_blocks():
    return [(r, (y * 2 + x) * 2 + zh) for r, y, x, zh in slot_places()]


def at(block, size):
    return pl.ds(pl.multiple_of(block * size, size), size)


def run(kernel, outs, *ins, after=(), us=1.0, anywhere=False, limit=16):
    smem = pl.BlockSpec(memory_space=pltpu.SMEM)
    vmem = pl.BlockSpec(memory_space=pltpu.VMEM)
    free = pl.BlockSpec(memory_space=pl.ANY)
    skip = len(after)

    def body(*refs):
        kernel(*refs[skip:])

    return pl.pallas_call(
        body,
        out_shape=tuple(outs),
        in_specs=[free] * skip
        + [smem if v.size == 4 else free if anywhere else vmem for v in ins],
        out_specs=tuple(vmem for _ in outs),
        scratch_shapes=getattr(kernel, "scratch", []),
        compiler_params=pltpu.CompilerParams(vmem_limit_bytes=limit << 20),
        cost_estimate=pl.CostEstimate(flops=int(us * 1e7), bytes_accessed=0, transcendentals=0),
    )(*after, *ins)


def gate(after, *values):
    skip = len(after)

    def body(*refs):
        refs[-1][...] = jnp.zeros_like(refs[-1])

    free = pl.BlockSpec(memory_space=pl.ANY)
    return pl.pallas_call(
        body,
        out_shape=tuple(shape(*v.shape, dtype=v.dtype) for v in values) + (shape(8, 128, dtype=F32),),
        in_specs=[free] * (skip + len(values)),
        out_specs=tuple(free for _ in values) + (pl.BlockSpec(memory_space=pltpu.VMEM),),
        input_output_aliases={skip + i: i for i in range(len(values))},
        compiler_params=pltpu.CompilerParams(vmem_limit_bytes=16 << 20),
        cost_estimate=pl.CostEstimate(flops=10**4, bytes_accessed=0, transcendentals=0),
    )(*after, *values)


def shape(*sizes, dtype=BF):
    return jax.ShapeDtypeStruct(sizes, dtype)


def with_scratch(kernel, *scratch):
    kernel.scratch = list(scratch)
    return kernel


def inner_columns(value):
    low = lax.broadcasted_iota(jnp.int32, (value.shape[0], 128), 1) < 64
    parts = []
    for i in range(0, value.shape[1], 256):
        a, b = value[:, i : i + 128], value[:, i + 128 : i + 256]
        parts.append(jnp.where(low, a, pltpu.roll(b, 64, 1)))
        parts.append(jnp.where(low, pltpu.roll(a, 64, 1), b))
    return jnp.concatenate(parts, axis=1)


def spread(value):
    n = value.shape[1]
    if n == 128:
        return value.astype(F32)
    hit = lax.broadcasted_iota(jnp.int32, (n, 128), 1) % n == lax.broadcasted_iota(
        jnp.int32, (n, 128), 0
    )
    return dot(value.astype(F32), hit.astype(F32))


RANKS = ((0, 0), (1, 0), (0, 1), (1, 1))


def qkv_blocks(core, zl):
    return [
        (s * 8 + zl * 4 + x * 2 + core, s * 2 + x) for s in range(3) for x in range(2)
    ]


def up_blocks(core, zl):
    return [
        (chip * 8 + core * 4 + zh * 2 + zl, chip * 2 + zh)
        for chip in range(4)
        for zh in range(2)
    ]


def fetch(sources, held, sems):
    copies = [pltpu.make_async_copy(*pair, sems.at[i]) for i, pair in enumerate(zip(sources, held))]
    for copy in copies:
        copy.start()
    for copy in copies:
        copy.wait()


def prepare_first(*refs):
    sources, refs = refs[:11], refs[11:]
    first, (out_a, out_b, down), (held, sems) = refs[0:4], refs[4:7], (refs[7:18], refs[18])
    fetch(sources[:9] + (sources[9].at[0], sources[10].at[0]), held, sems)
    rows = [spread(v[...]) for v in held[:8]]
    w_out, w_qkv, w_down = held[8:]
    small = jnp.concatenate([v[l : l + 1] for l in range(2) for v in rows], axis=0)
    for i, (dc, dl) in enumerate(RANKS):
        for src, dst in qkv_blocks(bit("core", dc), bit("zl", dl)):
            first[i][0:32, dst * 128 : dst * 128 + 128] = w_qkv[:, at(src, 128)]
        first[i][32:48, 0:128] = small.astype(BF)
        first[i][32:48, 128:768] = jnp.zeros((16, 640), BF)
    low_zl = lax.axis_index("zl") == 0
    for l in range(2):
        w = inner_columns(w_out[l].astype(F32)).astype(BF)
        out_a[l * 32 : l * 32 + 32] = jnp.where(low_zl, w[:, :512], w[:, 512:])
        out_b[l * 32 : l * 32 + 32] = jnp.where(low_zl, w[:, 512:], w[:, :512])
    down[...] = inner_columns(w_down[...].astype(F32)).astype(BF)


def prepare_rest(*refs):
    sources, refs = refs[:4], refs[4:]
    rest, (down, cot), (held, sems) = refs[0:4], refs[4:6], (refs[6:10], refs[10])
    fetch((sources[0].at[1], sources[1], sources[2].at[1], sources[3].at[0]), held, sems)
    w_qkv, w_up, w_down, cot_in = held
    for i, (dc, dl) in enumerate(RANKS):
        core, zl = bit("core", dc), bit("zl", dl)
        for src, dst in qkv_blocks(core, zl):
            rest[i][:, 1024 + dst * 128 : 1152 + dst * 128] = w_qkv[:, at(src, 128)]
        for src, dst in up_blocks(core, zl):
            rest[i][:, dst * 128 : dst * 128 + 128] = w_up[0, :, at(src, 128)]
            rest[i][:, 1792 + dst * 128 : 1920 + dst * 128] = w_up[1, :, at(src, 128)]
    down[...] = inner_columns(w_down[...].astype(F32)).astype(BF)
    cot[...] = inner_columns(cot_in[...].astype(F32)).astype(BF)


def put_out(piece, layer, out_a, out_b):
    for ref, flip in ((out_a, 0), (out_b, 1)):
        zl_from = bit("y", flip)
        for h in range(2):
            piece[pl.ds(pl.multiple_of(h * 64 + zl_from * 32, 32), 32), 768:1024] = ref[
                layer * 32 : layer * 32 + 32, h * 256 : h * 256 + 256
            ]


def pack_first(m0, m1, m2, m3, out_a, out_b, piece):
    lane = lax.broadcasted_iota(jnp.int32, (16, 128), 1)
    kind = lax.broadcasted_iota(jnp.int32, (16, 128), 0) % 8
    one = jnp.zeros((16, 128), F32)
    two = jnp.zeros((16, 128), F32)
    for i, m in enumerate((m0, m1, m2, m3)):
        core, zl = bit("core", RANKS[i][0]), bit("zl", RANKS[i][1])
        piece[at(core * 2 + zl, 32), 0:768] = m[0:32, :]
        s = m[32:48, 0:128].astype(F32)
        mine = (kind < 6) & (lane // 32 == core * 2 + zl)
        pair = (kind == 6) & (lane // 64 == zl)
        if i == 0:
            mine = mine | (kind == 7)
        one = one + jnp.where(mine | (pair & (core == 0)), s, 0.0)
        two = two + jnp.where(pair & (core == 1), s, 0.0)
    put_out(piece, 0, out_a, out_b)
    piece[128:144, 0:128] = one.astype(BF)
    piece[128:144, 128:256] = two.astype(BF)
    piece[128:144, 256:1024] = jnp.zeros((16, 768), BF)


def pack_rest(m0, m1, m2, m3, out_a, out_b, down_0, mlp_0, up_0, deep, pair):
    for i, m in enumerate((m0, m1, m2, m3)):
        spot = at(bit("core", RANKS[i][0]) * 2 + bit("zl", RANKS[i][1]), 32)
        up_0[spot, :] = m[:, 0:1024]
        deep[spot, 0:768] = m[:, 1024:1792]
        deep[at(4 + bit("core", RANKS[i][0]) * 2 + bit("zl", RANKS[i][1]), 32), :] = m[:, 1792:2816]
    put_out(deep, 1, out_a, out_b)
    mlp_0[0:128, :] = up_0[...]
    mlp_0[128:256, :] = down_0[...]
    pair[0:256, :] = mlp_0[...]
    pair[256:384, :] = deep[0:128, :]


def both_ways(value):
    return lax.ppermute(value, ("y", "x"), [(0, 3), (3, 0), (1, 2), (2, 1)])


def first_hops(piece):
    return swap(piece, "zh"), swap(piece, "x"), swap(piece, "y")


def load_rows(pieces, scratch, row, columns):
    for r, block in slot_blocks():
        scratch[at(block, 128), :] = pieces[r][row : row + 128, 0:columns]


def load_out(pieces, scratch):
    for r, y, x, zh in slot_places():
        for h in range(2):
            scratch[at(x * 2 + zh, 64), at(y * 2 + h, 256)] = pieces[r][
                h * 64 : h * 64 + 64, 768:1024
            ]


def normal(x):
    centred = x - jnp.mean(x, axis=-1, keepdims=True)
    inv = lax.rsqrt(jnp.mean(centred * centred, axis=-1, keepdims=True) + EPSILON)
    return centred * inv, inv


def load_stream(blocks, scratch):
    for i, (dc, dl) in enumerate(RANKS):
        spot = at(bit("core", dc) * 2 + bit("zl", dl), 128)
        scratch[spot, :] = inner_columns(blocks[i][0].astype(F32)).astype(scratch.dtype)


def load_blocks(blocks, scratch):
    for i, (dc, dl) in enumerate(RANKS):
        scratch[at(bit("core", dc) * 2 + bit("zl", dl), 128), :] = blocks[i][...]


def load_cores(mine, other, scratch):
    scratch[at(bit("core", 0), 256), :] = Rows(mine)[...]
    scratch[at(bit("core", 1), 256), :] = Rows(other)[...]


def split_product(left, right, keep, send):
    mine, other = at(bit("core", 0), 256), at(bit("core", 1), 256)
    Rows(send)[...] = right(left[other, :]).astype(BF)
    keep[...] = right(left[mine, :])


def row_positions(order, dim):
    shape_ = (512, 1) if dim == 0 else (1, 512)
    row = lax.broadcasted_iota(jnp.int32, shape_, dim)
    start = jnp.zeros(shape_, jnp.int32)
    for c in range(4):
        lead = order[c]
        start = jnp.where(row // 64 == 2 * c, lead, start)
        start = jnp.where(row // 64 == 2 * c + 1, 7 - lead, start)
    return start * 64 + row % 64


def masked_distance(seg_a, seg_b, order, dist):
    same = lax.axis_index("core") == lax.axis_index("zh")
    seg = jnp.where(same, seg_a[...], seg_b[...])
    ends = [jnp.sum((seg < d).astype(jnp.int32), axis=1, keepdims=True) for d in (1, 2)]

    def doc(pos):
        return (pos >= ends[0]).astype(jnp.int32) + (pos >= ends[1]).astype(jnp.int32)

    rows, cols = row_positions(order, 0), row_positions(order, 1)
    gap = rows - cols
    fine = (gap >= 0) & (doc(rows) == doc(cols))
    dist[...] = jnp.where(fine, gap.astype(F32), 1e32)


def slope_of(pair, half):
    core, zl = lax.axis_index("core"), lax.axis_index("zl")
    value = jnp.float32(0.0)
    for c in range(2):
        for z in range(2):
            head = 8 * z + 4 * pair + 2 * c + half
            value = jnp.where((core == c) & (zl == z), jnp.float32(2.0 ** (-8.0 * (head + 1) / HEADS)), value)
    return value


def attend(qkv, dist, probs, o):
    low = lax.broadcasted_iota(jnp.int32, (128, 128), 1) < 64
    for pair in range(2):
        k = qkv[:, 256 + pair * 128 : 384 + pair * 128]
        v = qkv[:, 512 + pair * 128 : 640 + pair * 128]

        def rows(step, carry):
            spot = at(step, 128)
            q = qkv[spot, pair * 128 : pair * 128 + 128]
            d = dist[spot, :]
            found = []
            for half in range(2):
                qh = jnp.where(low == (half == 0), q, jnp.zeros_like(q))
                s = dot_t(qh, k) * 0.125 - slope_of(pair, half) * d
                p = jnp.exp(s - jnp.max(s, axis=1, keepdims=True))
                p = (p / jnp.sum(p, axis=1, keepdims=True)).astype(BF)
                probs[pair * 2 + half, spot, :] = p
                found.append(dot(p, v))
            o[spot, pair * 128 : pair * 128 + 128] = jnp.where(low, *found).astype(BF)
            return carry

        lax.fori_loop(0, 4, rows, 0)


def attention_part(h1, vec, layer, pieces, seg_a, seg_b, order, outs, scratch):
    qkv, probs, o, keep, *send = outs
    wq, wo, dist = scratch
    load_rows(pieces, wq, 0, 768)
    load_out(pieces, wo)
    masked_distance(seg_a, seg_b, order, dist)
    qkv[...] = (dot(h1[...], wq[...]) + vec[layer * 8 + 6 : layer * 8 + 7, 0:768]).astype(BF)
    attend(qkv, dist, probs, o)
    split_product(o, lambda rows: dot(rows, wo[...]), keep, send)


def first_attention(t0, t1, t2, t3, *refs):
    pieces, (seg_a, seg_b, order), refs = att_0_slots(refs[:7]), refs[7:10], refs[10:]
    vec, h1, outs, scratch = refs[0], refs[1], refs[2:10], refs[10:]
    q_one, q_two, scratch = scratch[0], scratch[1], scratch[2:]
    for r, block in slot_blocks():
        vec[:, at(block, 128)] = pieces[r][128:144, 0:128].astype(F32)
        q_two[:, at(block, 128)] = pieces[r][128:144, 128:256].astype(F32)
    q_one[...] = vec[...]
    core, zl = lax.axis_index("core"), lax.axis_index("zl")
    for l in range(2):
        row = slice(l * 8 + 6, l * 8 + 7)
        for base, y in ((0, 0), (512, 1)):
            block = (y * 2 + zl) * 2 + core
            vec[row, base : base + 128] = q_one[row, at(block, 128)]
            vec[row, base + 128 : base + 256] = q_two[row, at(block, 128)]
        vec[row, 256:512] = jnp.zeros((1, 256), F32)
    load_stream((t0, t1, t2, t3), h1)
    for i in range(4):
        spot = slice(i * 128, i * 128 + 128)
        z, _ = normal(h1[spot, :].astype(F32))
        h1[spot, :] = (z * vec[0:1, :] + vec[1:2, :]).astype(BF)
    attention_part(h1, vec, 0, pieces, seg_a, seg_b, order, outs, scratch)


def next_attention(*refs):
    mine, other, refs = refs[:4], refs[4:8], refs[8:]
    pieces, (vec, seg_a, seg_b, order), refs = att_1_slots(refs[:7]), refs[7:11], refs[11:]
    h1, outs, scratch = refs[0], refs[1:9], refs[9:]
    load_cores(mine, other, h1)
    attention_part(h1, vec, 1, pieces, seg_a, seg_b, order, outs, scratch)


def add_parts(keep, *refs):
    came, out = Rows(refs[:4]), refs[4]
    out[...] = (keep[...] + came[...].astype(F32)).astype(BF)


def norm_stage(bias_row, gain_row):
    def kernel(x, part, came, vec, x_out, *h):
        h = Rows(h)
        for i in range(2):
            spot = slice(i * 128, i * 128 + 128)
            v = x[spot, :] + part[spot, :].astype(F32) + came[spot, :].astype(F32)
            v = v + vec[bias_row : bias_row + 1, :]
            x_out[spot, :] = v
            z, _ = normal(v)
            h[spot, :] = (z * vec[gain_row : gain_row + 1] + vec[gain_row + 1 : gain_row + 2]).astype(BF)

    return kernel


def first_norm_stage(t0, t2, part, came, vec, *refs):
    x_out, h, x0 = refs[0], refs[1:5], refs[5]
    x0[at(bit("zl", 0), 128), :] = inner_columns(t0[0].astype(F32))
    x0[at(bit("zl", 1), 128), :] = inner_columns(t2[0].astype(F32))
    norm_stage(2, 3)(x0, part, came, vec, x_out, *h)


def mlp_weights(refs, layer):
    count = 9 if layer else 8
    return (mlp_1_slots if layer else mlp_0_slots)(refs[:count]), refs[count:]


def mlp_stage(layer):
    def kernel(*refs):
        mine, other, refs = refs[:4], refs[4:8], refs[8:]
        pieces, refs = mlp_weights(refs, layer)
        vec, h2, u, a, keep, *send, w = refs
        load_cores(mine, other, h2)
        load_rows(pieces, w, 0, 1024)
        for i in range(4):
            spot = slice(i * 128, i * 128 + 128)
            z = dot(h2[spot, :], w[...]) + vec[layer * 8 + 7 : layer * 8 + 8, :]
            u[spot, :] = z
            a[spot, :] = gelu_tanh(z).astype(BF)
        load_rows(pieces, w, 128, 1024)
        split_product(a, lambda rows: dot(rows, w[...]), keep, send)

    return with_scratch(kernel, pltpu.VMEM((1024, 1024), BF))


def finish_rows(x, part, came, vec, out):
    v = x[at(bit("zl", 0), 128), :] + part[...].astype(F32) + came[...].astype(F32) + vec[13:14, :]
    out[0] = inner_columns(v).astype(BF)


def add_split(keep, *refs):
    came, mine, other = Rows(refs[:4]), refs[4], refs[5]
    for to, flip in ((mine, 0), (other, 1)):
        which = bit("zl", flip)
        to[...] = (keep[at(which, 128), :] + came.block(which).astype(F32)).astype(BF)


def gelu_slope(u):
    c = 0.7978845608028654
    t = jnp.tanh(c * (u + 0.044715 * u * u * u))
    return 0.5 * (1.0 + t) + 0.5 * u * (1.0 - t * t) * (c * (1.0 + 3 * 0.044715 * u * u))


def mlp_back(layer):
    def kernel(*refs):
        if layer == 1:
            blocks, u, refs = refs[:4], refs[4], refs[5:]
        else:
            blocks, u, refs = refs[:8], refs[8], refs[9:]
        pieces, (gy2, gu, keep, *send, w) = mlp_weights(refs, layer)
        load_blocks(blocks, gy2) if layer == 1 else load_cores(blocks[:4], blocks[4:], gy2)
        load_rows(pieces, w, 128, 1024)
        for i in range(4):
            spot = slice(i * 128, i * 128 + 128)
            gu[spot, :] = (dot_t(gy2[spot, :], w[...]) * gelu_slope(u[spot, :])).astype(BF)
        load_rows(pieces, w, 0, 1024)
        split_product(gu, lambda rows: dot_t(rows, w[...]), keep, send)

    return with_scratch(kernel, pltpu.VMEM((1024, 1024), BF))


def turned_dot(left, right):
    return lax.dot_general(left, right, (((0,), (0,)), ((), ())), preferred_element_type=F32)


def slot_spots(rows, to_y, to_x, near_0, near_1, far_0, far_1):
    return (
        near_0, far_0, near_1, View(to_x, 0), View(to_y, 0), far_1, View(to_y, rows), View(to_x, rows),
    )


def mlp_grads(h2, a, gy2, gu, *outs):
    spots = slot_spots(256, *outs)
    for r, block in slot_blocks():
        spots[r][0:128, :] = turned_dot(h2[:, at(block, 128)], gu[...]).astype(BF)
        spots[r][128:256, :] = turned_dot(a[:, at(block, 128)], gy2[...]).astype(BF)


def second_sums(rows, near_1, near, far_1, far, to_x, to_y):
    to_x[0:rows, :] = (near_1[...].astype(F32) + near[0:rows, :].astype(F32)).astype(BF)
    to_y[0:rows, :] = (far_1[...].astype(F32) + far[0:rows, :].astype(F32)).astype(BF)


def third_sum(rows, far_0, far, far_2, out):
    total = far_0[...].astype(F32) + far[0:rows, :].astype(F32) + far_2[0:rows, :].astype(F32)
    out[...] = total.astype(BF)


def norm_back(gx, part, came, x, gain, gm, gy, sums):
    totals = [jnp.zeros((1, x.shape[1]), F32) for _ in range(4)]
    for i in range(part.shape[0] // 128):
        spot = slice(i * 128, i * 128 + 128)
        dh = part[spot, :].astype(F32) + came[spot, :].astype(F32)
        z, inv = normal(x[spot, :])
        dz = dh * gain
        mean_a = jnp.mean(dz, axis=-1, keepdims=True)
        mean_b = jnp.mean(dz * z, axis=-1, keepdims=True)
        up = gx[spot, :]
        g = up + inv * (dz - mean_a - z * mean_b)
        gm[spot, :] = g
        rounded = g.astype(BF)
        gy[spot, :] = rounded
        new = (dh * z, dh, rounded.astype(F32), up.astype(BF).astype(F32))
        totals = [t + jnp.sum(v, axis=0, keepdims=True) for t, v in zip(totals, new)]
    sums[...] = jnp.concatenate(totals + [jnp.zeros((4, x.shape[1]), F32)], axis=0)


def norm_back_stage(gain_row):
    def kernel(gx, part, came, x, vec, gm, *refs):
        norm_back(gx, part, came, x, vec[gain_row : gain_row + 1, :], gm, Rows(refs[:4]), refs[4])

    return kernel


def first_norm_back(c0, c2, part, came, x, vec, gm, *refs):
    gy, sums, gx = Rows(refs[:4]), refs[4], refs[5]
    gx[at(bit("zl", 0), 128), :] = c0[...].astype(F32)
    gx[at(bit("zl", 1), 128), :] = c2[...].astype(F32)
    norm_back(gx, part, came, x, vec[11:12, :], gm, gy, sums)


def last_norm_back(gx, part, came, t0, vec, grad, up, x, gm, gy, sums):
    x[...] = inner_columns(t0[0].astype(F32))
    up[...] = gx[at(bit("zl", 0), 128), :]
    norm_back(up, part, came, x, vec[0:1, :], gm, gy, sums)
    grad[0] = inner_columns(gm[...]).astype(BF)


def attention_back(layer):
    def kernel(*refs):
        mine, other, (qkv, probs), refs = refs[:4], refs[4:8], refs[8:10], refs[10:]
        pieces = (att_1_slots if layer else att_0_slots)(refs[:7])
        attention_back_part(mine, other, qkv, probs, pieces, *refs[7:])

    return kernel


def attention_back_part(mine, other, qkv, probs, pieces, *refs):
    gy1, gqkv, keep, *send, wq, wo, go, gk, gv = refs
    load_cores(mine, other, gy1)
    load_rows(pieces, wq, 0, 768)
    load_out(pieces, wo)
    go[...] = dot_t(gy1[...], wo[...]).astype(BF)
    low = lax.broadcasted_iota(jnp.int32, (128, 128), 1) < 64
    low_all = lax.broadcasted_iota(jnp.int32, (512, 128), 1) < 64
    for pair in range(2):
        k = qkv[:, 256 + pair * 128 : 384 + pair * 128]
        v = qkv[:, 512 + pair * 128 : 640 + pair * 128]
        gk[...] = jnp.zeros_like(gk)
        gv[...] = jnp.zeros_like(gv)

        def rows(step, carry):
            spot = at(step, 128)
            q = qkv[spot, pair * 128 : pair * 128 + 128]
            g = go[spot, pair * 128 : pair * 128 + 128]
            gq = []
            for half in range(2):
                lanes = low == (half == 0)
                gh = jnp.where(lanes, g, jnp.zeros_like(g))
                qh = jnp.where(lanes, q, jnp.zeros_like(q))
                p = probs[pair * 2 + half, spot, :]
                pf = p.astype(F32)
                dp = dot_t(gh, v)
                ds = (pf * (dp - jnp.sum(dp * pf, axis=1, keepdims=True))).astype(BF)
                gq.append(dot(ds, k))
                gk[...] += turned_dot(ds, qh)
                gv[...] += turned_dot(p, gh)
            gqkv[spot, pair * 128 : pair * 128 + 128] = (0.125 * jnp.where(low, *gq)).astype(BF)
            return carry

        lax.fori_loop(0, 4, rows, 0)
        gqkv[:, 256 + pair * 128 : 384 + pair * 128] = (0.125 * gk[...]).astype(BF)
        gqkv[:, 512 + pair * 128 : 640 + pair * 128] = gv[...].astype(BF)
    split_product(gqkv, lambda rows: dot_t(rows, wq[...]), keep, send)


def attention_grads(rows, h1, o, gy1, gqkv, outs, d_out):
    spots = slot_spots(rows, *outs)
    d_out[...] = turned_dot(o[...], gy1[...]).astype(BF)
    for (r, block), (_, y, x, zh) in zip(slot_blocks(), slot_places()):
        spots[r][0:128, 0:768] = turned_dot(h1[:, at(block, 128)], gqkv[...]).astype(BF)
        for h in range(2):
            spots[r][h * 64 : h * 64 + 64, 768:1024] = d_out[at(x * 2 + zh, 64), at(y * 2 + h, 256)]
    return spots


def window_1(h2, a, gy2, gu, *outs):
    mlp_grads(h2, a, gy2, gu, *outs)


def window_2(h1, o, gy1, gqkv, near_1, y_1, far_1, x_1, to_y, to_x, *rest):
    attention_grads(128, h1, o, gy1, gqkv, (to_y, to_x) + rest[:4], rest[4])
    second_sums(256, near_1, View(y_1, 256), far_1, View(x_1, 256), View(to_x, 256), View(to_y, 256))


def window_3(h2, a, gy2, gu, near_1, y_2, far_1, x_2, far_0, x_1, to_y, to_x, *rest):
    mlp_grads(h2, a, gy2, gu, to_y, to_x, *rest[:4])
    second_sums(128, near_1, View(y_2, 128), far_1, View(x_2, 128), View(to_x, 512), View(to_y, 512))
    third_sum(256, far_0, x_1, View(y_2, 256), rest[4])


def window_4(near_1, y_3, far_1, x_3, far_0, x_2, to_x, to_y, to_zh):
    second_sums(256, near_1, View(y_3, 256), far_1, View(x_3, 256), to_x, to_y)
    third_sum(128, far_0, x_2, View(y_3, 512), to_zh)


def window_5(*refs):
    grads, (to_y, to_x), rest = refs[:19], refs[19:21], refs[21:]
    last_attention_grads(*grads, (to_y, to_x) + rest[:4], *rest[4:])


def second_only(near_1, y, far_1, x, to_x, to_y):
    second_sums(144, near_1, View(y, 144), far_1, View(x, 144), to_x, to_y)


def third_only(far_0, x, y, to_zh):
    third_sum(256, far_0, x, y, to_zh)


def window_6(far_0, x_4, y_5, to_zh):
    third_sum(144, far_0, x_4, y_5, to_zh)


def last_attention_grads(
    h1, o, gy1, gqkv, g1, e1, e0, gu1, gu0, gq1, keep, s0, s1, s2, s3, t0, t1, t2, t3, outs, d_out, ups, wide
):
    spots = attention_grads(144, h1, o, gy1, gqkv, outs, d_out)
    send = Rows((s0, s1, s2, s3))
    none = jnp.zeros((2, 1024), F32)
    gain = jnp.zeros((1, 1024), F32)
    shift = jnp.zeros((1, 1024), F32)
    for i, block in enumerate((t0, t1, t2, t3)):
        dc, dl = RANKS[i]
        z, _ = normal(inner_columns(block[0].astype(F32)))
        which = bit("zl", dl)
        dh = send.block(which).astype(F32) if dc else keep[at(which, 128), :]
        gain = gain + jnp.sum(dh * z, axis=0, keepdims=True)
        shift = shift + jnp.sum(dh, axis=0, keepdims=True)
    parts = [g1[0:2, :], e1[2:3, :], e1[0:2, :], e1[3:4, :], none, gain, shift]
    wide[...] = jnp.concatenate(parts + [e0[2:3, :], e0[0:2, :], e0[3:4, :], none], axis=0)
    sums = [jnp.sum(v[...].astype(F32), axis=0, keepdims=True) for v in (gu1, gu0)]
    ups[...] = jnp.concatenate(sums + [jnp.zeros((14, 1024), F32)], axis=0)
    q = [jnp.sum(v[...].astype(F32), axis=0, keepdims=True) for v in (gq1, gqkv)]
    q = jnp.concatenate(q + [jnp.zeros((14, 768), F32)], axis=0)
    core, zl = lax.axis_index("core"), lax.axis_index("zl")
    for r, block in slot_blocks():
        rows = slice(128, 144)
        spots[r][rows, 0:128] = wide[:, at(block, 128)].astype(BF)
        spots[r][rows, 128:256] = ups[:, at(block, 128)].astype(BF)
        mine = jnp.where(block == 4 + zl * 2 + core, q[:, 512:768], jnp.zeros((16, 256), F32))
        mine = jnp.where(block == zl * 2 + core, q[:, 0:256], mine)
        spots[r][rows, 256:512] = mine.astype(BF)
        spots[r][rows, 512:1024] = jnp.zeros((16, 512), BF)


def summed(parts, rows, columns):
    value = parts[0][rows, columns].astype(F32)
    for part in parts[1:]:
        value = value + part[rows, columns].astype(F32)
    return value


def own_out(parts, flip):
    row = bit("y", flip) * 32
    halves = []
    for h in range(2):
        spot = pl.ds(pl.multiple_of(h * 64 + row, 32), 32)
        halves.append(summed(parts, spot, slice(768, 1024)))
    return jnp.concatenate(halves, axis=1)


def rank_rows(i):
    return at(bit("core", RANKS[i][0]) * 2 + bit("zl", RANKS[i][1]), 32)


def unpack_first(y_1, y_2, x_2, x_3, m_near, m_far, a_near, a_far, mine, *refs):
    mlp = (m_near, y_1, View(x_2, 256), m_far)
    att = (a_near, y_2, View(x_3, 512), a_far)
    sends, a, b, down = refs[0:3], refs[3], refs[4], refs[5]
    for i in range(4):
        to = mine if i == 0 else sends[i - 1]
        for parts, start, width in ((att, 0, 768), (mlp, 768, 1024)):
            value = summed(parts, rank_rows(i), slice(0, width))
            to[:, start : start + width] = value.astype(to.dtype)
    a[...] = own_out(att, 0).astype(BF)
    b[...] = own_out(att, 1).astype(BF)
    down[...] = inner_columns(summed(mlp, slice(128, 256), slice(0, 1024)))


def unpack_last(y_3, y_5, x_4, x_6, m_near, m_far, a_near, a_far, a1, b1, down_1, mine, *refs):
    mlp = (m_near, y_3, x_4, m_far)
    att = (a_near, y_5, x_6, a_far)
    sends, (a, b), down = refs[0:3], refs[3:5], refs[5]
    for i in range(4):
        to = mine if i == 0 else sends[i - 1]
        to[0:32, 0:768] = summed(att, rank_rows(i), slice(0, 768)).astype(to.dtype)
        to[0:32, 768:1792] = summed(mlp, rank_rows(i), slice(0, 1024)).astype(to.dtype)
        to[32:48, 0:768] = summed(att, slice(128, 144), slice(0, 768)).astype(to.dtype)
        to[32:48, 768:1792] = jnp.zeros((16, 1024), to.dtype)
    a[0:32, :] = own_out(att, 0).astype(BF)
    b[0:32, :] = own_out(att, 1).astype(BF)
    a[32:64, :] = a1[...]
    b[32:64, :] = b1[...]
    down[0] = inner_columns(summed(mlp, slice(128, 256), slice(0, 1024)))
    down[1] = down_1[...]


def finish(rest, r1, r2, r3, last, l1, l2, l3, a, b, *outs):
    g1, b1, w_qkv, qv, w_out, bo, g2, b2, w_up, up, bd = outs
    for i, (rm, lm) in enumerate(((rest, last), (r1, l1), (r2, l2), (r3, l3))):
        core, zl = bit("core", RANKS[i][0]), bit("zl", RANKS[i][1])
        for src, dst in qkv_blocks(core, zl):
            w_qkv[0, :, at(src, 128)] = lm[0:32, dst * 128 : dst * 128 + 128].astype(F32)
            w_qkv[1, :, at(src, 128)] = rm[:, dst * 128 : dst * 128 + 128].astype(F32)
        for src, dst in up_blocks(core, zl):
            w_up[0, :, at(src, 128)] = lm[0:32, 768 + dst * 128 : 896 + dst * 128].astype(F32)
            w_up[1, :, at(src, 128)] = rm[:, 768 + dst * 128 : 896 + dst * 128].astype(F32)
    low_zl = lax.axis_index("zl") == 0
    for l in range(2):
        va, vb = a[l * 32 : l * 32 + 32].astype(F32), b[l * 32 : l * 32 + 32].astype(F32)
        w = jnp.concatenate([jnp.where(low_zl, va, vb), jnp.where(low_zl, vb, va)], axis=1)
        w_out[l] = inner_columns(w)
    spot = lax.axis_index("core") * 2 + lax.axis_index("zl")

    def chunk(value, size):
        found = jnp.zeros((value.shape[0], size), F32)
        for j in range(4):
            found = jnp.where(spot == j, value[:, j * size : j * size + size], found)
        return found

    mine, by_core = last[32:48, 0:128], l1[32:48, 0:128].astype(F32)
    wide = chunk(mine + by_core, 32)
    late = l2[32:48, 0:128].astype(F32) + l3[32:48, 0:128].astype(F32)
    late = chunk(mine + by_core + late, 32)
    for row, ref in ((2, bo), (3, g2), (4, b2), (5, bd)):
        ref[...] = jnp.concatenate([wide[row + 8 : row + 9], wide[row : row + 1]], axis=0)
    g1[...] = jnp.concatenate([late[8:9], wide[0:1]], axis=0)
    b1[...] = jnp.concatenate([late[9:10], wide[1:2]], axis=0)
    up[...] = jnp.concatenate([last[33:34, 128:256], last[32:33, 128:256]], axis=0)
    both = last[32:48, 256:512]
    for m in (l1, l2, l3):
        both = both + m[32:48, 256:512].astype(F32)
    both = chunk(both, 64)
    qv[...] = jnp.concatenate([both[1:2], both[0:1]], axis=0)


def corner(value):
    return lax.ppermute(value, ("core", "zh"), [(0, 0), (1, 2), (2, 1), (3, 3)])


def to_partners(messages):
    one, two, three = messages
    return (
        swap(one, "core"),
        swap(two, "zl"),
        lax.ppermute(three, ("core", "zl"), [(0, 3), (3, 0), (1, 2), (2, 1)]),
    )


def narrow_body(
    tokens, segment_ids, group_order, ln1_gain, ln1_bias, qkv_weight, qv_bias, out_weight, out_bias,
    ln2_gain, ln2_bias, up_weight, up_bias, down_weight, down_bias, cotangent,
):
    small = (ln1_gain, ln1_bias, out_bias, ln2_gain, ln2_bias, down_bias, qv_bias, up_bias)

    def held(*values):
        return [pltpu.VMEM(v, BF) for v in values] + [pltpu.SemaphoreType.DMA((len(values),))]

    row, rowf = shape(256, 1024), shape(256, 1024, dtype=F32)
    quarters = [shape(64, 1024)] * 4

    ready = run(
        with_scratch(
            prepare_first, *held(*[v.shape for v in small], (2, 32, 1024), (32, 3072), (128, 1024))
        ),
        [shape(48, 768)] * 4 + [shape(64, 512)] * 2 + [shape(128, 1024)],
        *small, out_weight, qkv_weight, down_weight, anywhere=True, limit=60, us=3,
    )
    out_b = lax.ppermute(ready[5], ("y", "zl"), [(0, 2), (1, 0), (2, 3), (3, 1)])
    out_a = lax.ppermute(ready[4], ("y", "zl"), [(0, 0), (1, 2), (2, 1), (3, 3)])
    first = (ready[0],) + to_partners(ready[1:4])
    (att_0,) = run(pack_first, [shape(144, 1024)], *first, out_a, out_b)
    far, near_x, near_y = first_hops(att_0)
    block = corner(tokens)
    rest = run(
        with_scratch(
            prepare_rest, *held((32, 3072), (2, 32, 4096), (128, 1024), (128, 1024))
        ),
        [shape(32, 2816)] * 4 + [shape(128, 1024)] * 2,
        qkv_weight, up_weight, down_weight, cotangent, after=(ready[0],), anywhere=True, us=2,
    )
    cot = rest[5]
    mlp_0, up_0, deep, pair = run(
        pack_rest, [row, shape(128, 1024), row, shape(384, 1024)],
        rest[0], *to_partners(gate((att_0,), *rest[1:4])[:3]), out_a, out_b, ready[6],
    )
    down_1 = rest[4]
    def second_hops(kernel, rows_x, rows_y, *ins, after=(), rows=0):
        outs = [shape(n, 1024) for n in (rows_x, rows_y, rows) if n]
        to = run(kernel, outs, *ins, after=after)
        return swap(to[0], "x"), swap(to[1], "y"), both_ways(to[2] if rows else ins[0]), to[0]

    by_x, by_y, both, sent = second_hops(
        att_0_message, 224, 208, far, near_x, near_y, after=(pair,)
    )
    att_0 = (att_0, far, near_x, near_y, by_x, by_y, both)
    up_0, down_0, _ = gate((sent,), up_0, ready[6])
    far_up, far_down = swap(up_0, "zh"), swap(down_0, "zh")
    pair, deep, token = gate((by_x, by_y, both, far_up), pair, deep)
    pair_x, pair_y = swap(pair, "x"), swap(pair, "y")
    by_zl = swap(block, "zl")
    blocks = (block, swap(block, "core"), by_zl, swap(by_zl, "core"))
    segments = (segment_ids, swap(segment_ids, "core"), group_order)

    def cores(values):
        return [swap(v, "core") for v in values]

    def summed_core(keep, *send):
        (part,) = run(add_parts, [row], keep, *cores(send))
        return part, swap(part, "zl")

    def split_core(keep, *send, after=()):
        part, other = run(add_split, [shape(128, 1024)] * 2, keep, *cores(send), after=after)
        return part, swap(other, "zl")

    def with_other(values):
        return (*values, *cores(values))

    attention_outs = [
        shape(512, 1024), shape(512, 768), shape(4, 512, 512), shape(512, 256), rowf, *quarters,
    ]
    weights_scratch = [pltpu.VMEM((1024, 768), BF), pltpu.VMEM((256, 1024), BF)]
    dist = pltpu.VMEM((512, 512), F32)
    vec_scratch = [pltpu.VMEM((16, 1024), F32)] * 2
    mlp_outs = [shape(512, 1024), shape(512, 1024, dtype=F32), shape(512, 1024), rowf, *quarters]

    vec, h1_0, qkv_0, probs_0, o_0, keep, *send = run(
        with_scratch(first_attention, *vec_scratch, *weights_scratch, dist),
        [shape(16, 1024, dtype=F32)] + attention_outs, *blocks, *att_0, *segments, after=(token,), us=10,
    )
    far_down, pair_x, pair_y, deep, down_1, *send, _ = gate(
        (keep,), far_down, pair_x, pair_y, deep, down_1, *send
    )
    deep_far = swap(deep, "zh")
    part, came = summed_core(keep, *send)
    by_x, by_y, both, token = second_hops(
        mlp_0_message, 384, 384, far_up, far_down, pair_x, pair_y, after=(part,), rows=256
    )
    mlp_0 = (mlp_0, far_up, far_down, pair_x, pair_y, by_x, by_y, both)
    x1_0, *h = run(
        with_scratch(first_norm_stage, pltpu.VMEM((256, 1024), F32)),
        [rowf, *quarters], blocks[0], blocks[2], part, came, vec, after=(token,), us=1.5,
    )
    h2_0, u_0, a_0, keep, *send = run(
        mlp_stage(0), mlp_outs, *with_other(h), *mlp_0, vec, after=(deep_far,), us=4
    )
    down_1_far = swap(down_1, "zh")
    one_x, one_y, both, token = second_hops(
        att_1_message, 448, 448, deep_far, pair_x, pair_y, deep, down_1, after=(keep,), rows=128
    )
    att_1 = (deep, deep_far, pair_x, pair_y, one_x, one_y, both)
    part, came = summed_core(keep, *send)
    x2_0, *h = run(norm_stage(5, 8), [rowf, *quarters], x1_0, part, came, vec, after=(token, down_1_far), us=1)
    by_x, by_y, both, token = second_hops(
        mlp_1_message, 384, 384, deep_far, down_1_far, one_x, one_y, rows=256
    )
    h1_1, qkv_1, probs_1, o_1, keep, *send = run(
        with_scratch(next_attention, *weights_scratch, dist),
        attention_outs, *with_other(h), *att_1, vec, *segments, after=(token,), us=9,
    )
    mlp_1 = (deep, down_1, deep_far, down_1_far, one_x, one_y, by_x, by_y, both)
    cot, _ = gate((keep,), cot)
    cot = corner(cot)
    part, came = summed_core(keep, *send)
    x1_1, *h = run(norm_stage(10, 11), [rowf, *quarters], x2_0, part, came, vec, after=(token,), us=1)
    by_zl = swap(cot, "zl")
    cots = (cot, swap(cot, "core"), by_zl, swap(by_zl, "core"))
    h2_1, u_1, a_1, keep, *send = run(mlp_stage(1), mlp_outs, *with_other(h), *mlp_1, vec, us=4)

    mlp_back_outs = [shape(512, 1024), shape(512, 1024), rowf, *quarters]
    norm_outs = [rowf, *quarters, shape(8, 1024, dtype=F32)]
    attention_back_outs = [shape(512, 1024), shape(512, 768), rowf, *quarters]
    attention_back_scratch = weights_scratch + [
        pltpu.VMEM((512, 256), BF), pltpu.VMEM((512, 128), F32), pltpu.VMEM((512, 128), F32),
    ]

    def grad_outs(sent, rows):
        return [shape(sent, 1024)] * 2 + [shape(rows, 1024)] * 4

    out_scratch = pltpu.VMEM((256, 1024), BF)

    keep_last, send_last = keep, send
    gy2, gu_1, keep, *send = run(mlp_back(1), mlp_back_outs, *cots, u_1, *mlp_1, us=6)
    part, came = summed_core(keep, *send)
    to_y, to_x, m1_near_0, m1_near_1, m1_far_0, m1_far_1 = run(
        window_1, grad_outs(512, 256), h2_1, a_1, gy2, gu_1, after=(part,), us=4
    )
    y_1, x_1 = swap(to_y, "y"), swap(to_x, "x")
    gm, *gy, e1 = run(
        with_scratch(first_norm_back, pltpu.VMEM((256, 1024), F32)),
        norm_outs, cots[0], cots[2], part, came, x1_1, vec, after=(m1_far_1,), us=1.5,
    )
    gy1, gqkv_1, keep, *send = run(
        with_scratch(attention_back(1), *attention_back_scratch),
        attention_back_outs, *with_other(gy), qkv_1, probs_1, *att_1, us=9,
    )
    part, came = summed_core(keep, *send)
    to_y, to_x, a1_near_0, a1_near_1, a1_far_0, a1_far_1 = run(
        with_scratch(window_2, out_scratch), grad_outs(512, 128), h1_1, o_1, gy1, gqkv_1,
        m1_near_1, y_1, m1_far_1, x_1, after=(part,), us=3,
    )
    y_2, x_2 = swap(to_y, "y"), swap(to_x, "x")
    part_last, came_last = split_core(keep_last, *send_last)
    (final,) = run(finish_rows, [shape(1, 128, 1024)], x1_1, part_last, came_last, vec)
    output = corner(final)
    gx, *gy, g1 = run(
        norm_back_stage(8), norm_outs, gm, part, came, x2_0, vec, after=(a1_far_1,), us=1.5
    )
    gy2, gu_0, keep, *send = run(
        mlp_back(0), mlp_back_outs, *with_other(gy), u_0, *mlp_0, us=6
    )
    part, came = summed_core(keep, *send)
    to_y, to_x, m0_near_0, m0_near_1, m0_far_0, m0_far_1, to_zh = run(
        window_3, grad_outs(640, 256) + [row], h2_0, a_0, gy2, gu_0,
        a1_near_1, y_2, a1_far_1, x_2, m1_far_0, x_1, after=(part,), us=4,
    )
    y_3, x_3, m1_far_3 = swap(to_y, "y"), swap(to_x, "x"), swap(to_zh, "zh")
    gm, *gy, e0 = run(
        norm_back_stage(3), norm_outs, gx, part, came, x1_0, vec, after=(m0_far_1,), us=1.5
    )
    gy1, gqkv_0, keep, *send = run(
        with_scratch(attention_back(0), *attention_back_scratch),
        attention_back_outs, *with_other(gy), qkv_0, probs_0, *att_0, us=9,
    )
    part, came = split_core(keep, *send, after=(m1_far_3, output))
    to_x, to_y, to_zh = run(
        window_4, [row, row, shape(128, 1024)], m0_near_1, y_3, m0_far_1, x_3, a1_far_0, x_2, after=(part,)
    )
    x_4, y_4, a1_far_3 = swap(to_x, "x"), swap(to_y, "y"), swap(to_zh, "zh")
    to_y, to_x, a0_near_0, a0_near_1, a0_far_0, a0_far_1 = run(
        with_scratch(window_5, out_scratch, *vec_scratch), grad_outs(288, 144),
        h1_0, o_0, gy1, gqkv_0, g1, e1, e0, gu_1, gu_0, gqkv_1, keep, *send, *blocks,
        after=(part, to_zh), us=3,
    )
    y_5, x_5 = swap(to_y, "y"), swap(to_x, "x")
    (grad,) = run(
        with_scratch(
            last_norm_back, *[pltpu.VMEM((128, 1024), F32)] * 3, pltpu.VMEM((128, 1024), BF),
            pltpu.VMEM((8, 1024), F32),
        ),
        [shape(1, 128, 1024)], gm, part, came, blocks[0], vec, after=(a0_far_1,), us=1.5,
    )
    tokens_grad = corner(grad).astype(F32)
    (to_zh,) = run(third_only, [row], m0_far_0, x_3, y_4, after=(grad, a1_far_3))
    m0_far_3 = swap(to_zh, "zh")
    to_x, to_y = run(second_only, [shape(144, 1024)] * 2, a0_near_1, y_5, a0_far_1, x_5, after=(to_zh,))
    x_6, y_6 = swap(to_x, "x"), swap(to_y, "y")
    rest = run(
        unpack_first,
        [shape(32, 1792, dtype=F32)] + [shape(32, 1792)] * 3 + [shape(32, 512)] * 2
        + [shape(128, 1024, dtype=F32)],
        y_1, y_2, x_2, x_3, m1_near_0, m1_far_3, a1_near_0, a1_far_3, us=2,
    )
    rest_came = to_partners(rest[1:4])
    (to_zh,) = run(window_6, [shape(144, 1024)], a0_far_0, x_5, y_6)
    a0_far_3 = swap(to_zh, "zh")
    last = run(
        unpack_last,
        [shape(48, 1792, dtype=F32)] + [shape(48, 1792)] * 3 + [shape(64, 512)] * 2
        + [shape(2, 128, 1024, dtype=F32)],
        y_3, y_5, x_4, x_6, m0_near_0, m0_far_3, a0_near_0, a0_far_3, rest[4], rest[5], rest[6],
        after=rest_came,
    )
    back_a = lax.ppermute(last[4], ("y", "zl"), [(0, 0), (1, 2), (2, 1), (3, 3)])
    back_b = lax.ppermute(last[5], ("y", "zl"), [(0, 1), (1, 3), (2, 0), (3, 2)])
    sizes = (
        (2, 32), (2, 32), (2, 32, 3072), (2, 64), (2, 32, 1024), (2, 32), (2, 32), (2, 32),
        (2, 32, 4096), (2, 128), (2, 32),
    )
    g = run(
        finish, [shape(*s, dtype=F32) for s in sizes],
        rest[0], *rest_came, last[0], *to_partners(last[1:4]), back_a, back_b, us=2,
    )
    return (output, tokens_grad) + tuple(g[:10]) + (last[6], g[10])


def solution(mesh):
    fsdp, ctx = mesh.shape["fsdp"], mesh.shape["ctx"]
    fine = Mesh(mesh.devices.reshape(fsdp // 4, 2, 2, 2, ctx // 2), AXES)
    body = narrow_body if fine.devices.shape == (2, 2, 2, 2, 2) else wide_body
    stream, place = ("y", "x", "core"), ("zh", "zl")
    rows = P(stream, place, None)
    flat, deep = P(None, AXES), P(None, AXES, None)
    params = (flat, flat, deep, flat, deep, flat, flat, flat, deep, flat, deep, flat)
    in_specs = (rows, P(stream, None), P()) + params + (rows,)
    out_specs = (rows, rows) + params
    return jax.shard_map(body, mesh=fine, in_specs=in_specs, out_specs=out_specs, check_vma=False)
```

```python
import jax
import jax.numpy as jnp
from jax import lax
from jax.experimental import pallas as pl
from jax.experimental.pallas import tpu as pltpu
from jax.sharding import Mesh, PartitionSpec as P

HEADS = 16
EPSILON = 1e-05
BF = jnp.bfloat16
F32 = jnp.float32
AXES = ("y", "x", "core", "zh", "zl")


def here(axis):
    return lax.axis_index(axis)


def swap(value, axis):
    return lax.ppermute(value, axis, [(0, 1), (1, 0)])


def ordered(mine, other, axis):
    first = here(axis) == 0
    return jnp.stack([jnp.where(first, mine, other), jnp.where(first, other, mine)])


def pick(value, axis):
    return lax.dynamic_index_in_dim(value, here(axis), 0, keepdims=False)


def pick_other(value, axis):
    return lax.dynamic_index_in_dim(value, 1 - here(axis), 0, keepdims=False)


def trade(value, axis):
    if lax.axis_size(axis) == 2:
        return ordered(pick(value, axis), swap(pick_other(value, axis), axis), axis)
    return lax.all_to_all(value, axis, 0, 0, tiled=True)


def collect(value, axis):
    if lax.axis_size(axis) == 2:
        return ordered(value, swap(value, axis), axis)
    return lax.all_gather(value, axis, axis=0, tiled=False)


def reduce_to(value, axis):
    if lax.axis_size(axis) == 2:
        return pick(value, axis) + swap(pick_other(value, axis), axis)
    return lax.psum_scatter(value, axis, scatter_dimension=0, tiled=False)


def flipped(value, axis, dim):
    return jnp.where(here(axis) == 0, value, jnp.flip(value, dim))


def gather_shards(shard):
    if lax.axis_size("y") != 2:
        return lax.all_gather(shard, ("y", "x", "zh"), axis=0, tiled=False)
    far = swap(shard, "zh")
    near_x = swap(shard, "x")
    far_y = swap(far, "y")
    near_y = swap(shard, "y")
    near_xy = swap(near_x, "y")
    far_x = swap(far, "x")
    far_yx = swap(far_y, "x")
    rel = jnp.stack([shard, far, near_x, far_x, near_y, far_y, near_xy, far_yx])
    rel = rel.reshape((2, 2, 2) + shard.shape)
    rel = flipped(flipped(flipped(rel, "y", 0), "x", 1), "zh", 2)
    return rel.reshape((8,) + shard.shape)


def scatter_shards(grads):
    shape = grads.shape[1:]
    if lax.axis_size("y") != 2:
        return lax.psum_scatter(
            grads, ("y", "x", "zh"), scatter_dimension=0, tiled=False
        )
    rel = grads.reshape((2, 2, 2) + shape)
    rel = flipped(flipped(flipped(rel, "y", 0), "x", 1), "zh", 2)
    near, far = rel[:, :, 0], rel[:, :, 1]
    far = far[:, 0] + swap(far[:, 1].astype(BF), "x").astype(F32)
    near = near[0] + swap(near[1].astype(BF), "y").astype(F32)
    far = far[0] + swap(far[1].astype(BF), "y").astype(F32)
    near = near[0] + swap(near[1].astype(BF), "x").astype(F32)
    return near + swap(far.astype(BF), "zh").astype(F32)


def corner_turn(value):
    return lax.ppermute(value, ("core", "zh"), [(0, 0), (1, 2), (2, 1), (3, 3)])


def norm_rows(values, gain, shift):
    row_mean = jnp.mean(values, axis=-1, keepdims=True)
    centred = values - row_mean
    row_var = jnp.mean(centred * centred, axis=-1, keepdims=True)
    return centred * lax.rsqrt(row_var + EPSILON) * gain + shift


def gelu_tanh(values):
    return jax.nn.gelu(values, approximate=True)


def dot(left, right):
    return jnp.dot(left, right, preferred_element_type=F32)


def dot_t(left, matrix):
    return lax.dot_general(
        left, matrix, (((1,), (1,)), ((), ())), preferred_element_type=F32
    )


def outer_sum(left, right):
    return jnp.einsum("td,te->de", left, right, preferred_element_type=F32)


def wide_body(
    tokens,
    segment_ids,
    group_order,
    ln1_gain,
    ln1_bias,
    qkv_weight,
    qv_bias,
    out_weight,
    out_bias,
    ln2_gain,
    ln2_bias,
    up_weight,
    up_bias,
    down_weight,
    down_bias,
    cotangent,
):
    ny, nx, nc, nzh, nzl = (lax.axis_size(a) for a in AXES)
    chips = ny * nx
    span = chips // nzl
    layers, width = ln1_gain.shape[0], tokens.shape[2]
    hidden = up_weight.shape[2]
    group = tokens.shape[1]
    ctx_count = nzh * nzl
    rank_width = width // (nc * nzl)
    rank_hidden = hidden // (nc * nzl)
    head_size = width // HEADS
    rank_heads = rank_width // head_size
    quarter = width // (chips * nc)
    unit = width // (chips * nc * nzh)
    core_rows = nzl * group
    rows = nc * core_rows
    scale = head_size ** (-0.5)

    def inner(value):
        shape = value.shape
        value = value.reshape(shape[:-1] + (chips, 2, 2, unit))
        return jnp.swapaxes(value, -3, -2).reshape(shape)

    small = (ln1_gain, ln1_bias, out_bias, ln2_gain, ln2_bias, down_bias)
    small_all = small + (qv_bias, up_bias)
    packed = jnp.concatenate([v.reshape(-1) for v in small_all])
    for axis in reversed(AXES):
        packed = collect(packed, axis)
    vectors = []
    at = 0
    for v in small_all:
        size = v.shape[0] * v.shape[1]
        part = packed[..., at : at + size].reshape((ny, nx, nc, nzh, nzl) + v.shape)
        part = jnp.moveaxis(part, 5, 0)
        vectors.append(part.reshape(layers, -1).astype(F32))
        at += size
    vec = [inner(v) for v in vectors[:6]]
    full_qv, full_up = vectors[6], vectors[7]

    def rank_columns(value):
        shape = value.shape[:-1]
        value = value.reshape(shape + (nzl, span, nc, quarter))
        value = lax.dynamic_index_in_dim(value, here("zl"), len(shape), keepdims=False)
        value = lax.dynamic_index_in_dim(value, here("core"), len(shape) + 1, keepdims=False)
        return value.reshape(shape + (rank_width,))

    q_bias = rank_columns(full_qv[:, :width])
    v_bias = rank_columns(full_qv[:, width:])
    qkv_bias = jnp.concatenate([q_bias, jnp.zeros_like(q_bias), v_bias], axis=1)
    up_b = full_up.reshape(layers, chips, nc, nzh, nzl, -1)
    up_b = lax.dynamic_index_in_dim(up_b, here("zl"), 4, keepdims=False)
    up_b = lax.dynamic_index_in_dim(up_b, here("core"), 2, keepdims=False)
    up_b = up_b.reshape(layers, rank_hidden)

    def to_ranks(value):
        value = trade(value, "core")
        return jnp.swapaxes(trade(jnp.swapaxes(value, 0, 1), "zl"), 0, 1)

    def fetch(layer):
        w = qkv_weight[layer]
        n = w.shape[0]
        w = w.reshape(n, 3, nzl, span, nc, quarter)
        w = jnp.transpose(w, (4, 2, 0, 1, 3, 5)).reshape(nc, nzl, n, 3 * rank_width)
        w_qkv = gather_shards(to_ranks(w).reshape(-1, 3 * rank_width))
        w = gather_shards(inner(out_weight[layer]))
        w = trade(w.reshape(nzl, span, nzh, n, width), "zl")
        w_out = jnp.transpose(w, (1, 2, 0, 3, 4)).reshape(rank_width, width)
        w = up_weight[layer].reshape(n, chips, nc, nzh, nzl, -1)
        w = jnp.transpose(w, (2, 4, 0, 1, 3, 5)).reshape(nc, nzl, n, rank_hidden)
        w_up = gather_shards(to_ranks(w).reshape(-1, rank_hidden))
        w_down = gather_shards(inner(down_weight[layer]))
        return (
            w_qkv.reshape(width, 3 * rank_width),
            w_out,
            w_up.reshape(width, rank_hidden),
            w_down.reshape(rank_hidden, width),
        )

    def from_ranks(value):
        value = jnp.swapaxes(trade(jnp.swapaxes(value, 0, 1), "zl"), 0, 1)
        return trade(value, "core")

    def send(grads):
        g_qkv, g_out, g_up, g_down = grads
        n = width // (chips * 2 * ctx_count)
        g = scatter_shards(g_qkv.reshape(chips * nzh, -1, 3 * rank_width))
        g = from_ranks(g.astype(BF).reshape(nc, nzl, n, 3 * rank_width)).astype(F32)
        g = g.reshape(nc, nzl, n, 3, span, quarter)
        d_qkv = jnp.transpose(g, (2, 3, 1, 4, 0, 5)).reshape(n, 3 * width)
        g = g_out.astype(BF).reshape(span, nzh, nzl, n, width)
        g = trade(jnp.transpose(g, (2, 0, 1, 3, 4)), "zl").astype(F32)
        d_out = inner(scatter_shards(g.reshape(chips * nzh, n, width)))
        g = scatter_shards(g_up.reshape(chips * nzh, -1, rank_hidden))
        g = from_ranks(g.astype(BF).reshape(nc, nzl, n, rank_hidden)).astype(F32)
        g = g.reshape(nc, nzl, n, chips, nzh, -1)
        d_up = jnp.transpose(g, (2, 3, 0, 4, 1, 5)).reshape(n, hidden)
        d_down = inner(scatter_shards(g_down.reshape(chips * nzh, -1, width)))
        return d_qkv, d_out, d_up, d_down

    def own_columns(value, mine):
        value = inner(value).reshape(ny, nx, nc, nzh, nzl, -1)
        keep = jnp.arange(nzl)[:, None] == here("zl")
        return jnp.where(keep, value, 0.0)

    def send_small(sums):
        g1, b1, gqv, bo, g2, b2, bu, bd = sums
        parts = [own_columns(v, None) for v in (g1, b1, bo, g2, b2, bd)]

        def placed(value):
            value = value.reshape(1, span, 1, quarter)
            keep = (jnp.arange(nzl)[:, None, None, None] == here("zl")) & (
                jnp.arange(nc)[None, None, :, None] == here("core")
            )
            return jnp.where(keep, value, 0.0).reshape(width)

        qv = jnp.concatenate([placed(gqv[0]), placed(gqv[1])])
        parts.append(qv.reshape(ny, nx, nc, nzh, nzl, -1))
        up = bu.reshape(ny, nx, 1, nzh, 1, -1)
        keep = (jnp.arange(nzl)[:, None] == here("zl")) & (
            jnp.arange(nc)[:, None, None, None] == here("core")
        )
        parts.append(jnp.where(keep, up, 0.0))
        value = jnp.concatenate(parts, axis=-1)
        for axis in AXES:
            value = reduce_to(value, axis)
        sizes = [p.shape[-1] for p in parts]
        cut, at = [], 0
        for s in sizes:
            cut.append(value[at : at + s])
            at += s
        g1, b1, bo, g2, b2, bd, qv, up = cut
        return g1, b1, qv, bo, g2, b2, up, bd

    def place(value):
        return collect(inner(corner_turn(value)), "zl").reshape(core_rows, width)

    def both_cores(value):
        return collect(value, "core").reshape(rows, -1)

    def total(partial):
        part = partial.reshape(nc, core_rows, width)
        part = pick(part, "core") + swap(pick_other(part, "core").astype(BF), "core").astype(F32)
        if nzl == 2:
            return part + swap(part.astype(BF), "zl").astype(F32)
        return lax.psum(part, "zl")

    seg = collect(segment_ids[0], "core")
    seg = lax.dynamic_index_in_dim(seg, here("zh"), 0, keepdims=False)
    half = group // 2
    block = jnp.stack([group_order, 2 * ctx_count - 1 - group_order], axis=1)
    pos = (block[:, :, None] * half + jnp.arange(half, dtype=jnp.int32)).reshape(rows)
    row_seg = jnp.take(seg, pos)
    distance = pos[:, None] - pos[None, :]
    allowed = (distance >= 0) & (row_seg[:, None] == row_seg[None, :])
    distance = distance.astype(F32)
    head_no = jnp.arange(rank_heads)
    head_no = (
        (here("zl") * span + head_no // (quarter // head_size)) * nc + here("core")
    ) * (quarter // head_size) + head_no % (quarter // head_size)
    slopes = jnp.exp2(-8.0 * (head_no.astype(F32) + 1.0) / HEADS)

    def scores_of(q, k):
        s = jnp.einsum("qhd,khd->hqk", q, k, preferred_element_type=F32) * scale
        return s - slopes[:, None, None] * distance[None]

    def split(qkv):
        return [
            v.reshape(rows, rank_heads, head_size) for v in jnp.split(qkv, 3, axis=1)
        ]

    weights = [fetch(layer) for layer in range(layers)]
    x = place(tokens[0]).astype(F32)
    kept = []
    for layer in range(layers):
        w_qkv, w_out, w_up, w_down = weights[layer]
        g1, b1, bo, g2, b2, bd = (v[layer] for v in vec)
        h1 = both_cores(norm_rows(x, g1, b1).astype(BF))
        qkv = (dot(h1, w_qkv) + qkv_bias[layer]).astype(BF)
        q, k, v = split(qkv)
        s = jnp.where(allowed, scores_of(q, k), -1e30)
        top = jnp.max(s, axis=-1, keepdims=True)
        p = jnp.where(allowed, jnp.exp(s - top), 0.0)
        den = jnp.sum(p, axis=-1, keepdims=True)
        p = p / den
        o = jnp.einsum("hqk,khd->qhd", p.astype(BF), v, preferred_element_type=F32)
        log_total = top + jnp.log(den)
        o = o.reshape(rows, rank_width).astype(BF)
        x1 = x + total(dot(o, w_out)) + bo
        h2 = both_cores(norm_rows(x1, g2, b2).astype(BF))
        u = dot(h2, w_up) + up_b[layer]
        a = gelu_tanh(u).astype(BF)
        x2 = x1 + total(dot(a, w_down)) + bd
        kept.append((x, h1, qkv, log_total, o, x1, h2, u, a))
        x = x2

    def leave(value):
        mine = lax.dynamic_index_in_dim(
            value.reshape(nzl, group, width), here("zl"), 0, keepdims=False
        )
        return corner_turn(inner(mine))[None]

    final_rows = leave(x.astype(BF))

    gx = place(cotangent[0]).astype(F32)
    result = [None] * layers
    for layer in reversed(range(layers)):
        w_qkv, w_out, w_up, w_down = weights[layer]
        g1, b1, bo, g2, b2, bd = (v[layer] for v in vec)
        x, h1, qkv, log_total, o, x1, h2, u, a = kept[layer]
        gy2_mine = gx.astype(BF)
        gy2 = both_cores(gy2_mine)
        d_down = outer_sum(a, gy2)
        d_bd = jnp.sum(gy2_mine.astype(F32), axis=0)
        _, gelu_back = jax.vjp(gelu_tanh, u)
        gu = gelu_back(dot_t(gy2, w_down))[0].astype(BF)
        d_up = outer_sum(h2, gu)
        d_bu = jnp.sum(gu.astype(F32), axis=0)
        _, back = jax.vjp(norm_rows, x1, g2, b2)
        gn, d_g2, d_b2 = back(total(dot_t(gu, w_up)))
        gm = gx + gn
        gy1_mine = gm.astype(BF)
        gy1 = both_cores(gy1_mine)
        d_out = outer_sum(o, gy1)
        d_bo = jnp.sum(gy1_mine.astype(F32), axis=0)
        go_f = dot_t(gy1, w_out)
        go = go_f.astype(BF).reshape(rows, rank_heads, head_size)
        q, k, v = split(qkv)
        p = jnp.where(allowed, jnp.exp(scores_of(q, k) - log_total), 0.0)
        dp = jnp.einsum("qhd,khd->hqk", go, v, preferred_element_type=F32)
        ds = (p * (dp - jnp.sum(dp * p, axis=-1, keepdims=True))).astype(BF)
        gq = scale * jnp.einsum("hqk,khd->qhd", ds, k, preferred_element_type=F32)
        gk = scale * jnp.einsum("hqk,qhd->khd", ds, q, preferred_element_type=F32)
        gv = jnp.einsum("hqk,qhd->khd", p.astype(BF), go, preferred_element_type=F32)
        gqkv = jnp.concatenate(
            [g.reshape(rows, rank_width) for g in (gq, gk, gv)], axis=1
        ).astype(BF)
        d_qkv = outer_sum(h1, gqkv)
        sums = jnp.sum(gqkv.astype(F32), axis=0)
        _, back = jax.vjp(norm_rows, x, g1, b1)
        gn, d_g1, d_b1 = back(total(dot_t(gqkv, w_qkv)))
        gx = gm + gn
        d_qv = (sums[:rank_width], sums[2 * rank_width :])
        big = send((d_qkv, d_out, d_up, d_down))
        tiny = send_small((d_g1, d_b1, d_qv, d_bo, d_g2, d_b2, d_bu, d_bd))
        result[layer] = (
            tiny[0], tiny[1], big[0], tiny[2], big[1], tiny[3],
            tiny[4], tiny[5], big[2], tiny[6], big[3], tiny[7],
        )
    stacked = [jnp.stack([result[layer][i] for layer in range(layers)]) for i in range(12)]
    return (final_rows, leave(gx)) + tuple(stacked)


def bit(axis, flip):
    place = lax.axis_index(axis)
    return 1 - place if flip else place


def slot_places():
    for slot in range(8):
        yield slot, bit("y", slot & 4), bit("x", slot & 2), bit("zh", slot & 1)


class View:
    def __init__(self, ref, row):
        self.ref, self.row = ref, row

    def _spot(self, spot):
        rows, columns = spot if isinstance(spot, tuple) else (spot, slice(None))
        if isinstance(rows, slice):
            return slice(rows.start + self.row, rows.stop + self.row), columns
        return pl.ds(rows.start + self.row, rows.size), columns

    def __getitem__(self, spot):
        return self.ref[self._spot(spot)]

    def __setitem__(self, spot, value):
        self.ref[self._spot(spot)] = value


class Rows:
    def __init__(self, refs):
        self.refs, self.size = refs, refs[0].shape[0]

    def _span(self, spot):
        rows = spot[0] if isinstance(spot, tuple) else spot
        if rows is Ellipsis:
            return 0, len(self.refs)
        return rows.start // self.size, rows.stop // self.size

    def __getitem__(self, spot):
        first, last = self._span(spot)
        return jnp.concatenate([r[...] for r in self.refs[first:last]], axis=0)

    def __setitem__(self, spot, value):
        first, last = self._span(spot)
        for i in range(first, last):
            self.refs[i][...] = value[(i - first) * self.size : (i - first + 1) * self.size]

    def block(self, which):
        low, high = self[slice(0, 128), :], self[slice(128, 256), :]
        return jnp.where(which == 0, low, high)


class Joined:
    def __init__(self, low, high, cut):
        self.low, self.high, self.cut = low, high, cut

    def __getitem__(self, spot):
        rows, columns = spot
        parts = []
        if rows.start < self.cut:
            parts.append(self.low[rows.start : min(rows.stop, self.cut), columns])
        if rows.stop > self.cut:
            parts.append(self.high[max(rows.start, self.cut) - self.cut : rows.stop - self.cut, columns])
        return parts[0] if len(parts) == 1 else jnp.concatenate(parts, axis=0)


def eight_slots(own, far, near_x, near_y, by_x, by_y, both, rows):
    cut = 128 if rows == 256 else 64
    across = Joined(View(by_y, rows), View(by_x, rows), cut)
    return own, far, near_x, by_x, near_y, by_y, across, both


def att_0_slots(refs):
    return eight_slots(*refs, 144)


def mlp_0_slots(refs):
    own, far_up, far_down, *refs = refs
    return eight_slots(own, Joined(far_up, far_down, 128), *refs, 256)


def att_1_slots(refs):
    own, far, by_x_1, by_y_1, by_x, by_y, both = refs
    return eight_slots(own, View(far, 0), View(by_x_1, 256), View(by_y_1, 256), by_x, by_y, both, 128)


def mlp_1_slots(refs):
    own, own_down, far, far_down, by_x_1, by_y_1, by_x, by_y, across_x, across_y, both = refs
    own, far = Joined(View(own, 128), own_down, 128), Joined(View(far, 128), far_down, 128)
    across = Joined(across_y, across_x, 128)
    return own, far, View(by_x_1, 192), by_x, View(by_y_1, 192), by_y, across, both


def second_message(far, near_x, near_y, to_x, to_y, rows):
    cut = 128 if rows == 256 else 64
    to_x[0:rows, :] = far[0:rows, :]
    to_y[0:rows, :] = far[0:rows, :]
    to_y[rows : rows + cut, :] = near_x[0:cut, :]
    to_x[rows : 2 * rows - cut, :] = near_y[cut:rows, :]


def att_0_message(far, near_x, near_y, to_x, to_y):
    second_message(far, near_x, near_y, to_x, to_y, 144)


def mlp_0_message(far_up, far_down, near_x, near_y, to_x, to_y, to_both):
    far = Joined(far_up, far_down, 128)
    to_both[...] = far[0:256, :]
    second_message(far, near_x, near_y, to_x, to_y, 256)


def att_1_message(far, near_x, near_y, own, own_down, to_x, to_y, to_both):
    to_both[...] = far[0:128, :]
    second_message(far, View(near_x, 256), View(near_y, 256), to_x, to_y, 128)
    for to in (to_x, to_y):
        to[192:320, :] = own[128:256, :]
        to[320:448, :] = own_down[...]


def mlp_1_message(far, far_down, near_x, near_y, to_all, to_x, to_y):
    to_all[...] = Joined(View(far, 128), far_down, 128)[0:256, :]
    to_y[...] = near_x[192:320, :]
    to_x[...] = near_y[320:448, :]


def slot_blocks():
    return [(r, (y * 2 + x) * 2 + zh) for r, y, x, zh in slot_places()]


def at(block, size):
    return pl.ds(pl.multiple_of(block * size, size), size)


def run(kernel, outs, *ins, after=(), us=1.0, anywhere=False, limit=16):
    smem = pl.BlockSpec(memory_space=pltpu.SMEM)
    vmem = pl.BlockSpec(memory_space=pltpu.VMEM)
    free = pl.BlockSpec(memory_space=pl.ANY)
    skip = len(after)

    def body(*refs):
        kernel(*refs[skip:])

    return pl.pallas_call(
        body,
        out_shape=tuple(outs),
        in_specs=[free] * skip
        + [smem if v.size == 4 else free if anywhere else vmem for v in ins],
        out_specs=tuple(vmem for _ in outs),
        scratch_shapes=getattr(kernel, "scratch", []),
        compiler_params=pltpu.CompilerParams(vmem_limit_bytes=limit << 20),
        cost_estimate=pl.CostEstimate(flops=int(us * 1e7), bytes_accessed=0, transcendentals=0),
    )(*after, *ins)


def gate(after, *values):
    skip = len(after)

    def body(*refs):
        refs[-1][...] = jnp.zeros_like(refs[-1])

    free = pl.BlockSpec(memory_space=pl.ANY)
    return pl.pallas_call(
        body,
        out_shape=tuple(shape(*v.shape, dtype=v.dtype) for v in values) + (shape(8, 128, dtype=F32),),
        in_specs=[free] * (skip + len(values)),
        out_specs=tuple(free for _ in values) + (pl.BlockSpec(memory_space=pltpu.VMEM),),
        input_output_aliases={skip + i: i for i in range(len(values))},
        compiler_params=pltpu.CompilerParams(vmem_limit_bytes=16 << 20),
        cost_estimate=pl.CostEstimate(flops=10**4, bytes_accessed=0, transcendentals=0),
    )(*after, *values)


def shape(*sizes, dtype=BF):
    return jax.ShapeDtypeStruct(sizes, dtype)


def with_scratch(kernel, *scratch):
    kernel.scratch = list(scratch)
    return kernel


def inner_columns(value):
    low = lax.broadcasted_iota(jnp.int32, (value.shape[0], 128), 1) < 64
    parts = []
    for i in range(0, value.shape[1], 256):
        a, b = value[:, i : i + 128], value[:, i + 128 : i + 256]
        parts.append(jnp.where(low, a, pltpu.roll(b, 64, 1)))
        parts.append(jnp.where(low, pltpu.roll(a, 64, 1), b))
    return jnp.concatenate(parts, axis=1)


def spread(value):
    n = value.shape[1]
    if n == 128:
        return value.astype(F32)
    hit = lax.broadcasted_iota(jnp.int32, (n, 128), 1) % n == lax.broadcasted_iota(
        jnp.int32, (n, 128), 0
    )
    return dot(value.astype(F32), hit.astype(F32))


RANKS = ((0, 0), (1, 0), (0, 1), (1, 1))


def qkv_blocks(core, zl):
    return [
        (s * 8 + zl * 4 + x * 2 + core, s * 2 + x) for s in range(3) for x in range(2)
    ]


def up_blocks(core, zl):
    return [
        (chip * 8 + core * 4 + zh * 2 + zl, chip * 2 + zh)
        for chip in range(4)
        for zh in range(2)
    ]


def fetch(sources, held, sems):
    copies = [pltpu.make_async_copy(*pair, sems.at[i]) for i, pair in enumerate(zip(sources, held))]
    for copy in copies:
        copy.start()
    for copy in copies:
        copy.wait()


def prepare_first(*refs):
    sources, refs = refs[:11], refs[11:]
    first, (out_a, out_b, down), (held, sems) = refs[0:4], refs[4:7], (refs[7:18], refs[18])
    fetch(sources[:9] + (sources[9].at[0], sources[10].at[0]), held, sems)
    rows = [spread(v[...]) for v in held[:8]]
    w_out, w_qkv, w_down = held[8:]
    small = jnp.concatenate([v[l : l + 1] for l in range(2) for v in rows], axis=0)
    for i, (dc, dl) in enumerate(RANKS):
        for src, dst in qkv_blocks(bit("core", dc), bit("zl", dl)):
            first[i][0:32, dst * 128 : dst * 128 + 128] = w_qkv[:, at(src, 128)]
        first[i][32:48, 0:128] = small.astype(BF)
        first[i][32:48, 128:768] = jnp.zeros((16, 640), BF)
    low_zl = lax.axis_index("zl") == 0
    for l in range(2):
        w = inner_columns(w_out[l].astype(F32)).astype(BF)
        out_a[l * 32 : l * 32 + 32] = jnp.where(low_zl, w[:, :512], w[:, 512:])
        out_b[l * 32 : l * 32 + 32] = jnp.where(low_zl, w[:, 512:], w[:, :512])
    down[...] = inner_columns(w_down[...].astype(F32)).astype(BF)


def prepare_rest(*refs):
    sources, refs = refs[:4], refs[4:]
    rest, (down, cot), (held, sems) = refs[0:4], refs[4:6], (refs[6:10], refs[10])
    fetch((sources[0].at[1], sources[1], sources[2].at[1], sources[3].at[0]), held, sems)
    w_qkv, w_up, w_down, cot_in = held
    for i, (dc, dl) in enumerate(RANKS):
        core, zl = bit("core", dc), bit("zl", dl)
        for src, dst in qkv_blocks(core, zl):
            rest[i][:, 1024 + dst * 128 : 1152 + dst * 128] = w_qkv[:, at(src, 128)]
        for src, dst in up_blocks(core, zl):
            rest[i][:, dst * 128 : dst * 128 + 128] = w_up[0, :, at(src, 128)]
            rest[i][:, 1792 + dst * 128 : 1920 + dst * 128] = w_up[1, :, at(src, 128)]
    down[...] = inner_columns(w_down[...].astype(F32)).astype(BF)
    cot[...] = inner_columns(cot_in[...].astype(F32)).astype(BF)


def put_out(piece, layer, out_a, out_b):
    for ref, flip in ((out_a, 0), (out_b, 1)):
        zl_from = bit("y", flip)
        for h in range(2):
            piece[pl.ds(pl.multiple_of(h * 64 + zl_from * 32, 32), 32), 768:1024] = ref[
                layer * 32 : layer * 32 + 32, h * 256 : h * 256 + 256
            ]


def pack_first(m0, m1, m2, m3, out_a, out_b, piece):
    lane = lax.broadcasted_iota(jnp.int32, (16, 128), 1)
    kind = lax.broadcasted_iota(jnp.int32, (16, 128), 0) % 8
    one = jnp.zeros((16, 128), F32)
    two = jnp.zeros((16, 128), F32)
    for i, m in enumerate((m0, m1, m2, m3)):
        core, zl = bit("core", RANKS[i][0]), bit("zl", RANKS[i][1])
        piece[at(core * 2 + zl, 32), 0:768] = m[0:32, :]
        s = m[32:48, 0:128].astype(F32)
        mine = (kind < 6) & (lane // 32 == core * 2 + zl)
        pair = (kind == 6) & (lane // 64 == zl)
        if i == 0:
            mine = mine | (kind == 7)
        one = one + jnp.where(mine | (pair & (core == 0)), s, 0.0)
        two = two + jnp.where(pair & (core == 1), s, 0.0)
    put_out(piece, 0, out_a, out_b)
    piece[128:144, 0:128] = one.astype(BF)
    piece[128:144, 128:256] = two.astype(BF)
    piece[128:144, 256:1024] = jnp.zeros((16, 768), BF)


def pack_rest(m0, m1, m2, m3, out_a, out_b, down_0, mlp_0, up_0, deep, pair):
    for i, m in enumerate((m0, m1, m2, m3)):
        spot = at(bit("core", RANKS[i][0]) * 2 + bit("zl", RANKS[i][1]), 32)
        up_0[spot, :] = m[:, 0:1024]
        deep[spot, 0:768] = m[:, 1024:1792]
        deep[at(4 + bit("core", RANKS[i][0]) * 2 + bit("zl", RANKS[i][1]), 32), :] = m[:, 1792:2816]
    put_out(deep, 1, out_a, out_b)
    mlp_0[0:128, :] = up_0[...]
    mlp_0[128:256, :] = down_0[...]
    pair[0:256, :] = mlp_0[...]
    pair[256:384, :] = deep[0:128, :]


def both_ways(value):
    return lax.ppermute(value, ("y", "x"), [(0, 3), (3, 0), (1, 2), (2, 1)])


def first_hops(piece):
    return swap(piece, "zh"), swap(piece, "x"), swap(piece, "y")


def load_rows(pieces, scratch, row, columns):
    for r, block in slot_blocks():
        scratch[at(block, 128), :] = pieces[r][row : row + 128, 0:columns]


def load_out(pieces, scratch):
    for r, y, x, zh in slot_places():
        for h in range(2):
            scratch[at(x * 2 + zh, 64), at(y * 2 + h, 256)] = pieces[r][
                h * 64 : h * 64 + 64, 768:1024
            ]


def normal(x):
    centred = x - jnp.mean(x, axis=-1, keepdims=True)
    inv = lax.rsqrt(jnp.mean(centred * centred, axis=-1, keepdims=True) + EPSILON)
    return centred * inv, inv


def load_stream(blocks, scratch):
    for i, (dc, dl) in enumerate(RANKS):
        spot = at(bit("core", dc) * 2 + bit("zl", dl), 128)
        scratch[spot, :] = inner_columns(blocks[i][0].astype(F32)).astype(scratch.dtype)


def load_blocks(blocks, scratch):
    for i, (dc, dl) in enumerate(RANKS):
        scratch[at(bit("core", dc) * 2 + bit("zl", dl), 128), :] = blocks[i][...]


def load_cores(mine, other, scratch):
    scratch[at(bit("core", 0), 256), :] = Rows(mine)[...]
    scratch[at(bit("core", 1), 256), :] = Rows(other)[...]


def split_product(left, right, keep, send):
    mine, other = at(bit("core", 0), 256), at(bit("core", 1), 256)
    Rows(send)[...] = right(left[other, :]).astype(BF)
    keep[...] = right(left[mine, :])


def row_positions(order, dim):
    shape_ = (512, 1) if dim == 0 else (1, 512)
    row = lax.broadcasted_iota(jnp.int32, shape_, dim)
    start = jnp.zeros(shape_, jnp.int32)
    for c in range(4):
        lead = order[c]
        start = jnp.where(row // 64 == 2 * c, lead, start)
        start = jnp.where(row // 64 == 2 * c + 1, 7 - lead, start)
    return start * 64 + row % 64


def masked_distance(seg_a, seg_b, order, dist):
    same = lax.axis_index("core") == lax.axis_index("zh")
    seg = jnp.where(same, seg_a[...], seg_b[...])
    ends = [jnp.sum((seg < d).astype(jnp.int32), axis=1, keepdims=True) for d in (1, 2)]

    def doc(pos):
        return (pos >= ends[0]).astype(jnp.int32) + (pos >= ends[1]).astype(jnp.int32)

    rows, cols = row_positions(order, 0), row_positions(order, 1)
    gap = rows - cols
    fine = (gap >= 0) & (doc(rows) == doc(cols))
    dist[...] = jnp.where(fine, gap.astype(F32), 1e32)


def slope_of(pair, half):
    core, zl = lax.axis_index("core"), lax.axis_index("zl")
    value = jnp.float32(0.0)
    for c in range(2):
        for z in range(2):
            head = 8 * z + 4 * pair + 2 * c + half
            value = jnp.where((core == c) & (zl == z), jnp.float32(2.0 ** (-8.0 * (head + 1) / HEADS)), value)
    return value


def attend(qkv, dist, probs, o):
    low = lax.broadcasted_iota(jnp.int32, (128, 128), 1) < 64
    for pair in range(2):
        k = qkv[:, 256 + pair * 128 : 384 + pair * 128]
        v = qkv[:, 512 + pair * 128 : 640 + pair * 128]

        def rows(step, carry):
            spot = at(step, 128)
            q = qkv[spot, pair * 128 : pair * 128 + 128]
            d = dist[spot, :]
            found = []
            for half in range(2):
                qh = jnp.where(low == (half == 0), q, jnp.zeros_like(q))
                s = dot_t(qh, k) * 0.125 - slope_of(pair, half) * d
                p = jnp.exp(s - jnp.max(s, axis=1, keepdims=True))
                p = (p / jnp.sum(p, axis=1, keepdims=True)).astype(BF)
                probs[pair * 2 + half, spot, :] = p
                found.append(dot(p, v))
            o[spot, pair * 128 : pair * 128 + 128] = jnp.where(low, *found).astype(BF)
            return carry

        lax.fori_loop(0, 4, rows, 0)


def attention_part(h1, vec, layer, pieces, seg_a, seg_b, order, outs, scratch):
    qkv, probs, o, keep, *send = outs
    wq, wo, dist = scratch
    load_rows(pieces, wq, 0, 768)
    load_out(pieces, wo)
    masked_distance(seg_a, seg_b, order, dist)
    qkv[...] = (dot(h1[...], wq[...]) + vec[layer * 8 + 6 : layer * 8 + 7, 0:768]).astype(BF)
    attend(qkv, dist, probs, o)
    split_product(o, lambda rows: dot(rows, wo[...]), keep, send)


def first_attention(t0, t1, t2, t3, *refs):
    pieces, (seg_a, seg_b, order), refs = att_0_slots(refs[:7]), refs[7:10], refs[10:]
    vec, h1, outs, scratch = refs[0], refs[1], refs[2:10], refs[10:]
    q_one, q_two, scratch = scratch[0], scratch[1], scratch[2:]
    for r, block in slot_blocks():
        vec[:, at(block, 128)] = pieces[r][128:144, 0:128].astype(F32)
        q_two[:, at(block, 128)] = pieces[r][128:144, 128:256].astype(F32)
    q_one[...] = vec[...]
    core, zl = lax.axis_index("core"), lax.axis_index("zl")
    for l in range(2):
        row = slice(l * 8 + 6, l * 8 + 7)
        for base, y in ((0, 0), (512, 1)):
            block = (y * 2 + zl) * 2 + core
            vec[row, base : base + 128] = q_one[row, at(block, 128)]
            vec[row, base + 128 : base + 256] = q_two[row, at(block, 128)]
        vec[row, 256:512] = jnp.zeros((1, 256), F32)
    load_stream((t0, t1, t2, t3), h1)
    for i in range(4):
        spot = slice(i * 128, i * 128 + 128)
        z, _ = normal(h1[spot, :].astype(F32))
        h1[spot, :] = (z * vec[0:1, :] + vec[1:2, :]).astype(BF)
    attention_part(h1, vec, 0, pieces, seg_a, seg_b, order, outs, scratch)


def next_attention(*refs):
    mine, other, refs = refs[:4], refs[4:8], refs[8:]
    pieces, (vec, seg_a, seg_b, order), refs = att_1_slots(refs[:7]), refs[7:11], refs[11:]
    h1, outs, scratch = refs[0], refs[1:9], refs[9:]
    load_cores(mine, other, h1)
    attention_part(h1, vec, 1, pieces, seg_a, seg_b, order, outs, scratch)


def add_parts(keep, *refs):
    came, out = Rows(refs[:4]), refs[4]
    out[...] = (keep[...] + came[...].astype(F32)).astype(BF)


def norm_stage(bias_row, gain_row):
    def kernel(x, part, came, vec, x_out, *h):
        h = Rows(h)
        for i in range(2):
            spot = slice(i * 128, i * 128 + 128)
            v = x[spot, :] + part[spot, :].astype(F32) + came[spot, :].astype(F32)
            v = v + vec[bias_row : bias_row + 1, :]
            x_out[spot, :] = v
            z, _ = normal(v)
            h[spot, :] = (z * vec[gain_row : gain_row + 1] + vec[gain_row + 1 : gain_row + 2]).astype(BF)

    return kernel


def first_norm_stage(t0, t2, part, came, vec, *refs):
    x_out, h, x0 = refs[0], refs[1:5], refs[5]
    x0[at(bit("zl", 0), 128), :] = inner_columns(t0[0].astype(F32))
    x0[at(bit("zl", 1), 128), :] = inner_columns(t2[0].astype(F32))
    norm_stage(2, 3)(x0, part, came, vec, x_out, *h)


def mlp_weights(refs, layer):
    count = 11 if layer else 8
    return (mlp_1_slots if layer else mlp_0_slots)(refs[:count]), refs[count:]


def mlp_stage(layer):
    def kernel(*refs):
        mine, other, refs = refs[:4], refs[4:8], refs[8:]
        pieces, refs = mlp_weights(refs, layer)
        vec, h2, u, a, keep, *send, w = refs
        load_cores(mine, other, h2)
        load_rows(pieces, w, 0, 1024)
        for i in range(4):
            spot = slice(i * 128, i * 128 + 128)
            z = dot(h2[spot, :], w[...]) + vec[layer * 8 + 7 : layer * 8 + 8, :]
            u[spot, :] = z
            a[spot, :] = gelu_tanh(z).astype(BF)
        load_rows(pieces, w, 128, 1024)
        split_product(a, lambda rows: dot(rows, w[...]), keep, send)

    return with_scratch(kernel, pltpu.VMEM((1024, 1024), BF))


def finish_rows(x, part, came, vec, out):
    v = x[at(bit("zl", 0), 128), :] + part[...].astype(F32) + came[...].astype(F32) + vec[13:14, :]
    out[0] = inner_columns(v).astype(BF)


def add_split(keep, *refs):
    came, mine, other = Rows(refs[:4]), refs[4], refs[5]
    for to, flip in ((mine, 0), (other, 1)):
        which = bit("zl", flip)
        to[...] = (keep[at(which, 128), :] + came.block(which).astype(F32)).astype(BF)


def gelu_slope(u):
    c = 0.7978845608028654
    t = jnp.tanh(c * (u + 0.044715 * u * u * u))
    return 0.5 * (1.0 + t) + 0.5 * u * (1.0 - t * t) * (c * (1.0 + 3 * 0.044715 * u * u))


def mlp_back(layer):
    def kernel(*refs):
        if layer == 1:
            blocks, u, refs = refs[:4], refs[4], refs[5:]
        else:
            blocks, u, refs = refs[:8], refs[8], refs[9:]
        pieces, (gy2, gu, keep, *send, w) = mlp_weights(refs, layer)
        load_blocks(blocks, gy2) if layer == 1 else load_cores(blocks[:4], blocks[4:], gy2)
        load_rows(pieces, w, 128, 1024)
        for i in range(4):
            spot = slice(i * 128, i * 128 + 128)
            gu[spot, :] = (dot_t(gy2[spot, :], w[...]) * gelu_slope(u[spot, :])).astype(BF)
        load_rows(pieces, w, 0, 1024)
        split_product(gu, lambda rows: dot_t(rows, w[...]), keep, send)

    return with_scratch(kernel, pltpu.VMEM((1024, 1024), BF))


def turned_dot(left, right):
    return lax.dot_general(left, right, (((0,), (0,)), ((), ())), preferred_element_type=F32)


def slot_spots(rows, to_y, to_x, near_0, near_1, far_0, far_1):
    return (
        near_0, far_0, near_1, View(to_x, 0), View(to_y, 0), far_1, View(to_y, rows), View(to_x, rows),
    )


def mlp_grads(h2, a, gy2, gu, *outs):
    spots = slot_spots(256, *outs)
    for r, block in slot_blocks():
        spots[r][0:128, :] = turned_dot(h2[:, at(block, 128)], gu[...]).astype(BF)
        spots[r][128:256, :] = turned_dot(a[:, at(block, 128)], gy2[...]).astype(BF)


def second_sums(rows, near_1, near, far_1, far, to_x, to_y):
    to_x[0:rows, :] = (near_1[...].astype(F32) + near[0:rows, :].astype(F32)).astype(BF)
    to_y[0:rows, :] = (far_1[...].astype(F32) + far[0:rows, :].astype(F32)).astype(BF)


def third_sum(rows, far_0, far, far_2, out):
    total = far_0[...].astype(F32) + far[0:rows, :].astype(F32) + far_2[0:rows, :].astype(F32)
    out[...] = total.astype(BF)


def norm_back(gx, part, came, x, gain, gm, gy, sums):
    totals = [jnp.zeros((1, x.shape[1]), F32) for _ in range(4)]
    for i in range(part.shape[0] // 128):
        spot = slice(i * 128, i * 128 + 128)
        dh = part[spot, :].astype(F32) + came[spot, :].astype(F32)
        z, inv = normal(x[spot, :])
        dz = dh * gain
        mean_a = jnp.mean(dz, axis=-1, keepdims=True)
        mean_b = jnp.mean(dz * z, axis=-1, keepdims=True)
        up = gx[spot, :]
        g = up + inv * (dz - mean_a - z * mean_b)
        gm[spot, :] = g
        rounded = g.astype(BF)
        gy[spot, :] = rounded
        new = (dh * z, dh, rounded.astype(F32), up.astype(BF).astype(F32))
        totals = [t + jnp.sum(v, axis=0, keepdims=True) for t, v in zip(totals, new)]
    sums[...] = jnp.concatenate(totals + [jnp.zeros((4, x.shape[1]), F32)], axis=0)


def norm_back_stage(gain_row):
    def kernel(gx, part, came, x, vec, gm, *refs):
        norm_back(gx, part, came, x, vec[gain_row : gain_row + 1, :], gm, Rows(refs[:4]), refs[4])

    return kernel


def first_norm_back(c0, c2, part, came, x, vec, gm, *refs):
    gy, sums, gx = Rows(refs[:4]), refs[4], refs[5]
    gx[at(bit("zl", 0), 128), :] = c0[...].astype(F32)
    gx[at(bit("zl", 1), 128), :] = c2[...].astype(F32)
    norm_back(gx, part, came, x, vec[11:12, :], gm, gy, sums)


def last_norm_back(gx, part, came, t0, vec, grad, up, x, gm, gy, sums):
    x[...] = inner_columns(t0[0].astype(F32))
    up[...] = gx[at(bit("zl", 0), 128), :]
    norm_back(up, part, came, x, vec[0:1, :], gm, gy, sums)
    grad[0] = inner_columns(gm[...]).astype(BF)


def attention_back(layer):
    def kernel(*refs):
        mine, other, (qkv, probs), refs = refs[:4], refs[4:8], refs[8:10], refs[10:]
        pieces = (att_1_slots if layer else att_0_slots)(refs[:7])
        attention_back_part(mine, other, qkv, probs, pieces, *refs[7:])

    return kernel


def attention_back_part(mine, other, qkv, probs, pieces, *refs):
    gy1, gqkv, keep, *send, wq, wo, go, gk, gv = refs
    load_cores(mine, other, gy1)
    load_rows(pieces, wq, 0, 768)
    load_out(pieces, wo)
    go[...] = dot_t(gy1[...], wo[...]).astype(BF)
    low = lax.broadcasted_iota(jnp.int32, (128, 128), 1) < 64
    low_all = lax.broadcasted_iota(jnp.int32, (512, 128), 1) < 64
    for pair in range(2):
        k = qkv[:, 256 + pair * 128 : 384 + pair * 128]
        v = qkv[:, 512 + pair * 128 : 640 + pair * 128]
        gk[...] = jnp.zeros_like(gk)
        gv[...] = jnp.zeros_like(gv)

        def rows(step, carry):
            spot = at(step, 128)
            q = qkv[spot, pair * 128 : pair * 128 + 128]
            g = go[spot, pair * 128 : pair * 128 + 128]
            gq = []
            for half in range(2):
                lanes = low == (half == 0)
                gh = jnp.where(lanes, g, jnp.zeros_like(g))
                qh = jnp.where(lanes, q, jnp.zeros_like(q))
                p = probs[pair * 2 + half, spot, :]
                pf = p.astype(F32)
                dp = dot_t(gh, v)
                ds = (pf * (dp - jnp.sum(dp * pf, axis=1, keepdims=True))).astype(BF)
                gq.append(dot(ds, k))
                gk[...] += turned_dot(ds, qh)
                gv[...] += turned_dot(p, gh)
            gqkv[spot, pair * 128 : pair * 128 + 128] = (0.125 * jnp.where(low, *gq)).astype(BF)
            return carry

        lax.fori_loop(0, 4, rows, 0)
        gqkv[:, 256 + pair * 128 : 384 + pair * 128] = (0.125 * gk[...]).astype(BF)
        gqkv[:, 512 + pair * 128 : 640 + pair * 128] = gv[...].astype(BF)
    split_product(gqkv, lambda rows: dot_t(rows, wq[...]), keep, send)


def attention_grads(rows, h1, o, gy1, gqkv, outs, d_out):
    spots = slot_spots(rows, *outs)
    d_out[...] = turned_dot(o[...], gy1[...]).astype(BF)
    for (r, block), (_, y, x, zh) in zip(slot_blocks(), slot_places()):
        spots[r][0:128, 0:768] = turned_dot(h1[:, at(block, 128)], gqkv[...]).astype(BF)
        for h in range(2):
            spots[r][h * 64 : h * 64 + 64, 768:1024] = d_out[at(x * 2 + zh, 64), at(y * 2 + h, 256)]
    return spots


def window_1(h2, a, gy2, gu, *outs):
    mlp_grads(h2, a, gy2, gu, *outs)


def window_2(h1, o, gy1, gqkv, near_1, y_1, far_1, x_1, to_y, to_x, *rest):
    attention_grads(128, h1, o, gy1, gqkv, (to_y, to_x) + rest[:4], rest[4])
    second_sums(256, near_1, View(y_1, 256), far_1, View(x_1, 256), View(to_x, 256), View(to_y, 256))


def window_3(h2, a, gy2, gu, near_1, y_2, far_1, x_2, far_0, x_1, to_y, to_x, *rest):
    mlp_grads(h2, a, gy2, gu, to_y, to_x, *rest[:4])
    second_sums(128, near_1, View(y_2, 128), far_1, View(x_2, 128), View(to_x, 512), View(to_y, 512))
    third_sum(256, far_0, x_1, View(y_2, 256), rest[4])


def window_4(near_1, y_3, far_1, x_3, far_0, x_2, to_x, to_y, to_zh):
    second_sums(256, near_1, View(y_3, 256), far_1, View(x_3, 256), to_x, to_y)
    third_sum(128, far_0, x_2, View(y_3, 512), to_zh)


def window_5(*refs):
    grads, (to_y, to_x), rest = refs[:19], refs[19:21], refs[21:]
    last_attention_grads(*grads, (to_y, to_x) + rest[:4], *rest[4:])


def second_only(near_1, y, far_1, x, to_x, to_y):
    second_sums(144, near_1, View(y, 144), far_1, View(x, 144), to_x, to_y)


def third_only(far_0, x, y, to_zh):
    third_sum(256, far_0, x, y, to_zh)


def window_6(far_0, x_4, y_5, to_zh):
    third_sum(144, far_0, x_4, y_5, to_zh)


def last_attention_grads(
    h1, o, gy1, gqkv, g1, e1, e0, gu1, gu0, gq1, keep, s0, s1, s2, s3, t0, t1, t2, t3, outs, d_out, ups, wide
):
    spots = attention_grads(144, h1, o, gy1, gqkv, outs, d_out)
    send = Rows((s0, s1, s2, s3))
    none = jnp.zeros((2, 1024), F32)
    gain = jnp.zeros((1, 1024), F32)
    shift = jnp.zeros((1, 1024), F32)
    for i, block in enumerate((t0, t1, t2, t3)):
        dc, dl = RANKS[i]
        z, _ = normal(inner_columns(block[0].astype(F32)))
        which = bit("zl", dl)
        dh = send.block(which).astype(F32) if dc else keep[at(which, 128), :]
        gain = gain + jnp.sum(dh * z, axis=0, keepdims=True)
        shift = shift + jnp.sum(dh, axis=0, keepdims=True)
    parts = [g1[0:2, :], e1[2:3, :], e1[0:2, :], e1[3:4, :], none, gain, shift]
    wide[...] = jnp.concatenate(parts + [e0[2:3, :], e0[0:2, :], e0[3:4, :], none], axis=0)
    sums = [jnp.sum(v[...].astype(F32), axis=0, keepdims=True) for v in (gu1, gu0)]
    ups[...] = jnp.concatenate(sums + [jnp.zeros((14, 1024), F32)], axis=0)
    q = [jnp.sum(v[...].astype(F32), axis=0, keepdims=True) for v in (gq1, gqkv)]
    q = jnp.concatenate(q + [jnp.zeros((14, 768), F32)], axis=0)
    core, zl = lax.axis_index("core"), lax.axis_index("zl")
    for r, block in slot_blocks():
        rows = slice(128, 144)
        spots[r][rows, 0:128] = wide[:, at(block, 128)].astype(BF)
        spots[r][rows, 128:256] = ups[:, at(block, 128)].astype(BF)
        mine = jnp.where(block == 4 + zl * 2 + core, q[:, 512:768], jnp.zeros((16, 256), F32))
        mine = jnp.where(block == zl * 2 + core, q[:, 0:256], mine)
        spots[r][rows, 256:512] = mine.astype(BF)
        spots[r][rows, 512:1024] = jnp.zeros((16, 512), BF)


def summed(parts, rows, columns):
    value = parts[0][rows, columns].astype(F32)
    for part in parts[1:]:
        value = value + part[rows, columns].astype(F32)
    return value


def own_out(parts, flip):
    row = bit("y", flip) * 32
    halves = []
    for h in range(2):
        spot = pl.ds(pl.multiple_of(h * 64 + row, 32), 32)
        halves.append(summed(parts, spot, slice(768, 1024)))
    return jnp.concatenate(halves, axis=1)


def rank_rows(i):
    return at(bit("core", RANKS[i][0]) * 2 + bit("zl", RANKS[i][1]), 32)


def unpack_first(y_1, y_2, x_2, x_3, m_near, m_far, a_near, a_far, mine, *refs):
    mlp = (m_near, y_1, View(x_2, 256), m_far)
    att = (a_near, y_2, View(x_3, 512), a_far)
    sends, a, b, down = refs[0:3], refs[3], refs[4], refs[5]
    for i in range(4):
        to = mine if i == 0 else sends[i - 1]
        for parts, start, width in ((att, 0, 768), (mlp, 768, 1024)):
            value = summed(parts, rank_rows(i), slice(0, width))
            to[:, start : start + width] = value.astype(to.dtype)
    a[...] = own_out(att, 0).astype(BF)
    b[...] = own_out(att, 1).astype(BF)
    down[...] = inner_columns(summed(mlp, slice(128, 256), slice(0, 1024)))


def unpack_last(y_3, y_5, x_4, x_6, m_near, m_far, a_near, a_far, a1, b1, down_1, mine, *refs):
    mlp = (m_near, y_3, x_4, m_far)
    att = (a_near, y_5, x_6, a_far)
    sends, (a, b), down = refs[0:3], refs[3:5], refs[5]
    for i in range(4):
        to = mine if i == 0 else sends[i - 1]
        to[0:32, 0:768] = summed(att, rank_rows(i), slice(0, 768)).astype(to.dtype)
        to[0:32, 768:1792] = summed(mlp, rank_rows(i), slice(0, 1024)).astype(to.dtype)
        to[32:48, 0:768] = summed(att, slice(128, 144), slice(0, 768)).astype(to.dtype)
        to[32:48, 768:1792] = jnp.zeros((16, 1024), to.dtype)
    a[0:32, :] = own_out(att, 0).astype(BF)
    b[0:32, :] = own_out(att, 1).astype(BF)
    a[32:64, :] = a1[...]
    b[32:64, :] = b1[...]
    down[0] = inner_columns(summed(mlp, slice(128, 256), slice(0, 1024)))
    down[1] = down_1[...]


def finish(rest, r1, r2, r3, last, l1, l2, l3, a, b, *outs):
    g1, b1, w_qkv, qv, w_out, bo, g2, b2, w_up, up, bd = outs
    for i, (rm, lm) in enumerate(((rest, last), (r1, l1), (r2, l2), (r3, l3))):
        core, zl = bit("core", RANKS[i][0]), bit("zl", RANKS[i][1])
        for src, dst in qkv_blocks(core, zl):
            w_qkv[0, :, at(src, 128)] = lm[0:32, dst * 128 : dst * 128 + 128].astype(F32)
            w_qkv[1, :, at(src, 128)] = rm[:, dst * 128 : dst * 128 + 128].astype(F32)
        for src, dst in up_blocks(core, zl):
            w_up[0, :, at(src, 128)] = lm[0:32, 768 + dst * 128 : 896 + dst * 128].astype(F32)
            w_up[1, :, at(src, 128)] = rm[:, 768 + dst * 128 : 896 + dst * 128].astype(F32)
    low_zl = lax.axis_index("zl") == 0
    for l in range(2):
        va, vb = a[l * 32 : l * 32 + 32].astype(F32), b[l * 32 : l * 32 + 32].astype(F32)
        w = jnp.concatenate([jnp.where(low_zl, va, vb), jnp.where(low_zl, vb, va)], axis=1)
        w_out[l] = inner_columns(w)
    spot = lax.axis_index("core") * 2 + lax.axis_index("zl")

    def chunk(value, size):
        found = jnp.zeros((value.shape[0], size), F32)
        for j in range(4):
            found = jnp.where(spot == j, value[:, j * size : j * size + size], found)
        return found

    mine, by_core = last[32:48, 0:128], l1[32:48, 0:128].astype(F32)
    wide = chunk(mine + by_core, 32)
    late = l2[32:48, 0:128].astype(F32) + l3[32:48, 0:128].astype(F32)
    late = chunk(mine + by_core + late, 32)
    for row, ref in ((2, bo), (3, g2), (4, b2), (5, bd)):
        ref[...] = jnp.concatenate([wide[row + 8 : row + 9], wide[row : row + 1]], axis=0)
    g1[...] = jnp.concatenate([late[8:9], wide[0:1]], axis=0)
    b1[...] = jnp.concatenate([late[9:10], wide[1:2]], axis=0)
    up[...] = jnp.concatenate([last[33:34, 128:256], last[32:33, 128:256]], axis=0)
    both = last[32:48, 256:512]
    for m in (l1, l2, l3):
        both = both + m[32:48, 256:512].astype(F32)
    both = chunk(both, 64)
    qv[...] = jnp.concatenate([both[1:2], both[0:1]], axis=0)


def corner(value):
    return lax.ppermute(value, ("core", "zh"), [(0, 0), (1, 2), (2, 1), (3, 3)])


def to_partners(messages):
    one, two, three = messages
    return (
        swap(one, "core"),
        swap(two, "zl"),
        lax.ppermute(three, ("core", "zl"), [(0, 3), (3, 0), (1, 2), (2, 1)]),
    )


def narrow_body(
    tokens, segment_ids, group_order, ln1_gain, ln1_bias, qkv_weight, qv_bias, out_weight, out_bias,
    ln2_gain, ln2_bias, up_weight, up_bias, down_weight, down_bias, cotangent,
):
    small = (ln1_gain, ln1_bias, out_bias, ln2_gain, ln2_bias, down_bias, qv_bias, up_bias)

    def held(*values):
        return [pltpu.VMEM(v, BF) for v in values] + [pltpu.SemaphoreType.DMA((len(values),))]

    row, rowf = shape(256, 1024), shape(256, 1024, dtype=F32)
    quarters = [shape(64, 1024)] * 4

    ready = run(
        with_scratch(
            prepare_first, *held(*[v.shape for v in small], (2, 32, 1024), (32, 3072), (128, 1024))
        ),
        [shape(48, 768)] * 4 + [shape(64, 512)] * 2 + [shape(128, 1024)],
        *small, out_weight, qkv_weight, down_weight, anywhere=True, limit=60, us=3,
    )
    out_b = lax.ppermute(ready[5], ("y", "zl"), [(0, 2), (1, 0), (2, 3), (3, 1)])
    out_a = lax.ppermute(ready[4], ("y", "zl"), [(0, 0), (1, 2), (2, 1), (3, 3)])
    first = (ready[0],) + to_partners(ready[1:4])
    (att_0,) = run(pack_first, [shape(144, 1024)], *first, out_a, out_b)
    far, near_x, near_y = first_hops(att_0)
    block = corner(tokens)
    rest = run(
        with_scratch(
            prepare_rest, *held((32, 3072), (2, 32, 4096), (128, 1024), (128, 1024))
        ),
        [shape(32, 2816)] * 4 + [shape(128, 1024)] * 2,
        qkv_weight, up_weight, down_weight, cotangent, after=(ready[0],), anywhere=True, us=2,
    )
    cot = rest[5]
    mlp_0, up_0, deep, pair = run(
        pack_rest, [row, shape(128, 1024), row, shape(384, 1024)],
        rest[0], *to_partners(gate((att_0,), *rest[1:4])[:3]), out_a, out_b, ready[6],
    )
    down_1 = rest[4]
    def second_hops(kernel, rows_x, rows_y, *ins, after=(), rows=0):
        outs = [shape(n, 1024) for n in (rows_x, rows_y, rows) if n]
        to = run(kernel, outs, *ins, after=after)
        return swap(to[0], "x"), swap(to[1], "y"), both_ways(to[2] if rows else ins[0]), to[0]

    by_x, by_y, both, sent = second_hops(
        att_0_message, 224, 208, far, near_x, near_y, after=(pair, block)
    )
    att_0 = (att_0, far, near_x, near_y, by_x, by_y, both)
    up_0, down_0, _ = gate((sent,), up_0, ready[6])
    far_up, far_down = swap(up_0, "zh"), swap(down_0, "zh")
    by_zl = swap(block, "zl")
    pair, deep, token = gate((by_x, by_y, both, far_up, by_zl), pair, deep)
    pair_x, pair_y = swap(pair, "x"), swap(pair, "y")
    blocks = (block, swap(block, "core"), by_zl, swap(by_zl, "core"))
    segments = (segment_ids, swap(segment_ids, "core"), group_order)

    def cores(values):
        return [swap(v, "core") for v in values]

    def summed_core(keep, *send, after=()):
        (part,) = run(add_parts, [row], keep, *cores(send), after=after)
        return part, swap(part, "zl")

    def split_core(keep, *send, after=()):
        part, other = run(add_split, [shape(128, 1024)] * 2, keep, *cores(send), after=after)
        return part, swap(other, "zl")

    def with_other(values):
        return (*values, *cores(values))

    attention_outs = [
        shape(512, 1024), shape(512, 768), shape(4, 512, 512), shape(512, 256), rowf, *quarters,
    ]
    weights_scratch = [pltpu.VMEM((1024, 768), BF), pltpu.VMEM((256, 1024), BF)]
    dist = pltpu.VMEM((512, 512), F32)
    vec_scratch = [pltpu.VMEM((16, 1024), F32)] * 2
    mlp_outs = [shape(512, 1024), shape(512, 1024, dtype=F32), shape(512, 1024), rowf, *quarters]

    vec, h1_0, qkv_0, probs_0, o_0, keep, *send = run(
        with_scratch(first_attention, *vec_scratch, *weights_scratch, dist),
        [shape(16, 1024, dtype=F32)] + attention_outs, *blocks, *att_0, *segments, after=(token,), us=10,
    )
    far_down, pair_x, pair_y, deep, down_1, *send, _ = gate(
        (keep,), far_down, pair_x, pair_y, deep, down_1, *send
    )
    deep_far = swap(deep, "zh")
    part, came = summed_core(keep, *send)
    by_x, by_y, both, token = second_hops(
        mlp_0_message, 384, 384, far_up, far_down, pair_x, pair_y, after=(part,), rows=256
    )
    mlp_0 = (mlp_0, far_up, far_down, pair_x, pair_y, by_x, by_y, both)
    x1_0, *h = run(
        with_scratch(first_norm_stage, pltpu.VMEM((256, 1024), F32)),
        [rowf, *quarters], blocks[0], blocks[2], part, came, vec, after=(token,), us=1.5,
    )
    h2_0, u_0, a_0, keep, *send = run(
        mlp_stage(0), mlp_outs, *with_other(h), *mlp_0, vec, after=(deep_far,), us=4
    )
    down_1_far = swap(down_1, "zh")
    one_x, one_y, both, token = second_hops(
        att_1_message, 448, 448, deep_far, pair_x, pair_y, deep, down_1, after=(keep,), rows=128
    )
    att_1 = (deep, deep_far, pair_x, pair_y, one_x, one_y, both)
    part, came = summed_core(keep, *send)
    x2_0, *h = run(norm_stage(5, 8), [rowf, *quarters], x1_0, part, came, vec, after=(token, down_1_far), us=1)
    to_all, to_x, to_y = run(
        mlp_1_message, [row, shape(128, 1024), shape(128, 1024)], deep_far, down_1_far, one_x, one_y,
        after=(both,),
    )
    by_x, by_y = swap(to_all, "x"), swap(to_all, "y")
    h1_1, qkv_1, probs_1, o_1, keep, *send = run(
        with_scratch(next_attention, *weights_scratch, dist),
        attention_outs, *with_other(h), *att_1, vec, *segments, after=(to_all,), us=9,
    )
    by_x, by_y, to_x, to_y, *send, _ = gate((keep,), by_x, by_y, to_x, to_y, *send)
    mlp_1 = (
        deep, down_1, deep_far, down_1_far, one_x, one_y, by_x, by_y,
        swap(to_x, "x"), swap(to_y, "y"), both_ways(to_all),
    )
    cot, _ = gate((keep,), cot)
    cot = corner(cot)
    part, came = summed_core(keep, *send)
    x1_1, *h = run(norm_stage(10, 11), [rowf, *quarters], x2_0, part, came, vec, after=(token,), us=1)
    by_zl = swap(cot, "zl")
    cots = (cot, swap(cot, "core"), by_zl, swap(by_zl, "core"))
    h2_1, u_1, a_1, keep, *send = run(mlp_stage(1), mlp_outs, *with_other(h), *mlp_1, vec, us=4)

    mlp_back_outs = [shape(512, 1024), shape(512, 1024), rowf, *quarters]
    norm_outs = [rowf, *quarters, shape(8, 1024, dtype=F32)]
    attention_back_outs = [shape(512, 1024), shape(512, 768), rowf, *quarters]
    attention_back_scratch = weights_scratch + [
        pltpu.VMEM((512, 256), BF), pltpu.VMEM((512, 128), F32), pltpu.VMEM((512, 128), F32),
    ]

    def grad_outs(sent, rows):
        return [shape(sent, 1024)] * 2 + [shape(rows, 1024)] * 4

    out_scratch = pltpu.VMEM((256, 1024), BF)

    keep_last, send_last = keep, send
    part_last, came_last = split_core(keep_last, *send_last)
    gy2, gu_1, keep, *send = run(mlp_back(1), mlp_back_outs, *cots, u_1, *mlp_1, after=(part_last,), us=6)
    part, came = summed_core(keep, *send, after=(came_last,))
    to_y, to_x, m1_near_0, m1_near_1, m1_far_0, m1_far_1 = run(
        window_1, grad_outs(512, 256), h2_1, a_1, gy2, gu_1, after=(part,), us=4
    )
    y_1, x_1 = swap(to_y, "y"), swap(to_x, "x")
    gm, *gy, e1 = run(
        with_scratch(first_norm_back, pltpu.VMEM((256, 1024), F32)),
        norm_outs, cots[0], cots[2], part, came, x1_1, vec, after=(m1_far_1,), us=1.5,
    )
    gy1, gqkv_1, keep, *send = run(
        with_scratch(attention_back(1), *attention_back_scratch),
        attention_back_outs, *with_other(gy), qkv_1, probs_1, *att_1, us=9,
    )
    part, came = summed_core(keep, *send)
    (final,) = run(finish_rows, [shape(1, 128, 1024)], x1_1, part_last, came_last, vec)
    output = corner(final)
    to_y, to_x, a1_near_0, a1_near_1, a1_far_0, a1_far_1 = run(
        with_scratch(window_2, out_scratch), grad_outs(512, 128), h1_1, o_1, gy1, gqkv_1,
        m1_near_1, y_1, m1_far_1, x_1, after=(part, output), us=3,
    )
    y_2, x_2 = swap(to_y, "y"), swap(to_x, "x")
    gx, *gy, g1 = run(
        norm_back_stage(8), norm_outs, gm, part, came, x2_0, vec, after=(a1_far_1,), us=1.5
    )
    gy2, gu_0, keep, *send = run(
        mlp_back(0), mlp_back_outs, *with_other(gy), u_0, *mlp_0, us=6
    )
    part, came = summed_core(keep, *send)
    to_y, to_x, m0_near_0, m0_near_1, m0_far_0, m0_far_1, to_zh = run(
        window_3, grad_outs(640, 256) + [row], h2_0, a_0, gy2, gu_0,
        a1_near_1, y_2, a1_far_1, x_2, m1_far_0, x_1, after=(part,), us=4,
    )
    y_3, x_3, m1_far_3 = swap(to_y, "y"), swap(to_x, "x"), swap(to_zh, "zh")
    gm, *gy, e0 = run(
        norm_back_stage(3), norm_outs, gx, part, came, x1_0, vec, after=(m0_far_1,), us=1.5
    )
    gy1, gqkv_0, keep, *send = run(
        with_scratch(attention_back(0), *attention_back_scratch),
        attention_back_outs, *with_other(gy), qkv_0, probs_0, *att_0, us=9,
    )
    to_x, to_y, to_zh = run(
        window_4, [row, row, shape(128, 1024)], m0_near_1, y_3, m0_far_1, x_3, a1_far_0, x_2, after=(keep,)
    )
    x_4, y_4, a1_far_3 = swap(to_x, "x"), swap(to_y, "y"), swap(to_zh, "zh")
    part, came = split_core(keep, *send, after=(to_zh, m1_far_3))
    to_y, to_x, a0_near_0, a0_near_1, a0_far_0, a0_far_1 = run(
        with_scratch(window_5, out_scratch, *vec_scratch), grad_outs(288, 144),
        h1_0, o_0, gy1, gqkv_0, g1, e1, e0, gu_1, gu_0, gqkv_1, keep, *send, *blocks,
        after=(part, x_4, y_4), us=3,
    )
    y_5, x_5 = swap(to_y, "y"), swap(to_x, "x")
    (to_zh,) = run(third_only, [row], m0_far_0, x_3, y_4, after=(a0_far_1,))
    m0_far_3 = swap(to_zh, "zh")
    (grad,) = run(
        with_scratch(
            last_norm_back, *[pltpu.VMEM((128, 1024), F32)] * 3, pltpu.VMEM((128, 1024), BF),
            pltpu.VMEM((8, 1024), F32),
        ),
        [shape(1, 128, 1024)], gm, part, came, blocks[0], vec, after=(to_zh,), us=1.5,
    )
    tokens_grad = corner(grad).astype(F32)
    to_x, to_y = run(second_only, [shape(144, 1024)] * 2, a0_near_1, y_5, a0_far_1, x_5, after=(grad,))
    x_6, y_6 = swap(to_x, "x"), swap(to_y, "y")
    rest = run(
        unpack_first,
        [shape(32, 1792, dtype=F32)] + [shape(32, 1792)] * 3 + [shape(32, 512)] * 2
        + [shape(128, 1024, dtype=F32)],
        y_1, y_2, x_2, x_3, m1_near_0, m1_far_3, a1_near_0, a1_far_3, us=2,
    )
    rest_came = to_partners(rest[1:4])
    (to_zh,) = run(window_6, [shape(144, 1024)], a0_far_0, x_5, y_6, after=rest_came)
    a0_far_3 = swap(to_zh, "zh")
    last = run(
        unpack_last,
        [shape(48, 1792, dtype=F32)] + [shape(48, 1792)] * 3 + [shape(64, 512)] * 2
        + [shape(2, 128, 1024, dtype=F32)],
        y_3, y_5, x_4, x_6, m0_near_0, m0_far_3, a0_near_0, a0_far_3, rest[4], rest[5], rest[6],
        after=rest_came,
    )
    back_a = lax.ppermute(last[4], ("y", "zl"), [(0, 0), (1, 2), (2, 1), (3, 3)])
    back_b = lax.ppermute(last[5], ("y", "zl"), [(0, 1), (1, 3), (2, 0), (3, 2)])
    sizes = (
        (2, 32), (2, 32), (2, 32, 3072), (2, 64), (2, 32, 1024), (2, 32), (2, 32), (2, 32),
        (2, 32, 4096), (2, 128), (2, 32),
    )
    g = run(
        finish, [shape(*s, dtype=F32) for s in sizes],
        rest[0], *rest_came, last[0], *to_partners(last[1:4]), back_a, back_b, us=2,
    )
    return (output, tokens_grad) + tuple(g[:10]) + (last[6], g[10])


def solution(mesh):
    fsdp, ctx = mesh.shape["fsdp"], mesh.shape["ctx"]
    fine = Mesh(mesh.devices.reshape(fsdp // 4, 2, 2, 2, ctx // 2), AXES)
    body = narrow_body if fine.devices.shape == (2, 2, 2, 2, 2) else wide_body
    stream, place = ("y", "x", "core"), ("zh", "zl")
    rows = P(stream, place, None)
    flat, deep = P(None, AXES), P(None, AXES, None)
    params = (flat, flat, deep, flat, deep, flat, flat, flat, deep, flat, deep, flat)
    in_specs = (rows, P(stream, None), P()) + params + (rows,)
    out_specs = (rows, rows) + params
    return jax.shard_map(body, mesh=fine, in_specs=in_specs, out_specs=out_specs, check_vma=False)
```

```python
import jax
import jax.numpy as jnp
from jax import lax
from jax.experimental import pallas as pl
from jax.experimental.pallas import tpu as pltpu
from jax.sharding import Mesh, PartitionSpec as P

HEADS = 16
EPSILON = 1e-05
BF = jnp.bfloat16
F32 = jnp.float32
AXES = ("y", "x", "core", "zh", "zl")


def here(axis):
    return lax.axis_index(axis)


def swap(value, axis):
    return lax.ppermute(value, axis, [(0, 1), (1, 0)])


def ordered(mine, other, axis):
    first = here(axis) == 0
    return jnp.stack([jnp.where(first, mine, other), jnp.where(first, other, mine)])


def pick(value, axis):
    return lax.dynamic_index_in_dim(value, here(axis), 0, keepdims=False)


def pick_other(value, axis):
    return lax.dynamic_index_in_dim(value, 1 - here(axis), 0, keepdims=False)


def trade(value, axis):
    if lax.axis_size(axis) == 2:
        return ordered(pick(value, axis), swap(pick_other(value, axis), axis), axis)
    return lax.all_to_all(value, axis, 0, 0, tiled=True)


def collect(value, axis):
    if lax.axis_size(axis) == 2:
        return ordered(value, swap(value, axis), axis)
    return lax.all_gather(value, axis, axis=0, tiled=False)


def reduce_to(value, axis):
    if lax.axis_size(axis) == 2:
        return pick(value, axis) + swap(pick_other(value, axis), axis)
    return lax.psum_scatter(value, axis, scatter_dimension=0, tiled=False)


def flipped(value, axis, dim):
    return jnp.where(here(axis) == 0, value, jnp.flip(value, dim))


def gather_shards(shard):
    if lax.axis_size("y") != 2:
        return lax.all_gather(shard, ("y", "x", "zh"), axis=0, tiled=False)
    far = swap(shard, "zh")
    near_x = swap(shard, "x")
    far_y = swap(far, "y")
    near_y = swap(shard, "y")
    near_xy = swap(near_x, "y")
    far_x = swap(far, "x")
    far_yx = swap(far_y, "x")
    rel = jnp.stack([shard, far, near_x, far_x, near_y, far_y, near_xy, far_yx])
    rel = rel.reshape((2, 2, 2) + shard.shape)
    rel = flipped(flipped(flipped(rel, "y", 0), "x", 1), "zh", 2)
    return rel.reshape((8,) + shard.shape)


def scatter_shards(grads):
    shape = grads.shape[1:]
    if lax.axis_size("y") != 2:
        return lax.psum_scatter(
            grads, ("y", "x", "zh"), scatter_dimension=0, tiled=False
        )
    rel = grads.reshape((2, 2, 2) + shape)
    rel = flipped(flipped(flipped(rel, "y", 0), "x", 1), "zh", 2)
    near, far = rel[:, :, 0], rel[:, :, 1]
    far = far[:, 0] + swap(far[:, 1].astype(BF), "x").astype(F32)
    near = near[0] + swap(near[1].astype(BF), "y").astype(F32)
    far = far[0] + swap(far[1].astype(BF), "y").astype(F32)
    near = near[0] + swap(near[1].astype(BF), "x").astype(F32)
    return near + swap(far.astype(BF), "zh").astype(F32)


def corner_turn(value):
    return lax.ppermute(value, ("core", "zh"), [(0, 0), (1, 2), (2, 1), (3, 3)])


def norm_rows(values, gain, shift):
    row_mean = jnp.mean(values, axis=-1, keepdims=True)
    centred = values - row_mean
    row_var = jnp.mean(centred * centred, axis=-1, keepdims=True)
    return centred * lax.rsqrt(row_var + EPSILON) * gain + shift


def gelu_tanh(values):
    return jax.nn.gelu(values, approximate=True)


def dot(left, right):
    return jnp.dot(left, right, preferred_element_type=F32)


def dot_t(left, matrix):
    return lax.dot_general(
        left, matrix, (((1,), (1,)), ((), ())), preferred_element_type=F32
    )


def outer_sum(left, right):
    return jnp.einsum("td,te->de", left, right, preferred_element_type=F32)


def wide_body(
    tokens,
    segment_ids,
    group_order,
    ln1_gain,
    ln1_bias,
    qkv_weight,
    qv_bias,
    out_weight,
    out_bias,
    ln2_gain,
    ln2_bias,
    up_weight,
    up_bias,
    down_weight,
    down_bias,
    cotangent,
):
    ny, nx, nc, nzh, nzl = (lax.axis_size(a) for a in AXES)
    chips = ny * nx
    span = chips // nzl
    layers, width = ln1_gain.shape[0], tokens.shape[2]
    hidden = up_weight.shape[2]
    group = tokens.shape[1]
    ctx_count = nzh * nzl
    rank_width = width // (nc * nzl)
    rank_hidden = hidden // (nc * nzl)
    head_size = width // HEADS
    rank_heads = rank_width // head_size
    quarter = width // (chips * nc)
    unit = width // (chips * nc * nzh)
    core_rows = nzl * group
    rows = nc * core_rows
    scale = head_size ** (-0.5)

    def inner(value):
        shape = value.shape
        value = value.reshape(shape[:-1] + (chips, 2, 2, unit))
        return jnp.swapaxes(value, -3, -2).reshape(shape)

    small = (ln1_gain, ln1_bias, out_bias, ln2_gain, ln2_bias, down_bias)
    small_all = small + (qv_bias, up_bias)
    packed = jnp.concatenate([v.reshape(-1) for v in small_all])
    for axis in reversed(AXES):
        packed = collect(packed, axis)
    vectors = []
    at = 0
    for v in small_all:
        size = v.shape[0] * v.shape[1]
        part = packed[..., at : at + size].reshape((ny, nx, nc, nzh, nzl) + v.shape)
        part = jnp.moveaxis(part, 5, 0)
        vectors.append(part.reshape(layers, -1).astype(F32))
        at += size
    vec = [inner(v) for v in vectors[:6]]
    full_qv, full_up = vectors[6], vectors[7]

    def rank_columns(value):
        shape = value.shape[:-1]
        value = value.reshape(shape + (nzl, span, nc, quarter))
        value = lax.dynamic_index_in_dim(value, here("zl"), len(shape), keepdims=False)
        value = lax.dynamic_index_in_dim(value, here("core"), len(shape) + 1, keepdims=False)
        return value.reshape(shape + (rank_width,))

    q_bias = rank_columns(full_qv[:, :width])
    v_bias = rank_columns(full_qv[:, width:])
    qkv_bias = jnp.concatenate([q_bias, jnp.zeros_like(q_bias), v_bias], axis=1)
    up_b = full_up.reshape(layers, chips, nc, nzh, nzl, -1)
    up_b = lax.dynamic_index_in_dim(up_b, here("zl"), 4, keepdims=False)
    up_b = lax.dynamic_index_in_dim(up_b, here("core"), 2, keepdims=False)
    up_b = up_b.reshape(layers, rank_hidden)

    def to_ranks(value):
        value = trade(value, "core")
        return jnp.swapaxes(trade(jnp.swapaxes(value, 0, 1), "zl"), 0, 1)

    def fetch(layer):
        w = qkv_weight[layer]
        n = w.shape[0]
        w = w.reshape(n, 3, nzl, span, nc, quarter)
        w = jnp.transpose(w, (4, 2, 0, 1, 3, 5)).reshape(nc, nzl, n, 3 * rank_width)
        w_qkv = gather_shards(to_ranks(w).reshape(-1, 3 * rank_width))
        w = gather_shards(inner(out_weight[layer]))
        w = trade(w.reshape(nzl, span, nzh, n, width), "zl")
        w_out = jnp.transpose(w, (1, 2, 0, 3, 4)).reshape(rank_width, width)
        w = up_weight[layer].reshape(n, chips, nc, nzh, nzl, -1)
        w = jnp.transpose(w, (2, 4, 0, 1, 3, 5)).reshape(nc, nzl, n, rank_hidden)
        w_up = gather_shards(to_ranks(w).reshape(-1, rank_hidden))
        w_down = gather_shards(inner(down_weight[layer]))
        return (
            w_qkv.reshape(width, 3 * rank_width),
            w_out,
            w_up.reshape(width, rank_hidden),
            w_down.reshape(rank_hidden, width),
        )

    def from_ranks(value):
        value = jnp.swapaxes(trade(jnp.swapaxes(value, 0, 1), "zl"), 0, 1)
        return trade(value, "core")

    def send(grads):
        g_qkv, g_out, g_up, g_down = grads
        n = width // (chips * 2 * ctx_count)
        g = scatter_shards(g_qkv.reshape(chips * nzh, -1, 3 * rank_width))
        g = from_ranks(g.astype(BF).reshape(nc, nzl, n, 3 * rank_width)).astype(F32)
        g = g.reshape(nc, nzl, n, 3, span, quarter)
        d_qkv = jnp.transpose(g, (2, 3, 1, 4, 0, 5)).reshape(n, 3 * width)
        g = g_out.astype(BF).reshape(span, nzh, nzl, n, width)
        g = trade(jnp.transpose(g, (2, 0, 1, 3, 4)), "zl").astype(F32)
        d_out = inner(scatter_shards(g.reshape(chips * nzh, n, width)))
        g = scatter_shards(g_up.reshape(chips * nzh, -1, rank_hidden))
        g = from_ranks(g.astype(BF).reshape(nc, nzl, n, rank_hidden)).astype(F32)
        g = g.reshape(nc, nzl, n, chips, nzh, -1)
        d_up = jnp.transpose(g, (2, 3, 0, 4, 1, 5)).reshape(n, hidden)
        d_down = inner(scatter_shards(g_down.reshape(chips * nzh, -1, width)))
        return d_qkv, d_out, d_up, d_down

    def own_columns(value, mine):
        value = inner(value).reshape(ny, nx, nc, nzh, nzl, -1)
        keep = jnp.arange(nzl)[:, None] == here("zl")
        return jnp.where(keep, value, 0.0)

    def send_small(sums):
        g1, b1, gqv, bo, g2, b2, bu, bd = sums
        parts = [own_columns(v, None) for v in (g1, b1, bo, g2, b2, bd)]

        def placed(value):
            value = value.reshape(1, span, 1, quarter)
            keep = (jnp.arange(nzl)[:, None, None, None] == here("zl")) & (
                jnp.arange(nc)[None, None, :, None] == here("core")
            )
            return jnp.where(keep, value, 0.0).reshape(width)

        qv = jnp.concatenate([placed(gqv[0]), placed(gqv[1])])
        parts.append(qv.reshape(ny, nx, nc, nzh, nzl, -1))
        up = bu.reshape(ny, nx, 1, nzh, 1, -1)
        keep = (jnp.arange(nzl)[:, None] == here("zl")) & (
            jnp.arange(nc)[:, None, None, None] == here("core")
        )
        parts.append(jnp.where(keep, up, 0.0))
        value = jnp.concatenate(parts, axis=-1)
        for axis in AXES:
            value = reduce_to(value, axis)
        sizes = [p.shape[-1] for p in parts]
        cut, at = [], 0
        for s in sizes:
            cut.append(value[at : at + s])
            at += s
        g1, b1, bo, g2, b2, bd, qv, up = cut
        return g1, b1, qv, bo, g2, b2, up, bd

    def place(value):
        return collect(inner(corner_turn(value)), "zl").reshape(core_rows, width)

    def both_cores(value):
        return collect(value, "core").reshape(rows, -1)

    def total(partial):
        part = partial.reshape(nc, core_rows, width)
        part = pick(part, "core") + swap(pick_other(part, "core").astype(BF), "core").astype(F32)
        if nzl == 2:
            return part + swap(part.astype(BF), "zl").astype(F32)
        return lax.psum(part, "zl")

    seg = collect(segment_ids[0], "core")
    seg = lax.dynamic_index_in_dim(seg, here("zh"), 0, keepdims=False)
    half = group // 2
    block = jnp.stack([group_order, 2 * ctx_count - 1 - group_order], axis=1)
    pos = (block[:, :, None] * half + jnp.arange(half, dtype=jnp.int32)).reshape(rows)
    row_seg = jnp.take(seg, pos)
    distance = pos[:, None] - pos[None, :]
    allowed = (distance >= 0) & (row_seg[:, None] == row_seg[None, :])
    distance = distance.astype(F32)
    head_no = jnp.arange(rank_heads)
    head_no = (
        (here("zl") * span + head_no // (quarter // head_size)) * nc + here("core")
    ) * (quarter // head_size) + head_no % (quarter // head_size)
    slopes = jnp.exp2(-8.0 * (head_no.astype(F32) + 1.0) / HEADS)

    def scores_of(q, k):
        s = jnp.einsum("qhd,khd->hqk", q, k, preferred_element_type=F32) * scale
        return s - slopes[:, None, None] * distance[None]

    def split(qkv):
        return [
            v.reshape(rows, rank_heads, head_size) for v in jnp.split(qkv, 3, axis=1)
        ]

    weights = [fetch(layer) for layer in range(layers)]
    x = place(tokens[0]).astype(F32)
    kept = []
    for layer in range(layers):
        w_qkv, w_out, w_up, w_down = weights[layer]
        g1, b1, bo, g2, b2, bd = (v[layer] for v in vec)
        h1 = both_cores(norm_rows(x, g1, b1).astype(BF))
        qkv = (dot(h1, w_qkv) + qkv_bias[layer]).astype(BF)
        q, k, v = split(qkv)
        s = jnp.where(allowed, scores_of(q, k), -1e30)
        top = jnp.max(s, axis=-1, keepdims=True)
        p = jnp.where(allowed, jnp.exp(s - top), 0.0)
        den = jnp.sum(p, axis=-1, keepdims=True)
        p = p / den
        o = jnp.einsum("hqk,khd->qhd", p.astype(BF), v, preferred_element_type=F32)
        log_total = top + jnp.log(den)
        o = o.reshape(rows, rank_width).astype(BF)
        x1 = x + total(dot(o, w_out)) + bo
        h2 = both_cores(norm_rows(x1, g2, b2).astype(BF))
        u = dot(h2, w_up) + up_b[layer]
        a = gelu_tanh(u).astype(BF)
        x2 = x1 + total(dot(a, w_down)) + bd
        kept.append((x, h1, qkv, log_total, o, x1, h2, u, a))
        x = x2

    def leave(value):
        mine = lax.dynamic_index_in_dim(
            value.reshape(nzl, group, width), here("zl"), 0, keepdims=False
        )
        return corner_turn(inner(mine))[None]

    final_rows = leave(x.astype(BF))

    gx = place(cotangent[0]).astype(F32)
    result = [None] * layers
    for layer in reversed(range(layers)):
        w_qkv, w_out, w_up, w_down = weights[layer]
        g1, b1, bo, g2, b2, bd = (v[layer] for v in vec)
        x, h1, qkv, log_total, o, x1, h2, u, a = kept[layer]
        gy2_mine = gx.astype(BF)
        gy2 = both_cores(gy2_mine)
        d_down = outer_sum(a, gy2)
        d_bd = jnp.sum(gy2_mine.astype(F32), axis=0)
        _, gelu_back = jax.vjp(gelu_tanh, u)
        gu = gelu_back(dot_t(gy2, w_down))[0].astype(BF)
        d_up = outer_sum(h2, gu)
        d_bu = jnp.sum(gu.astype(F32), axis=0)
        _, back = jax.vjp(norm_rows, x1, g2, b2)
        gn, d_g2, d_b2 = back(total(dot_t(gu, w_up)))
        gm = gx + gn
        gy1_mine = gm.astype(BF)
        gy1 = both_cores(gy1_mine)
        d_out = outer_sum(o, gy1)
        d_bo = jnp.sum(gy1_mine.astype(F32), axis=0)
        go_f = dot_t(gy1, w_out)
        go = go_f.astype(BF).reshape(rows, rank_heads, head_size)
        q, k, v = split(qkv)
        p = jnp.where(allowed, jnp.exp(scores_of(q, k) - log_total), 0.0)
        dp = jnp.einsum("qhd,khd->hqk", go, v, preferred_element_type=F32)
        ds = (p * (dp - jnp.sum(dp * p, axis=-1, keepdims=True))).astype(BF)
        gq = scale * jnp.einsum("hqk,khd->qhd", ds, k, preferred_element_type=F32)
        gk = scale * jnp.einsum("hqk,qhd->khd", ds, q, preferred_element_type=F32)
        gv = jnp.einsum("hqk,qhd->khd", p.astype(BF), go, preferred_element_type=F32)
        gqkv = jnp.concatenate(
            [g.reshape(rows, rank_width) for g in (gq, gk, gv)], axis=1
        ).astype(BF)
        d_qkv = outer_sum(h1, gqkv)
        sums = jnp.sum(gqkv.astype(F32), axis=0)
        _, back = jax.vjp(norm_rows, x, g1, b1)
        gn, d_g1, d_b1 = back(total(dot_t(gqkv, w_qkv)))
        gx = gm + gn
        d_qv = (sums[:rank_width], sums[2 * rank_width :])
        big = send((d_qkv, d_out, d_up, d_down))
        tiny = send_small((d_g1, d_b1, d_qv, d_bo, d_g2, d_b2, d_bu, d_bd))
        result[layer] = (
            tiny[0], tiny[1], big[0], tiny[2], big[1], tiny[3],
            tiny[4], tiny[5], big[2], tiny[6], big[3], tiny[7],
        )
    stacked = [jnp.stack([result[layer][i] for layer in range(layers)]) for i in range(12)]
    return (final_rows, leave(gx)) + tuple(stacked)


def bit(axis, flip):
    place = lax.axis_index(axis)
    return 1 - place if flip else place


def slot_places():
    for slot in range(8):
        yield slot, bit("y", slot & 4), bit("x", slot & 2), bit("zh", slot & 1)


class View:
    def __init__(self, ref, row):
        self.ref, self.row = ref, row

    def _spot(self, spot):
        rows, columns = spot if isinstance(spot, tuple) else (spot, slice(None))
        if isinstance(rows, slice):
            return slice(rows.start + self.row, rows.stop + self.row), columns
        return pl.ds(rows.start + self.row, rows.size), columns

    def __getitem__(self, spot):
        return self.ref[self._spot(spot)]

    def __setitem__(self, spot, value):
        self.ref[self._spot(spot)] = value


class Rows:
    def __init__(self, refs):
        self.refs, self.size = refs, refs[0].shape[0]

    def _span(self, spot):
        rows = spot[0] if isinstance(spot, tuple) else spot
        if rows is Ellipsis:
            return 0, len(self.refs)
        return rows.start // self.size, rows.stop // self.size

    def __getitem__(self, spot):
        first, last = self._span(spot)
        return jnp.concatenate([r[...] for r in self.refs[first:last]], axis=0)

    def __setitem__(self, spot, value):
        first, last = self._span(spot)
        for i in range(first, last):
            self.refs[i][...] = value[(i - first) * self.size : (i - first + 1) * self.size]

    def block(self, which):
        low, high = self[slice(0, 128), :], self[slice(128, 256), :]
        return jnp.where(which == 0, low, high)


class Joined:
    def __init__(self, low, high, cut):
        self.low, self.high, self.cut = low, high, cut

    def __getitem__(self, spot):
        rows, columns = spot
        parts = []
        if rows.start < self.cut:
            parts.append(self.low[rows.start : min(rows.stop, self.cut), columns])
        if rows.stop > self.cut:
            parts.append(self.high[max(rows.start, self.cut) - self.cut : rows.stop - self.cut, columns])
        return parts[0] if len(parts) == 1 else jnp.concatenate(parts, axis=0)


def eight_slots(own, far, near_x, near_y, by_x, by_y, both, rows):
    cut = 128 if rows == 256 else 64
    across = Joined(View(by_y, rows), View(by_x, rows), cut)
    return own, far, near_x, by_x, near_y, by_y, across, both


def att_0_slots(refs):
    return eight_slots(*refs, 144)


def mlp_0_slots(refs):
    own, far_up, far_down, *refs = refs
    return eight_slots(own, Joined(far_up, far_down, 128), *refs, 256)


def att_1_slots(refs):
    own, far, by_x_1, by_y_1, by_x, by_y, both = refs
    return eight_slots(own, View(far, 0), View(by_x_1, 256), View(by_y_1, 256), by_x, by_y, both, 128)


def mlp_1_slots(refs):
    own, own_down, far, far_down, by_x_1, by_y_1, by_x, by_y, across_x, across_y, both = refs
    own, far = Joined(View(own, 128), own_down, 128), Joined(View(far, 128), far_down, 128)
    across = Joined(across_y, across_x, 128)
    return own, far, View(by_x_1, 192), by_x, View(by_y_1, 192), by_y, across, both


def second_message(far, near_x, near_y, to_x, to_y, rows):
    cut = 128 if rows == 256 else 64
    to_x[0:rows, :] = far[0:rows, :]
    to_y[0:rows, :] = far[0:rows, :]
    to_y[rows : rows + cut, :] = near_x[0:cut, :]
    to_x[rows : 2 * rows - cut, :] = near_y[cut:rows, :]


def att_0_message(far, near_x, near_y, to_x, to_y):
    second_message(far, near_x, near_y, to_x, to_y, 144)


def mlp_0_message(far_up, far_down, near_x, near_y, to_x, to_y, to_both):
    far = Joined(far_up, far_down, 128)
    to_both[...] = far[0:256, :]
    second_message(far, near_x, near_y, to_x, to_y, 256)


def att_1_message(far, near_x, near_y, own, own_down, to_x, to_y, to_both):
    to_both[...] = far[0:128, :]
    second_message(far, View(near_x, 256), View(near_y, 256), to_x, to_y, 128)
    for to in (to_x, to_y):
        to[192:320, :] = own[128:256, :]
        to[320:448, :] = own_down[...]


def mlp_1_message(far, far_down, near_x, near_y, to_all, to_x, to_y):
    to_all[...] = Joined(View(far, 128), far_down, 128)[0:256, :]
    to_y[...] = near_x[192:320, :]
    to_x[...] = near_y[320:448, :]


def slot_blocks():
    return [(r, (y * 2 + x) * 2 + zh) for r, y, x, zh in slot_places()]


def at(block, size):
    return pl.ds(pl.multiple_of(block * size, size), size)


def run(kernel, outs, *ins, after=(), us=1.0, anywhere=False, limit=16):
    smem = pl.BlockSpec(memory_space=pltpu.SMEM)
    vmem = pl.BlockSpec(memory_space=pltpu.VMEM)
    free = pl.BlockSpec(memory_space=pl.ANY)
    skip = len(after)

    def body(*refs):
        kernel(*refs[skip:])

    return pl.pallas_call(
        body,
        out_shape=tuple(outs),
        in_specs=[free] * skip
        + [smem if v.size == 4 else free if anywhere else vmem for v in ins],
        out_specs=tuple(vmem for _ in outs),
        scratch_shapes=getattr(kernel, "scratch", []),
        compiler_params=pltpu.CompilerParams(vmem_limit_bytes=limit << 20),
        cost_estimate=pl.CostEstimate(flops=int(us * 1e7), bytes_accessed=0, transcendentals=0),
    )(*after, *ins)


def gate(after, *values):
    skip = len(after)

    def body(*refs):
        refs[-1][...] = jnp.zeros_like(refs[-1])

    free = pl.BlockSpec(memory_space=pl.ANY)
    return pl.pallas_call(
        body,
        out_shape=tuple(shape(*v.shape, dtype=v.dtype) for v in values) + (shape(8, 128, dtype=F32),),
        in_specs=[free] * (skip + len(values)),
        out_specs=tuple(free for _ in values) + (pl.BlockSpec(memory_space=pltpu.VMEM),),
        input_output_aliases={skip + i: i for i in range(len(values))},
        compiler_params=pltpu.CompilerParams(vmem_limit_bytes=16 << 20),
        cost_estimate=pl.CostEstimate(flops=10**4, bytes_accessed=0, transcendentals=0),
    )(*after, *values)


def shape(*sizes, dtype=BF):
    return jax.ShapeDtypeStruct(sizes, dtype)


def with_scratch(kernel, *scratch):
    kernel.scratch = list(scratch)
    return kernel


def inner_columns(value):
    low = lax.broadcasted_iota(jnp.int32, (value.shape[0], 128), 1) < 64
    parts = []
    for i in range(0, value.shape[1], 256):
        a, b = value[:, i : i + 128], value[:, i + 128 : i + 256]
        parts.append(jnp.where(low, a, pltpu.roll(b, 64, 1)))
        parts.append(jnp.where(low, pltpu.roll(a, 64, 1), b))
    return jnp.concatenate(parts, axis=1)


def spread(value):
    n = value.shape[1]
    if n == 128:
        return value.astype(F32)
    hit = lax.broadcasted_iota(jnp.int32, (n, 128), 1) % n == lax.broadcasted_iota(
        jnp.int32, (n, 128), 0
    )
    return dot(value.astype(F32), hit.astype(F32))


RANKS = ((0, 0), (1, 0), (0, 1), (1, 1))


def qkv_blocks(core, zl):
    return [
        (s * 8 + zl * 4 + x * 2 + core, s * 2 + x) for s in range(3) for x in range(2)
    ]


def up_blocks(core, zl):
    return [
        (chip * 8 + core * 4 + zh * 2 + zl, chip * 2 + zh)
        for chip in range(4)
        for zh in range(2)
    ]


def fetch(sources, held, sems):
    copies = [pltpu.make_async_copy(*pair, sems.at[i]) for i, pair in enumerate(zip(sources, held))]
    for copy in copies:
        copy.start()
    for copy in copies:
        copy.wait()


def prepare_first(*refs):
    sources, refs = refs[:11], refs[11:]
    first, (out_a, out_b, down), (held, sems) = refs[0:4], refs[4:7], (refs[7:18], refs[18])
    fetch(sources[:9] + (sources[9].at[0], sources[10].at[0]), held, sems)
    rows = [spread(v[...]) for v in held[:8]]
    w_out, w_qkv, w_down = held[8:]
    small = jnp.concatenate([v[l : l + 1] for l in range(2) for v in rows], axis=0)
    for i, (dc, dl) in enumerate(RANKS):
        for src, dst in qkv_blocks(bit("core", dc), bit("zl", dl)):
            first[i][0:32, dst * 128 : dst * 128 + 128] = w_qkv[:, at(src, 128)]
        first[i][32:48, 0:128] = small.astype(BF)
        first[i][32:48, 128:768] = jnp.zeros((16, 640), BF)
    low_zl = lax.axis_index("zl") == 0
    for l in range(2):
        w = inner_columns(w_out[l].astype(F32)).astype(BF)
        out_a[l * 32 : l * 32 + 32] = jnp.where(low_zl, w[:, :512], w[:, 512:])
        out_b[l * 32 : l * 32 + 32] = jnp.where(low_zl, w[:, 512:], w[:, :512])
    down[...] = inner_columns(w_down[...].astype(F32)).astype(BF)


def prepare_rest(*refs):
    sources, refs = refs[:4], refs[4:]
    rest, (down, cot), (held, sems) = refs[0:4], refs[4:6], (refs[6:10], refs[10])
    fetch((sources[0].at[1], sources[1], sources[2].at[1], sources[3].at[0]), held, sems)
    w_qkv, w_up, w_down, cot_in = held
    for i, (dc, dl) in enumerate(RANKS):
        core, zl = bit("core", dc), bit("zl", dl)
        for src, dst in qkv_blocks(core, zl):
            rest[i][:, 1024 + dst * 128 : 1152 + dst * 128] = w_qkv[:, at(src, 128)]
        for src, dst in up_blocks(core, zl):
            rest[i][:, dst * 128 : dst * 128 + 128] = w_up[0, :, at(src, 128)]
            rest[i][:, 1792 + dst * 128 : 1920 + dst * 128] = w_up[1, :, at(src, 128)]
    down[...] = inner_columns(w_down[...].astype(F32)).astype(BF)
    cot[...] = inner_columns(cot_in[...].astype(F32)).astype(BF)


def put_out(piece, layer, out_a, out_b):
    for ref, flip in ((out_a, 0), (out_b, 1)):
        zl_from = bit("y", flip)
        for h in range(2):
            piece[pl.ds(pl.multiple_of(h * 64 + zl_from * 32, 32), 32), 768:1024] = ref[
                layer * 32 : layer * 32 + 32, h * 256 : h * 256 + 256
            ]


def pack_first(m0, m1, m2, m3, out_a, out_b, piece):
    lane = lax.broadcasted_iota(jnp.int32, (16, 128), 1)
    kind = lax.broadcasted_iota(jnp.int32, (16, 128), 0) % 8
    one = jnp.zeros((16, 128), F32)
    two = jnp.zeros((16, 128), F32)
    for i, m in enumerate((m0, m1, m2, m3)):
        core, zl = bit("core", RANKS[i][0]), bit("zl", RANKS[i][1])
        piece[at(core * 2 + zl, 32), 0:768] = m[0:32, :]
        s = m[32:48, 0:128].astype(F32)
        mine = (kind < 6) & (lane // 32 == core * 2 + zl)
        pair = (kind == 6) & (lane // 64 == zl)
        if i == 0:
            mine = mine | (kind == 7)
        one = one + jnp.where(mine | (pair & (core == 0)), s, 0.0)
        two = two + jnp.where(pair & (core == 1), s, 0.0)
    put_out(piece, 0, out_a, out_b)
    piece[128:144, 0:128] = one.astype(BF)
    piece[128:144, 128:256] = two.astype(BF)
    piece[128:144, 256:1024] = jnp.zeros((16, 768), BF)


def pack_rest(m0, m1, m2, m3, out_a, out_b, down_0, mlp_0, up_0, deep, pair):
    for i, m in enumerate((m0, m1, m2, m3)):
        spot = at(bit("core", RANKS[i][0]) * 2 + bit("zl", RANKS[i][1]), 32)
        up_0[spot, :] = m[:, 0:1024]
        deep[spot, 0:768] = m[:, 1024:1792]
        deep[at(4 + bit("core", RANKS[i][0]) * 2 + bit("zl", RANKS[i][1]), 32), :] = m[:, 1792:2816]
    put_out(deep, 1, out_a, out_b)
    mlp_0[0:128, :] = up_0[...]
    mlp_0[128:256, :] = down_0[...]
    pair[0:256, :] = mlp_0[...]
    pair[256:384, :] = deep[0:128, :]


def both_ways(value):
    return lax.ppermute(value, ("y", "x"), [(0, 3), (3, 0), (1, 2), (2, 1)])


def first_hops(piece):
    return swap(piece, "zh"), swap(piece, "x"), swap(piece, "y")


def load_rows(pieces, scratch, row, columns):
    for r, block in slot_blocks():
        scratch[at(block, 128), :] = pieces[r][row : row + 128, 0:columns]


def load_out(pieces, scratch):
    for r, y, x, zh in slot_places():
        for h in range(2):
            scratch[at(x * 2 + zh, 64), at(y * 2 + h, 256)] = pieces[r][
                h * 64 : h * 64 + 64, 768:1024
            ]


def normal(x):
    centred = x - jnp.mean(x, axis=-1, keepdims=True)
    inv = lax.rsqrt(jnp.mean(centred * centred, axis=-1, keepdims=True) + EPSILON)
    return centred * inv, inv


def load_stream(blocks, scratch):
    for i, (dc, dl) in enumerate(RANKS):
        spot = at(bit("core", dc) * 2 + bit("zl", dl), 128)
        scratch[spot, :] = inner_columns(blocks[i][0].astype(F32)).astype(scratch.dtype)


def load_blocks(blocks, scratch):
    for i, (dc, dl) in enumerate(RANKS):
        scratch[at(bit("core", dc) * 2 + bit("zl", dl), 128), :] = blocks[i][...]


def load_cores(mine, other, scratch):
    scratch[at(bit("core", 0), 256), :] = Rows(mine)[...]
    scratch[at(bit("core", 1), 256), :] = Rows(other)[...]


def split_product(left, right, keep, send):
    mine, other = at(bit("core", 0), 256), at(bit("core", 1), 256)
    Rows(send)[...] = right(left[other, :]).astype(BF)
    keep[...] = right(left[mine, :])


def row_positions(order, dim):
    shape_ = (512, 1) if dim == 0 else (1, 512)
    row = lax.broadcasted_iota(jnp.int32, shape_, dim)
    start = jnp.zeros(shape_, jnp.int32)
    for c in range(4):
        lead = order[c]
        start = jnp.where(row // 64 == 2 * c, lead, start)
        start = jnp.where(row // 64 == 2 * c + 1, 7 - lead, start)
    return start * 64 + row % 64


def masked_distance(seg_a, seg_b, order, dist):
    same = lax.axis_index("core") == lax.axis_index("zh")
    seg = jnp.where(same, seg_a[...], seg_b[...])
    ends = [jnp.sum((seg < d).astype(jnp.int32), axis=1, keepdims=True) for d in (1, 2)]

    def doc(pos):
        return (pos >= ends[0]).astype(jnp.int32) + (pos >= ends[1]).astype(jnp.int32)

    rows, cols = row_positions(order, 0), row_positions(order, 1)
    gap = rows - cols
    fine = (gap >= 0) & (doc(rows) == doc(cols))
    dist[...] = jnp.where(fine, gap.astype(F32), 1e32)


def slope_of(pair, half):
    core, zl = lax.axis_index("core"), lax.axis_index("zl")
    value = jnp.float32(0.0)
    for c in range(2):
        for z in range(2):
            head = 8 * z + 4 * pair + 2 * c + half
            value = jnp.where((core == c) & (zl == z), jnp.float32(2.0 ** (-8.0 * (head + 1) / HEADS)), value)
    return value


def attend(qkv, dist, probs, o):
    low = lax.broadcasted_iota(jnp.int32, (512, 128), 1) < 64

    def heads(pair, carry):
        q = qkv[:, at(pair, 128)]
        k = qkv[:, at(2 + pair, 128)]
        v = qkv[:, at(4 + pair, 128)]
        found = []
        for half in range(2):
            qh = jnp.where(low == (half == 0), q, jnp.zeros_like(q))
            slope = jnp.where(pair == 0, slope_of(0, half), slope_of(1, half))
            s = dot_t(qh, k) * 0.125 - slope * dist[...]
            p = jnp.exp(s - jnp.max(s, axis=1, keepdims=True))
            p = (p / jnp.sum(p, axis=1, keepdims=True)).astype(BF)
            probs[pair * 2 + half] = p
            found.append(dot(p, v))
        o[:, at(pair, 128)] = jnp.where(low, *found).astype(BF)
        return carry

    lax.fori_loop(0, 2, heads, 0)


def attention_part(h1, vec, layer, pieces, seg_a, seg_b, order, outs, scratch):
    qkv, probs, o, keep, *send = outs
    wq, wo, dist = scratch
    load_rows(pieces, wq, 0, 768)
    load_out(pieces, wo)
    masked_distance(seg_a, seg_b, order, dist)
    qkv[...] = (dot(h1[...], wq[...]) + vec[layer * 8 + 6 : layer * 8 + 7, 0:768]).astype(BF)
    attend(qkv, dist, probs, o)
    split_product(o, lambda rows: dot(rows, wo[...]), keep, send)


def first_attention(t0, t1, t2, t3, *refs):
    pieces, (seg_a, seg_b, order), refs = att_0_slots(refs[:7]), refs[7:10], refs[10:]
    vec, h1, outs, scratch = refs[0], refs[1], refs[2:8], refs[8:]
    q_one, q_two, scratch = scratch[0], scratch[1], scratch[2:]
    for r, block in slot_blocks():
        vec[:, at(block, 128)] = pieces[r][128:144, 0:128].astype(F32)
        q_two[:, at(block, 128)] = pieces[r][128:144, 128:256].astype(F32)
    q_one[...] = vec[...]
    core, zl = lax.axis_index("core"), lax.axis_index("zl")
    for l in range(2):
        row = slice(l * 8 + 6, l * 8 + 7)
        for base, y in ((0, 0), (512, 1)):
            block = (y * 2 + zl) * 2 + core
            vec[row, base : base + 128] = q_one[row, at(block, 128)]
            vec[row, base + 128 : base + 256] = q_two[row, at(block, 128)]
        vec[row, 256:512] = jnp.zeros((1, 256), F32)
    load_stream((t0, t1, t2, t3), h1)
    for i in range(4):
        spot = slice(i * 128, i * 128 + 128)
        z, _ = normal(h1[spot, :].astype(F32))
        h1[spot, :] = (z * vec[0:1, :] + vec[1:2, :]).astype(BF)
    attention_part(h1, vec, 0, pieces, seg_a, seg_b, order, outs, scratch)


def next_attention(*refs):
    mine, other, refs = refs[:2], refs[2:4], refs[4:]
    pieces, (vec, seg_a, seg_b, order), refs = att_1_slots(refs[:7]), refs[7:11], refs[11:]
    h1, outs, scratch = refs[0], refs[1:7], refs[7:]
    load_cores(mine, other, h1)
    attention_part(h1, vec, 1, pieces, seg_a, seg_b, order, outs, scratch)


def add_parts(keep, *refs):
    came, out = Rows(refs[:2]), refs[2]
    out[...] = (keep[...] + came[...].astype(F32)).astype(BF)


def norm_stage(bias_row, gain_row):
    def kernel(x, part, came, vec, x_out, *h):
        h = Rows(h)
        for i in range(2):
            spot = slice(i * 128, i * 128 + 128)
            v = x[spot, :] + part[spot, :].astype(F32) + came[spot, :].astype(F32)
            v = v + vec[bias_row : bias_row + 1, :]
            x_out[spot, :] = v
            z, _ = normal(v)
            h[spot, :] = (z * vec[gain_row : gain_row + 1] + vec[gain_row + 1 : gain_row + 2]).astype(BF)

    return kernel


def first_norm_stage(t0, t2, part, came, vec, *refs):
    x_out, h, x0 = refs[0], refs[1:3], refs[3]
    x0[at(bit("zl", 0), 128), :] = inner_columns(t0[0].astype(F32))
    x0[at(bit("zl", 1), 128), :] = inner_columns(t2[0].astype(F32))
    norm_stage(2, 3)(x0, part, came, vec, x_out, *h)


def mlp_weights(refs, layer):
    count = 11 if layer else 8
    return (mlp_1_slots if layer else mlp_0_slots)(refs[:count]), refs[count:]


def mlp_stage(layer):
    def kernel(*refs):
        mine, other, refs = refs[:2], refs[2:4], refs[4:]
        pieces, refs = mlp_weights(refs, layer)
        vec, h2, u, a, keep, *send, w = refs
        load_cores(mine, other, h2)
        load_rows(pieces, w, 0, 1024)
        for i in range(4):
            spot = slice(i * 128, i * 128 + 128)
            z = dot(h2[spot, :], w[...]) + vec[layer * 8 + 7 : layer * 8 + 8, :]
            u[spot, :] = z
            a[spot, :] = gelu_tanh(z).astype(BF)
        load_rows(pieces, w, 128, 1024)
        split_product(a, lambda rows: dot(rows, w[...]), keep, send)

    return with_scratch(kernel, pltpu.VMEM((1024, 1024), BF))


def finish_rows(x, part, came, vec, out):
    v = x[at(bit("zl", 0), 128), :] + part[...].astype(F32) + came[...].astype(F32) + vec[13:14, :]
    out[0] = inner_columns(v).astype(BF)


def add_split(keep, *refs):
    came, mine, other = Rows(refs[:2]), refs[2], refs[3]
    for to, flip in ((mine, 0), (other, 1)):
        which = bit("zl", flip)
        to[...] = (keep[at(which, 128), :] + came.block(which).astype(F32)).astype(BF)


def gelu_slope(u):
    c = 0.7978845608028654
    t = jnp.tanh(c * (u + 0.044715 * u * u * u))
    return 0.5 * (1.0 + t) + 0.5 * u * (1.0 - t * t) * (c * (1.0 + 3 * 0.044715 * u * u))


def mlp_back(layer):
    def kernel(*refs):
        if layer == 1:
            blocks, u, refs = refs[:4], refs[4], refs[5:]
        else:
            blocks, u, refs = refs[:4], refs[4], refs[5:]
        pieces, (gy2, gu, keep, *send, w) = mlp_weights(refs, layer)
        load_blocks(blocks, gy2) if layer == 1 else load_cores(blocks[:2], blocks[2:], gy2)
        load_rows(pieces, w, 128, 1024)
        for i in range(4):
            spot = slice(i * 128, i * 128 + 128)
            gu[spot, :] = (dot_t(gy2[spot, :], w[...]) * gelu_slope(u[spot, :])).astype(BF)
        load_rows(pieces, w, 0, 1024)
        split_product(gu, lambda rows: dot_t(rows, w[...]), keep, send)

    return with_scratch(kernel, pltpu.VMEM((1024, 1024), BF))


def turned_dot(left, right):
    return lax.dot_general(left, right, (((0,), (0,)), ((), ())), preferred_element_type=F32)


def slot_spots(rows, to_y, to_x, near_0, near_1, far_0, far_1):
    return (
        near_0, far_0, near_1, View(to_x, 0), View(to_y, 0), far_1, View(to_y, rows), View(to_x, rows),
    )


def mlp_grads(h2, a, gy2, gu, *outs):
    spots = slot_spots(256, *outs)
    for r, block in slot_blocks():
        spots[r][0:128, :] = turned_dot(h2[:, at(block, 128)], gu[...]).astype(BF)
        spots[r][128:256, :] = turned_dot(a[:, at(block, 128)], gy2[...]).astype(BF)


def second_sums(rows, near_1, near, far_1, far, to_x, to_y):
    to_x[0:rows, :] = (near_1[...].astype(F32) + near[0:rows, :].astype(F32)).astype(BF)
    to_y[0:rows, :] = (far_1[...].astype(F32) + far[0:rows, :].astype(F32)).astype(BF)


def third_sum(rows, far_0, far, far_2, out):
    total = far_0[...].astype(F32) + far[0:rows, :].astype(F32) + far_2[0:rows, :].astype(F32)
    out[...] = total.astype(BF)


def norm_back(gx, part, came, x, gain, gm, gy, sums):
    totals = [jnp.zeros((1, x.shape[1]), F32) for _ in range(4)]
    for i in range(part.shape[0] // 128):
        spot = slice(i * 128, i * 128 + 128)
        dh = part[spot, :].astype(F32) + came[spot, :].astype(F32)
        z, inv = normal(x[spot, :])
        dz = dh * gain
        mean_a = jnp.mean(dz, axis=-1, keepdims=True)
        mean_b = jnp.mean(dz * z, axis=-1, keepdims=True)
        up = gx[spot, :]
        g = up + inv * (dz - mean_a - z * mean_b)
        gm[spot, :] = g
        rounded = g.astype(BF)
        gy[spot, :] = rounded
        new = (dh * z, dh, rounded.astype(F32), up.astype(BF).astype(F32))
        totals = [t + jnp.sum(v, axis=0, keepdims=True) for t, v in zip(totals, new)]
    sums[...] = jnp.concatenate(totals + [jnp.zeros((4, x.shape[1]), F32)], axis=0)


def norm_back_stage(gain_row):
    def kernel(gx, part, came, x, vec, gm, *refs):
        norm_back(gx, part, came, x, vec[gain_row : gain_row + 1, :], gm, Rows(refs[:2]), refs[2])

    return kernel


def first_norm_back(c0, c2, part, came, x, vec, gm, *refs):
    gy, sums, gx = Rows(refs[:2]), refs[2], refs[3]
    gx[at(bit("zl", 0), 128), :] = c0[...].astype(F32)
    gx[at(bit("zl", 1), 128), :] = c2[...].astype(F32)
    norm_back(gx, part, came, x, vec[11:12, :], gm, gy, sums)


def last_norm_back(gx, part, came, t0, vec, grad, up, x, gm, gy, sums):
    x[...] = inner_columns(t0[0].astype(F32))
    up[...] = gx[at(bit("zl", 0), 128), :]
    norm_back(up, part, came, x, vec[0:1, :], gm, gy, sums)
    grad[0] = inner_columns(gm[...]).astype(BF)


def attention_back(layer):
    def kernel(*refs):
        mine, other, (qkv, probs), refs = refs[:2], refs[2:4], refs[4:6], refs[6:]
        pieces = (att_1_slots if layer else att_0_slots)(refs[:7])
        attention_back_part(mine, other, qkv, probs, pieces, *refs[7:])

    return kernel


def attention_back_part(mine, other, qkv, probs, pieces, *refs):
    gy1, gqkv, keep, *send, wq, wo, go, gk, gv = refs
    load_cores(mine, other, gy1)
    load_rows(pieces, wq, 0, 768)
    load_out(pieces, wo)
    go[...] = dot_t(gy1[...], wo[...]).astype(BF)
    low = lax.broadcasted_iota(jnp.int32, (512, 128), 1) < 64

    def heads(pair, carry):
        q = qkv[:, at(pair, 128)]
        k = qkv[:, at(2 + pair, 128)]
        v = qkv[:, at(4 + pair, 128)]
        g = go[:, at(pair, 128)]
        found = []
        for half in range(2):
            lanes = low == (half == 0)
            gh = jnp.where(lanes, g, jnp.zeros_like(g))
            p = probs[pair * 2 + half]
            pf = p.astype(F32)
            dp = dot_t(gh, v)
            ds = (pf * (dp - jnp.sum(dp * pf, axis=1, keepdims=True))).astype(BF)
            found.append((dot(ds, k), turned_dot(ds, q), turned_dot(p, g)))
        for part, scale in ((0, 0.125), (1, 0.125), (2, 1.0)):
            value = scale * jnp.where(low, found[0][part], found[1][part])
            gqkv[:, at(part * 2 + pair, 128)] = value.astype(BF)
        return carry

    lax.fori_loop(0, 2, heads, 0)
    split_product(gqkv, lambda rows: dot_t(rows, wq[...]), keep, send)


def attention_grads(rows, h1, o, gy1, gqkv, outs, d_out):
    spots = slot_spots(rows, *outs)
    d_out[...] = turned_dot(o[...], gy1[...]).astype(BF)
    for (r, block), (_, y, x, zh) in zip(slot_blocks(), slot_places()):
        spots[r][0:128, 0:768] = turned_dot(h1[:, at(block, 128)], gqkv[...]).astype(BF)
        for h in range(2):
            spots[r][h * 64 : h * 64 + 64, 768:1024] = d_out[at(x * 2 + zh, 64), at(y * 2 + h, 256)]
    return spots


def window_1(h2, a, gy2, gu, *outs):
    mlp_grads(h2, a, gy2, gu, *outs)


def window_2(h1, o, gy1, gqkv, near_1, y_1, far_1, x_1, to_y, to_x, *rest):
    attention_grads(128, h1, o, gy1, gqkv, (to_y, to_x) + rest[:4], rest[4])
    second_sums(256, near_1, View(y_1, 256), far_1, View(x_1, 256), View(to_x, 256), View(to_y, 256))


def window_3(h2, a, gy2, gu, near_1, y_2, far_1, x_2, far_0, x_1, to_y, to_x, *rest):
    mlp_grads(h2, a, gy2, gu, to_y, to_x, *rest[:4])
    second_sums(128, near_1, View(y_2, 128), far_1, View(x_2, 128), View(to_x, 512), View(to_y, 512))
    third_sum(256, far_0, x_1, View(y_2, 256), rest[4])


def window_4(near_1, y_3, far_1, x_3, far_0, x_2, to_x, to_y, to_zh):
    second_sums(256, near_1, View(y_3, 256), far_1, View(x_3, 256), to_x, to_y)
    third_sum(128, far_0, x_2, View(y_3, 512), to_zh)


def window_5(*refs):
    grads, (to_y, to_x), rest = refs[:17], refs[17:19], refs[19:]
    last_attention_grads(*grads, (to_y, to_x) + rest[:4], *rest[4:])


def second_only(near_1, y, far_1, x, to_x, to_y):
    second_sums(144, near_1, View(y, 144), far_1, View(x, 144), to_x, to_y)


def third_only(far_0, x, y, to_zh):
    third_sum(256, far_0, x, y, to_zh)


def window_6(far_0, x_4, y_5, to_zh):
    third_sum(144, far_0, x_4, y_5, to_zh)


def last_attention_grads(
    h1, o, gy1, gqkv, g1, e1, e0, gu1, gu0, gq1, keep, s0, s1, t0, t1, t2, t3, outs, d_out, ups, wide
):
    spots = attention_grads(144, h1, o, gy1, gqkv, outs, d_out)
    send = Rows((s0, s1))
    none = jnp.zeros((2, 1024), F32)
    gain = jnp.zeros((1, 1024), F32)
    shift = jnp.zeros((1, 1024), F32)
    for i, block in enumerate((t0, t1, t2, t3)):
        dc, dl = RANKS[i]
        z, _ = normal(inner_columns(block[0].astype(F32)))
        which = bit("zl", dl)
        dh = send.block(which).astype(F32) if dc else keep[at(which, 128), :]
        gain = gain + jnp.sum(dh * z, axis=0, keepdims=True)
        shift = shift + jnp.sum(dh, axis=0, keepdims=True)
    parts = [g1[0:2, :], e1[2:3, :], e1[0:2, :], e1[3:4, :], none, gain, shift]
    wide[...] = jnp.concatenate(parts + [e0[2:3, :], e0[0:2, :], e0[3:4, :], none], axis=0)
    sums = [jnp.sum(v[...].astype(F32), axis=0, keepdims=True) for v in (gu1, gu0)]
    ups[...] = jnp.concatenate(sums + [jnp.zeros((14, 1024), F32)], axis=0)
    q = [jnp.sum(v[...].astype(F32), axis=0, keepdims=True) for v in (gq1, gqkv)]
    q = jnp.concatenate(q + [jnp.zeros((14, 768), F32)], axis=0)
    core, zl = lax.axis_index("core"), lax.axis_index("zl")
    for r, block in slot_blocks():
        rows = slice(128, 144)
        spots[r][rows, 0:128] = wide[:, at(block, 128)].astype(BF)
        spots[r][rows, 128:256] = ups[:, at(block, 128)].astype(BF)
        mine = jnp.where(block == 4 + zl * 2 + core, q[:, 512:768], jnp.zeros((16, 256), F32))
        mine = jnp.where(block == zl * 2 + core, q[:, 0:256], mine)
        spots[r][rows, 256:512] = mine.astype(BF)
        spots[r][rows, 512:1024] = jnp.zeros((16, 512), BF)


def summed(parts, rows, columns):
    value = parts[0][rows, columns].astype(F32)
    for part in parts[1:]:
        value = value + part[rows, columns].astype(F32)
    return value


def own_out(parts, flip):
    row = bit("y", flip) * 32
    halves = []
    for h in range(2):
        spot = pl.ds(pl.multiple_of(h * 64 + row, 32), 32)
        halves.append(summed(parts, spot, slice(768, 1024)))
    return jnp.concatenate(halves, axis=1)


def rank_rows(i):
    return at(bit("core", RANKS[i][0]) * 2 + bit("zl", RANKS[i][1]), 32)


def unpack_first(y_1, y_2, x_2, x_3, m_near, m_far, a_near, a_far, mine, *refs):
    mlp = (m_near, y_1, View(x_2, 256), m_far)
    att = (a_near, y_2, View(x_3, 512), a_far)
    sends, a, b, down = refs[0:3], refs[3], refs[4], refs[5]
    for i in range(4):
        to = mine if i == 0 else sends[i - 1]
        for parts, start, width in ((att, 0, 768), (mlp, 768, 1024)):
            value = summed(parts, rank_rows(i), slice(0, width))
            to[:, start : start + width] = value.astype(to.dtype)
    a[...] = own_out(att, 0).astype(BF)
    b[...] = own_out(att, 1).astype(BF)
    down[...] = inner_columns(summed(mlp, slice(128, 256), slice(0, 1024)))


def unpack_last(y_3, y_5, x_4, x_6, m_near, m_far, a_near, a_far, a1, b1, down_1, mine, *refs):
    mlp = (m_near, y_3, x_4, m_far)
    att = (a_near, y_5, x_6, a_far)
    sends, (a, b), down = refs[0:3], refs[3:5], refs[5]
    for i in range(4):
        to = mine if i == 0 else sends[i - 1]
        to[0:32, 0:768] = summed(att, rank_rows(i), slice(0, 768)).astype(to.dtype)
        to[0:32, 768:1792] = summed(mlp, rank_rows(i), slice(0, 1024)).astype(to.dtype)
        to[32:48, 0:768] = summed(att, slice(128, 144), slice(0, 768)).astype(to.dtype)
        to[32:48, 768:1792] = jnp.zeros((16, 1024), to.dtype)
    a[0:32, :] = own_out(att, 0).astype(BF)
    b[0:32, :] = own_out(att, 1).astype(BF)
    a[32:64, :] = a1[...]
    b[32:64, :] = b1[...]
    down[0] = inner_columns(summed(mlp, slice(128, 256), slice(0, 1024)))
    down[1] = down_1[...]


def finish(rest, r1, r2, r3, last, l1, l2, l3, a, b, *outs):
    g1, b1, w_qkv, qv, w_out, bo, g2, b2, w_up, up, bd = outs
    for i, (rm, lm) in enumerate(((rest, last), (r1, l1), (r2, l2), (r3, l3))):
        core, zl = bit("core", RANKS[i][0]), bit("zl", RANKS[i][1])
        for src, dst in qkv_blocks(core, zl):
            w_qkv[0, :, at(src, 128)] = lm[0:32, dst * 128 : dst * 128 + 128].astype(F32)
            w_qkv[1, :, at(src, 128)] = rm[:, dst * 128 : dst * 128 + 128].astype(F32)
        for src, dst in up_blocks(core, zl):
            w_up[0, :, at(src, 128)] = lm[0:32, 768 + dst * 128 : 896 + dst * 128].astype(F32)
            w_up[1, :, at(src, 128)] = rm[:, 768 + dst * 128 : 896 + dst * 128].astype(F32)
    low_zl = lax.axis_index("zl") == 0
    for l in range(2):
        va, vb = a[l * 32 : l * 32 + 32].astype(F32), b[l * 32 : l * 32 + 32].astype(F32)
        w = jnp.concatenate([jnp.where(low_zl, va, vb), jnp.where(low_zl, vb, va)], axis=1)
        w_out[l] = inner_columns(w)
    spot = lax.axis_index("core") * 2 + lax.axis_index("zl")

    def chunk(value, size):
        found = jnp.zeros((value.shape[0], size), F32)
        for j in range(4):
            found = jnp.where(spot == j, value[:, j * size : j * size + size], found)
        return found

    mine, by_core = last[32:48, 0:128], l1[32:48, 0:128].astype(F32)
    wide = chunk(mine + by_core, 32)
    late = l2[32:48, 0:128].astype(F32) + l3[32:48, 0:128].astype(F32)
    late = chunk(mine + by_core + late, 32)
    for row, ref in ((2, bo), (3, g2), (4, b2), (5, bd)):
        ref[...] = jnp.concatenate([wide[row + 8 : row + 9], wide[row : row + 1]], axis=0)
    g1[...] = jnp.concatenate([late[8:9], wide[0:1]], axis=0)
    b1[...] = jnp.concatenate([late[9:10], wide[1:2]], axis=0)
    up[...] = jnp.concatenate([last[33:34, 128:256], last[32:33, 128:256]], axis=0)
    both = last[32:48, 256:512]
    for m in (l1, l2, l3):
        both = both + m[32:48, 256:512].astype(F32)
    both = chunk(both, 64)
    qv[...] = jnp.concatenate([both[1:2], both[0:1]], axis=0)


def corner(value):
    return lax.ppermute(value, ("core", "zh"), [(0, 0), (1, 2), (2, 1), (3, 3)])


def to_partners(messages):
    one, two, three = messages
    return (
        swap(one, "core"),
        swap(two, "zl"),
        lax.ppermute(three, ("core", "zl"), [(0, 3), (3, 0), (1, 2), (2, 1)]),
    )


def narrow_body(
    tokens, segment_ids, group_order, ln1_gain, ln1_bias, qkv_weight, qv_bias, out_weight, out_bias,
    ln2_gain, ln2_bias, up_weight, up_bias, down_weight, down_bias, cotangent,
):
    small = (ln1_gain, ln1_bias, out_bias, ln2_gain, ln2_bias, down_bias, qv_bias, up_bias)

    def held(*values):
        return [pltpu.VMEM(v, BF) for v in values] + [pltpu.SemaphoreType.DMA((len(values),))]

    row, rowf = shape(256, 1024), shape(256, 1024, dtype=F32)
    halves = [shape(128, 1024)] * 2

    ready = run(
        with_scratch(
            prepare_first, *held(*[v.shape for v in small], (2, 32, 1024), (32, 3072), (128, 1024))
        ),
        [shape(48, 768)] * 4 + [shape(64, 512)] * 2 + [shape(128, 1024)],
        *small, out_weight, qkv_weight, down_weight, anywhere=True, limit=60, us=3,
    )
    out_b = lax.ppermute(ready[5], ("y", "zl"), [(0, 2), (1, 0), (2, 3), (3, 1)])
    out_a = lax.ppermute(ready[4], ("y", "zl"), [(0, 0), (1, 2), (2, 1), (3, 3)])
    first = (ready[0],) + to_partners(ready[1:4])
    (att_0,) = run(pack_first, [shape(144, 1024)], *first, out_a, out_b)
    far, near_x, near_y = first_hops(att_0)
    block = corner(tokens)
    rest = run(
        with_scratch(
            prepare_rest, *held((32, 3072), (2, 32, 4096), (128, 1024), (128, 1024))
        ),
        [shape(32, 2816)] * 4 + [shape(128, 1024)] * 2,
        qkv_weight, up_weight, down_weight, cotangent, after=(ready[0],), anywhere=True, us=2,
    )
    cot = rest[5]
    mlp_0, up_0, deep, pair = run(
        pack_rest, [row, shape(128, 1024), row, shape(384, 1024)],
        rest[0], *to_partners(gate((att_0,), *rest[1:4])[:3]), out_a, out_b, ready[6],
    )
    down_1 = rest[4]
    def second_hops(kernel, rows_x, rows_y, *ins, after=(), rows=0):
        outs = [shape(n, 1024) for n in (rows_x, rows_y, rows) if n]
        to = run(kernel, outs, *ins, after=after)
        return swap(to[0], "x"), swap(to[1], "y"), both_ways(to[2] if rows else ins[0]), to[0]

    by_x, by_y, both, sent = second_hops(
        att_0_message, 224, 208, far, near_x, near_y, after=(pair, block)
    )
    att_0 = (att_0, far, near_x, near_y, by_x, by_y, both)
    up_0, down_0, _ = gate((sent,), up_0, ready[6])
    far_up, far_down = swap(up_0, "zh"), swap(down_0, "zh")
    by_zl = swap(block, "zl")
    pair, deep, token = gate((by_x, by_y, both, far_up, by_zl), pair, deep)
    pair_x, pair_y = swap(pair, "x"), swap(pair, "y")
    blocks = (block, swap(block, "core"), by_zl, swap(by_zl, "core"))
    segments = (segment_ids, swap(segment_ids, "core"), group_order)

    def cores(values):
        return [swap(v, "core") for v in values]

    def summed_core(keep, *send, after=()):
        (part,) = run(add_parts, [row], keep, *cores(send), after=after)
        return part, swap(part, "zl")

    def split_core(keep, *send, after=()):
        part, other = run(add_split, [shape(128, 1024)] * 2, keep, *cores(send), after=after)
        return part, swap(other, "zl")

    def with_other(values):
        return (*values, *cores(values))

    attention_outs = [
        shape(512, 1024), shape(512, 768), shape(4, 512, 512), shape(512, 256), rowf, *halves,
    ]
    weights_scratch = [pltpu.VMEM((1024, 768), BF), pltpu.VMEM((256, 1024), BF)]
    dist = pltpu.VMEM((512, 512), F32)
    vec_scratch = [pltpu.VMEM((16, 1024), F32)] * 2
    mlp_outs = [shape(512, 1024), shape(512, 1024, dtype=F32), shape(512, 1024), rowf, *halves]

    vec, h1_0, qkv_0, probs_0, o_0, keep, *send = run(
        with_scratch(first_attention, *vec_scratch, *weights_scratch, dist),
        [shape(16, 1024, dtype=F32)] + attention_outs, *blocks, *att_0, *segments, after=(token,), us=10,
    )
    far_down, pair_x, pair_y, deep, down_1, *send, _ = gate(
        (keep,), far_down, pair_x, pair_y, deep, down_1, *send
    )
    deep_far = swap(deep, "zh")
    part, came = summed_core(keep, *send)
    by_x, by_y, both, token = second_hops(
        mlp_0_message, 384, 384, far_up, far_down, pair_x, pair_y, after=(part,), rows=256
    )
    mlp_0 = (mlp_0, far_up, far_down, pair_x, pair_y, by_x, by_y, both)
    x1_0, *h = run(
        with_scratch(first_norm_stage, pltpu.VMEM((256, 1024), F32)),
        [rowf, *halves], blocks[0], blocks[2], part, came, vec, after=(token,), us=1.5,
    )
    h2_0, u_0, a_0, keep, *send = run(
        mlp_stage(0), mlp_outs, *with_other(h), *mlp_0, vec, after=(deep_far,), us=4
    )
    down_1_far = swap(down_1, "zh")
    one_x, one_y, both, token = second_hops(
        att_1_message, 448, 448, deep_far, pair_x, pair_y, deep, down_1, after=(keep,), rows=128
    )
    att_1 = (deep, deep_far, pair_x, pair_y, one_x, one_y, both)
    part, came = summed_core(keep, *send)
    x2_0, *h = run(norm_stage(5, 8), [rowf, *halves], x1_0, part, came, vec, after=(token, down_1_far), us=1)
    to_all, to_x, to_y = run(
        mlp_1_message, [row, shape(128, 1024), shape(128, 1024)], deep_far, down_1_far, one_x, one_y,
        after=(both,),
    )
    by_x, by_y = swap(to_all, "x"), swap(to_all, "y")
    h1_1, qkv_1, probs_1, o_1, keep, *send = run(
        with_scratch(next_attention, *weights_scratch, dist),
        attention_outs, *with_other(h), *att_1, vec, *segments, after=(to_all,), us=9,
    )
    by_x, by_y, to_x, to_y, *send, _ = gate((keep,), by_x, by_y, to_x, to_y, *send)
    mlp_1 = (
        deep, down_1, deep_far, down_1_far, one_x, one_y, by_x, by_y,
        swap(to_x, "x"), swap(to_y, "y"), both_ways(to_all),
    )
    cot, _ = gate((keep,), cot)
    cot = corner(cot)
    part, came = summed_core(keep, *send)
    x1_1, *h = run(norm_stage(10, 11), [rowf, *halves], x2_0, part, came, vec, after=(token,), us=1)
    by_zl = swap(cot, "zl")
    cots = (cot, swap(cot, "core"), by_zl, swap(by_zl, "core"))
    h2_1, u_1, a_1, keep, *send = run(mlp_stage(1), mlp_outs, *with_other(h), *mlp_1, vec, us=4)

    mlp_back_outs = [shape(512, 1024), shape(512, 1024), rowf, *halves]
    norm_outs = [rowf, *halves, shape(8, 1024, dtype=F32)]
    attention_back_outs = [shape(512, 1024), shape(512, 768), rowf, *halves]
    attention_back_scratch = weights_scratch + [
        pltpu.VMEM((512, 256), BF), pltpu.VMEM((512, 128), F32), pltpu.VMEM((512, 128), F32),
    ]

    def grad_outs(sent, rows):
        return [shape(sent, 1024)] * 2 + [shape(rows, 1024)] * 4

    out_scratch = pltpu.VMEM((256, 1024), BF)

    keep_last, send_last = keep, send
    part_last, came_last = split_core(keep_last, *send_last)
    gy2, gu_1, keep, *send = run(mlp_back(1), mlp_back_outs, *cots, u_1, *mlp_1, after=(part_last,), us=6)
    came_last, *send, _ = gate((keep,), came_last, *send)
    part, came = summed_core(keep, *send)
    to_y, to_x, m1_near_0, m1_near_1, m1_far_0, m1_far_1 = run(
        window_1, grad_outs(512, 256), h2_1, a_1, gy2, gu_1, after=(part,), us=4
    )
    y_1, x_1 = swap(to_y, "y"), swap(to_x, "x")
    gm, *gy, e1 = run(
        with_scratch(first_norm_back, pltpu.VMEM((256, 1024), F32)),
        norm_outs, cots[0], cots[2], part, came, x1_1, vec, after=(m1_far_1,), us=1.5,
    )
    gy1, gqkv_1, keep, *send = run(
        with_scratch(attention_back(1), *attention_back_scratch),
        attention_back_outs, *with_other(gy), qkv_1, probs_1, *att_1, us=9,
    )
    part, came = summed_core(keep, *send)
    (final,) = run(finish_rows, [shape(1, 128, 1024)], x1_1, part_last, came_last, vec)
    output = corner(final)
    to_y, to_x, a1_near_0, a1_near_1, a1_far_0, a1_far_1 = run(
        with_scratch(window_2, out_scratch), grad_outs(512, 128), h1_1, o_1, gy1, gqkv_1,
        m1_near_1, y_1, m1_far_1, x_1, after=(part, output), us=3,
    )
    y_2, x_2 = swap(to_y, "y"), swap(to_x, "x")
    gx, *gy, g1 = run(
        norm_back_stage(8), norm_outs, gm, part, came, x2_0, vec, after=(a1_far_1,), us=1.5
    )
    gy2, gu_0, keep, *send = run(
        mlp_back(0), mlp_back_outs, *with_other(gy), u_0, *mlp_0, us=6
    )
    part, came = summed_core(keep, *send)
    to_y, to_x, m0_near_0, m0_near_1, m0_far_0, m0_far_1, to_zh = run(
        window_3, grad_outs(640, 256) + [row], h2_0, a_0, gy2, gu_0,
        a1_near_1, y_2, a1_far_1, x_2, m1_far_0, x_1, after=(part,), us=4,
    )
    y_3, x_3, m1_far_3 = swap(to_y, "y"), swap(to_x, "x"), swap(to_zh, "zh")
    gm, *gy, e0 = run(
        norm_back_stage(3), norm_outs, gx, part, came, x1_0, vec, after=(m0_far_1,), us=1.5
    )
    gy1, gqkv_0, keep, *send = run(
        with_scratch(attention_back(0), *attention_back_scratch),
        attention_back_outs, *with_other(gy), qkv_0, probs_0, *att_0, us=9,
    )
    to_x, to_y, to_zh = run(
        window_4, [row, row, shape(128, 1024)], m0_near_1, y_3, m0_far_1, x_3, a1_far_0, x_2, after=(keep,)
    )
    x_4, y_4, a1_far_3 = swap(to_x, "x"), swap(to_y, "y"), swap(to_zh, "zh")
    part, came = split_core(keep, *send, after=(to_zh, m1_far_3))
    to_y, to_x, a0_near_0, a0_near_1, a0_far_0, a0_far_1 = run(
        with_scratch(window_5, out_scratch, *vec_scratch), grad_outs(288, 144),
        h1_0, o_0, gy1, gqkv_0, g1, e1, e0, gu_1, gu_0, gqkv_1, keep, *send, *blocks,
        after=(part, x_4, y_4), us=3,
    )
    y_5, x_5 = swap(to_y, "y"), swap(to_x, "x")
    (to_zh,) = run(third_only, [row], m0_far_0, x_3, y_4, after=(a0_far_1,))
    m0_far_3 = swap(to_zh, "zh")
    (grad,) = run(
        with_scratch(
            last_norm_back, *[pltpu.VMEM((128, 1024), F32)] * 3, pltpu.VMEM((128, 1024), BF),
            pltpu.VMEM((8, 1024), F32),
        ),
        [shape(1, 128, 1024)], gm, part, came, blocks[0], vec, after=(to_zh,), us=1.5,
    )
    tokens_grad = corner(grad).astype(F32)
    to_x, to_y = run(second_only, [shape(144, 1024)] * 2, a0_near_1, y_5, a0_far_1, x_5, after=(grad,))
    x_6, y_6 = swap(to_x, "x"), swap(to_y, "y")
    rest = run(
        unpack_first,
        [shape(32, 1792, dtype=F32)] + [shape(32, 1792)] * 3 + [shape(32, 512)] * 2
        + [shape(128, 1024, dtype=F32)],
        y_1, y_2, x_2, x_3, m1_near_0, m1_far_3, a1_near_0, a1_far_3, us=2,
    )
    rest_came = to_partners(rest[1:4])
    (to_zh,) = run(window_6, [shape(144, 1024)], a0_far_0, x_5, y_6, after=rest_came)
    a0_far_3 = swap(to_zh, "zh")
    last = run(
        unpack_last,
        [shape(48, 1792, dtype=F32)] + [shape(48, 1792)] * 3 + [shape(64, 512)] * 2
        + [shape(2, 128, 1024, dtype=F32)],
        y_3, y_5, x_4, x_6, m0_near_0, m0_far_3, a0_near_0, a0_far_3, rest[4], rest[5], rest[6],
        after=rest_came,
    )
    back_a = lax.ppermute(last[4], ("y", "zl"), [(0, 0), (1, 2), (2, 1), (3, 3)])
    back_b = lax.ppermute(last[5], ("y", "zl"), [(0, 1), (1, 3), (2, 0), (3, 2)])
    sizes = (
        (2, 32), (2, 32), (2, 32, 3072), (2, 64), (2, 32, 1024), (2, 32), (2, 32), (2, 32),
        (2, 32, 4096), (2, 128), (2, 32),
    )
    g = run(
        finish, [shape(*s, dtype=F32) for s in sizes],
        rest[0], *rest_came, last[0], *to_partners(last[1:4]), back_a, back_b, us=2,
    )
    return (output, tokens_grad) + tuple(g[:10]) + (last[6], g[10])


def solution(mesh):
    fsdp, ctx = mesh.shape["fsdp"], mesh.shape["ctx"]
    fine = Mesh(mesh.devices.reshape(fsdp // 4, 2, 2, 2, ctx // 2), AXES)
    body = narrow_body if fine.devices.shape == (2, 2, 2, 2, 2) else wide_body
    stream, place = ("y", "x", "core"), ("zh", "zl")
    rows = P(stream, place, None)
    flat, deep = P(None, AXES), P(None, AXES, None)
    params = (flat, flat, deep, flat, deep, flat, flat, flat, deep, flat, deep, flat)
    in_specs = (rows, P(stream, None), P()) + params + (rows,)
    out_specs = (rows, rows) + params
    return jax.shard_map(body, mesh=fine, in_specs=in_specs, out_specs=out_specs, check_vma=False)
```

```python
import jax
import jax.numpy as jnp
from jax import lax
from jax.experimental import pallas as pl
from jax.experimental.pallas import tpu as pltpu
from jax.sharding import Mesh, PartitionSpec as P

HEADS = 16
EPSILON = 1e-05
BF = jnp.bfloat16
F32 = jnp.float32
AXES = ("y", "x", "core", "zh", "zl")


def here(axis):
    return lax.axis_index(axis)


def swap(value, axis):
    return lax.ppermute(value, axis, [(0, 1), (1, 0)])


def ordered(mine, other, axis):
    first = here(axis) == 0
    return jnp.stack([jnp.where(first, mine, other), jnp.where(first, other, mine)])


def pick(value, axis):
    return lax.dynamic_index_in_dim(value, here(axis), 0, keepdims=False)


def pick_other(value, axis):
    return lax.dynamic_index_in_dim(value, 1 - here(axis), 0, keepdims=False)


def trade(value, axis):
    if lax.axis_size(axis) == 2:
        return ordered(pick(value, axis), swap(pick_other(value, axis), axis), axis)
    return lax.all_to_all(value, axis, 0, 0, tiled=True)


def collect(value, axis):
    if lax.axis_size(axis) == 2:
        return ordered(value, swap(value, axis), axis)
    return lax.all_gather(value, axis, axis=0, tiled=False)


def reduce_to(value, axis):
    if lax.axis_size(axis) == 2:
        return pick(value, axis) + swap(pick_other(value, axis), axis)
    return lax.psum_scatter(value, axis, scatter_dimension=0, tiled=False)


def flipped(value, axis, dim):
    return jnp.where(here(axis) == 0, value, jnp.flip(value, dim))


def gather_shards(shard):
    if lax.axis_size("y") != 2:
        return lax.all_gather(shard, ("y", "x", "zh"), axis=0, tiled=False)
    far = swap(shard, "zh")
    near_x = swap(shard, "x")
    far_y = swap(far, "y")
    near_y = swap(shard, "y")
    near_xy = swap(near_x, "y")
    far_x = swap(far, "x")
    far_yx = swap(far_y, "x")
    rel = jnp.stack([shard, far, near_x, far_x, near_y, far_y, near_xy, far_yx])
    rel = rel.reshape((2, 2, 2) + shard.shape)
    rel = flipped(flipped(flipped(rel, "y", 0), "x", 1), "zh", 2)
    return rel.reshape((8,) + shard.shape)


def scatter_shards(grads):
    shape = grads.shape[1:]
    if lax.axis_size("y") != 2:
        return lax.psum_scatter(
            grads, ("y", "x", "zh"), scatter_dimension=0, tiled=False
        )
    rel = grads.reshape((2, 2, 2) + shape)
    rel = flipped(flipped(flipped(rel, "y", 0), "x", 1), "zh", 2)
    near, far = rel[:, :, 0], rel[:, :, 1]
    far = far[:, 0] + swap(far[:, 1].astype(BF), "x").astype(F32)
    near = near[0] + swap(near[1].astype(BF), "y").astype(F32)
    far = far[0] + swap(far[1].astype(BF), "y").astype(F32)
    near = near[0] + swap(near[1].astype(BF), "x").astype(F32)
    return near + swap(far.astype(BF), "zh").astype(F32)


def corner_turn(value):
    return lax.ppermute(value, ("core", "zh"), [(0, 0), (1, 2), (2, 1), (3, 3)])


def norm_rows(values, gain, shift):
    row_mean = jnp.mean(values, axis=-1, keepdims=True)
    centred = values - row_mean
    row_var = jnp.mean(centred * centred, axis=-1, keepdims=True)
    return centred * lax.rsqrt(row_var + EPSILON) * gain + shift


def gelu_tanh(values):
    return jax.nn.gelu(values, approximate=True)


def dot(left, right):
    return jnp.dot(left, right, preferred_element_type=F32)


def dot_t(left, matrix):
    return lax.dot_general(
        left, matrix, (((1,), (1,)), ((), ())), preferred_element_type=F32
    )


def outer_sum(left, right):
    return jnp.einsum("td,te->de", left, right, preferred_element_type=F32)


def wide_body(
    tokens,
    segment_ids,
    group_order,
    ln1_gain,
    ln1_bias,
    qkv_weight,
    qv_bias,
    out_weight,
    out_bias,
    ln2_gain,
    ln2_bias,
    up_weight,
    up_bias,
    down_weight,
    down_bias,
    cotangent,
):
    ny, nx, nc, nzh, nzl = (lax.axis_size(a) for a in AXES)
    chips = ny * nx
    span = chips // nzl
    layers, width = ln1_gain.shape[0], tokens.shape[2]
    hidden = up_weight.shape[2]
    group = tokens.shape[1]
    ctx_count = nzh * nzl
    rank_width = width // (nc * nzl)
    rank_hidden = hidden // (nc * nzl)
    head_size = width // HEADS
    rank_heads = rank_width // head_size
    quarter = width // (chips * nc)
    unit = width // (chips * nc * nzh)
    core_rows = nzl * group
    rows = nc * core_rows
    scale = head_size ** (-0.5)

    def inner(value):
        shape = value.shape
        value = value.reshape(shape[:-1] + (chips, 2, 2, unit))
        return jnp.swapaxes(value, -3, -2).reshape(shape)

    small = (ln1_gain, ln1_bias, out_bias, ln2_gain, ln2_bias, down_bias)
    small_all = small + (qv_bias, up_bias)
    packed = jnp.concatenate([v.reshape(-1) for v in small_all])
    for axis in reversed(AXES):
        packed = collect(packed, axis)
    vectors = []
    at = 0
    for v in small_all:
        size = v.shape[0] * v.shape[1]
        part = packed[..., at : at + size].reshape((ny, nx, nc, nzh, nzl) + v.shape)
        part = jnp.moveaxis(part, 5, 0)
        vectors.append(part.reshape(layers, -1).astype(F32))
        at += size
    vec = [inner(v) for v in vectors[:6]]
    full_qv, full_up = vectors[6], vectors[7]

    def rank_columns(value):
        shape = value.shape[:-1]
        value = value.reshape(shape + (nzl, span, nc, quarter))
        value = lax.dynamic_index_in_dim(value, here("zl"), len(shape), keepdims=False)
        value = lax.dynamic_index_in_dim(value, here("core"), len(shape) + 1, keepdims=False)
        return value.reshape(shape + (rank_width,))

    q_bias = rank_columns(full_qv[:, :width])
    v_bias = rank_columns(full_qv[:, width:])
    qkv_bias = jnp.concatenate([q_bias, jnp.zeros_like(q_bias), v_bias], axis=1)
    up_b = full_up.reshape(layers, chips, nc, nzh, nzl, -1)
    up_b = lax.dynamic_index_in_dim(up_b, here("zl"), 4, keepdims=False)
    up_b = lax.dynamic_index_in_dim(up_b, here("core"), 2, keepdims=False)
    up_b = up_b.reshape(layers, rank_hidden)

    def to_ranks(value):
        value = trade(value, "core")
        return jnp.swapaxes(trade(jnp.swapaxes(value, 0, 1), "zl"), 0, 1)

    def fetch(layer):
        w = qkv_weight[layer]
        n = w.shape[0]
        w = w.reshape(n, 3, nzl, span, nc, quarter)
        w = jnp.transpose(w, (4, 2, 0, 1, 3, 5)).reshape(nc, nzl, n, 3 * rank_width)
        w_qkv = gather_shards(to_ranks(w).reshape(-1, 3 * rank_width))
        w = gather_shards(inner(out_weight[layer]))
        w = trade(w.reshape(nzl, span, nzh, n, width), "zl")
        w_out = jnp.transpose(w, (1, 2, 0, 3, 4)).reshape(rank_width, width)
        w = up_weight[layer].reshape(n, chips, nc, nzh, nzl, -1)
        w = jnp.transpose(w, (2, 4, 0, 1, 3, 5)).reshape(nc, nzl, n, rank_hidden)
        w_up = gather_shards(to_ranks(w).reshape(-1, rank_hidden))
        w_down = gather_shards(inner(down_weight[layer]))
        return (
            w_qkv.reshape(width, 3 * rank_width),
            w_out,
            w_up.reshape(width, rank_hidden),
            w_down.reshape(rank_hidden, width),
        )

    def from_ranks(value):
        value = jnp.swapaxes(trade(jnp.swapaxes(value, 0, 1), "zl"), 0, 1)
        return trade(value, "core")

    def send(grads):
        g_qkv, g_out, g_up, g_down = grads
        n = width // (chips * 2 * ctx_count)
        g = scatter_shards(g_qkv.reshape(chips * nzh, -1, 3 * rank_width))
        g = from_ranks(g.astype(BF).reshape(nc, nzl, n, 3 * rank_width)).astype(F32)
        g = g.reshape(nc, nzl, n, 3, span, quarter)
        d_qkv = jnp.transpose(g, (2, 3, 1, 4, 0, 5)).reshape(n, 3 * width)
        g = g_out.astype(BF).reshape(span, nzh, nzl, n, width)
        g = trade(jnp.transpose(g, (2, 0, 1, 3, 4)), "zl").astype(F32)
        d_out = inner(scatter_shards(g.reshape(chips * nzh, n, width)))
        g = scatter_shards(g_up.reshape(chips * nzh, -1, rank_hidden))
        g = from_ranks(g.astype(BF).reshape(nc, nzl, n, rank_hidden)).astype(F32)
        g = g.reshape(nc, nzl, n, chips, nzh, -1)
        d_up = jnp.transpose(g, (2, 3, 0, 4, 1, 5)).reshape(n, hidden)
        d_down = inner(scatter_shards(g_down.reshape(chips * nzh, -1, width)))
        return d_qkv, d_out, d_up, d_down

    def own_columns(value, mine):
        value = inner(value).reshape(ny, nx, nc, nzh, nzl, -1)
        keep = jnp.arange(nzl)[:, None] == here("zl")
        return jnp.where(keep, value, 0.0)

    def send_small(sums):
        g1, b1, gqv, bo, g2, b2, bu, bd = sums
        parts = [own_columns(v, None) for v in (g1, b1, bo, g2, b2, bd)]

        def placed(value):
            value = value.reshape(1, span, 1, quarter)
            keep = (jnp.arange(nzl)[:, None, None, None] == here("zl")) & (
                jnp.arange(nc)[None, None, :, None] == here("core")
            )
            return jnp.where(keep, value, 0.0).reshape(width)

        qv = jnp.concatenate([placed(gqv[0]), placed(gqv[1])])
        parts.append(qv.reshape(ny, nx, nc, nzh, nzl, -1))
        up = bu.reshape(ny, nx, 1, nzh, 1, -1)
        keep = (jnp.arange(nzl)[:, None] == here("zl")) & (
            jnp.arange(nc)[:, None, None, None] == here("core")
        )
        parts.append(jnp.where(keep, up, 0.0))
        value = jnp.concatenate(parts, axis=-1)
        for axis in AXES:
            value = reduce_to(value, axis)
        sizes = [p.shape[-1] for p in parts]
        cut, at = [], 0
        for s in sizes:
            cut.append(value[at : at + s])
            at += s
        g1, b1, bo, g2, b2, bd, qv, up = cut
        return g1, b1, qv, bo, g2, b2, up, bd

    def place(value):
        return collect(inner(corner_turn(value)), "zl").reshape(core_rows, width)

    def both_cores(value):
        return collect(value, "core").reshape(rows, -1)

    def total(partial):
        part = partial.reshape(nc, core_rows, width)
        part = pick(part, "core") + swap(pick_other(part, "core").astype(BF), "core").astype(F32)
        if nzl == 2:
            return part + swap(part.astype(BF), "zl").astype(F32)
        return lax.psum(part, "zl")

    seg = collect(segment_ids[0], "core")
    seg = lax.dynamic_index_in_dim(seg, here("zh"), 0, keepdims=False)
    half = group // 2
    block = jnp.stack([group_order, 2 * ctx_count - 1 - group_order], axis=1)
    pos = (block[:, :, None] * half + jnp.arange(half, dtype=jnp.int32)).reshape(rows)
    row_seg = jnp.take(seg, pos)
    distance = pos[:, None] - pos[None, :]
    allowed = (distance >= 0) & (row_seg[:, None] == row_seg[None, :])
    distance = distance.astype(F32)
    head_no = jnp.arange(rank_heads)
    head_no = (
        (here("zl") * span + head_no // (quarter // head_size)) * nc + here("core")
    ) * (quarter // head_size) + head_no % (quarter // head_size)
    slopes = jnp.exp2(-8.0 * (head_no.astype(F32) + 1.0) / HEADS)

    def scores_of(q, k):
        s = jnp.einsum("qhd,khd->hqk", q, k, preferred_element_type=F32) * scale
        return s - slopes[:, None, None] * distance[None]

    def split(qkv):
        return [
            v.reshape(rows, rank_heads, head_size) for v in jnp.split(qkv, 3, axis=1)
        ]

    weights = [fetch(layer) for layer in range(layers)]
    x = place(tokens[0]).astype(F32)
    kept = []
    for layer in range(layers):
        w_qkv, w_out, w_up, w_down = weights[layer]
        g1, b1, bo, g2, b2, bd = (v[layer] for v in vec)
        h1 = both_cores(norm_rows(x, g1, b1).astype(BF))
        qkv = (dot(h1, w_qkv) + qkv_bias[layer]).astype(BF)
        q, k, v = split(qkv)
        s = jnp.where(allowed, scores_of(q, k), -1e30)
        top = jnp.max(s, axis=-1, keepdims=True)
        p = jnp.where(allowed, jnp.exp(s - top), 0.0)
        den = jnp.sum(p, axis=-1, keepdims=True)
        p = p / den
        o = jnp.einsum("hqk,khd->qhd", p.astype(BF), v, preferred_element_type=F32)
        log_total = top + jnp.log(den)
        o = o.reshape(rows, rank_width).astype(BF)
        x1 = x + total(dot(o, w_out)) + bo
        h2 = both_cores(norm_rows(x1, g2, b2).astype(BF))
        u = dot(h2, w_up) + up_b[layer]
        a = gelu_tanh(u).astype(BF)
        x2 = x1 + total(dot(a, w_down)) + bd
        kept.append((x, h1, qkv, log_total, o, x1, h2, u, a))
        x = x2

    def leave(value):
        mine = lax.dynamic_index_in_dim(
            value.reshape(nzl, group, width), here("zl"), 0, keepdims=False
        )
        return corner_turn(inner(mine))[None]

    final_rows = leave(x.astype(BF))

    gx = place(cotangent[0]).astype(F32)
    result = [None] * layers
    for layer in reversed(range(layers)):
        w_qkv, w_out, w_up, w_down = weights[layer]
        g1, b1, bo, g2, b2, bd = (v[layer] for v in vec)
        x, h1, qkv, log_total, o, x1, h2, u, a = kept[layer]
        gy2_mine = gx.astype(BF)
        gy2 = both_cores(gy2_mine)
        d_down = outer_sum(a, gy2)
        d_bd = jnp.sum(gy2_mine.astype(F32), axis=0)
        _, gelu_back = jax.vjp(gelu_tanh, u)
        gu = gelu_back(dot_t(gy2, w_down))[0].astype(BF)
        d_up = outer_sum(h2, gu)
        d_bu = jnp.sum(gu.astype(F32), axis=0)
        _, back = jax.vjp(norm_rows, x1, g2, b2)
        gn, d_g2, d_b2 = back(total(dot_t(gu, w_up)))
        gm = gx + gn
        gy1_mine = gm.astype(BF)
        gy1 = both_cores(gy1_mine)
        d_out = outer_sum(o, gy1)
        d_bo = jnp.sum(gy1_mine.astype(F32), axis=0)
        go_f = dot_t(gy1, w_out)
        go = go_f.astype(BF).reshape(rows, rank_heads, head_size)
        q, k, v = split(qkv)
        p = jnp.where(allowed, jnp.exp(scores_of(q, k) - log_total), 0.0)
        dp = jnp.einsum("qhd,khd->hqk", go, v, preferred_element_type=F32)
        ds = (p * (dp - jnp.sum(dp * p, axis=-1, keepdims=True))).astype(BF)
        gq = scale * jnp.einsum("hqk,khd->qhd", ds, k, preferred_element_type=F32)
        gk = scale * jnp.einsum("hqk,qhd->khd", ds, q, preferred_element_type=F32)
        gv = jnp.einsum("hqk,qhd->khd", p.astype(BF), go, preferred_element_type=F32)
        gqkv = jnp.concatenate(
            [g.reshape(rows, rank_width) for g in (gq, gk, gv)], axis=1
        ).astype(BF)
        d_qkv = outer_sum(h1, gqkv)
        sums = jnp.sum(gqkv.astype(F32), axis=0)
        _, back = jax.vjp(norm_rows, x, g1, b1)
        gn, d_g1, d_b1 = back(total(dot_t(gqkv, w_qkv)))
        gx = gm + gn
        d_qv = (sums[:rank_width], sums[2 * rank_width :])
        big = send((d_qkv, d_out, d_up, d_down))
        tiny = send_small((d_g1, d_b1, d_qv, d_bo, d_g2, d_b2, d_bu, d_bd))
        result[layer] = (
            tiny[0], tiny[1], big[0], tiny[2], big[1], tiny[3],
            tiny[4], tiny[5], big[2], tiny[6], big[3], tiny[7],
        )
    stacked = [jnp.stack([result[layer][i] for layer in range(layers)]) for i in range(12)]
    return (final_rows, leave(gx)) + tuple(stacked)


def bit(axis, flip):
    place = lax.axis_index(axis)
    return 1 - place if flip else place


def slot_places():
    for slot in range(8):
        yield slot, bit("y", slot & 4), bit("x", slot & 2), bit("zh", slot & 1)


class View:
    def __init__(self, ref, row):
        self.ref, self.row = ref, row

    def _spot(self, spot):
        rows, columns = spot if isinstance(spot, tuple) else (spot, slice(None))
        if isinstance(rows, slice):
            return slice(rows.start + self.row, rows.stop + self.row), columns
        return pl.ds(rows.start + self.row, rows.size), columns

    def __getitem__(self, spot):
        return self.ref[self._spot(spot)]

    def __setitem__(self, spot, value):
        self.ref[self._spot(spot)] = value


class Rows:
    def __init__(self, refs):
        self.refs, self.size = refs, refs[0].shape[0]

    def _span(self, spot):
        rows = spot[0] if isinstance(spot, tuple) else spot
        if rows is Ellipsis:
            return 0, len(self.refs)
        return rows.start // self.size, rows.stop // self.size

    def __getitem__(self, spot):
        first, last = self._span(spot)
        return jnp.concatenate([r[...] for r in self.refs[first:last]], axis=0)

    def __setitem__(self, spot, value):
        first, last = self._span(spot)
        for i in range(first, last):
            self.refs[i][...] = value[(i - first) * self.size : (i - first + 1) * self.size]

    def block(self, which):
        low, high = self[slice(0, 128), :], self[slice(128, 256), :]
        return jnp.where(which == 0, low, high)


class Joined:
    def __init__(self, low, high, cut):
        self.low, self.high, self.cut = low, high, cut

    def __getitem__(self, spot):
        rows, columns = spot
        parts = []
        if rows.start < self.cut:
            parts.append(self.low[rows.start : min(rows.stop, self.cut), columns])
        if rows.stop > self.cut:
            parts.append(self.high[max(rows.start, self.cut) - self.cut : rows.stop - self.cut, columns])
        return parts[0] if len(parts) == 1 else jnp.concatenate(parts, axis=0)


def eight_slots(own, far, near_x, near_y, by_x, by_y, both, rows):
    cut = 128 if rows == 256 else 64
    across = Joined(View(by_y, rows), View(by_x, rows), cut)
    return own, far, near_x, by_x, near_y, by_y, across, both


def att_0_slots(refs):
    return eight_slots(*refs, 144)


def mlp_0_slots(refs):
    own, far_up, far_down, *refs = refs
    return eight_slots(own, Joined(far_up, far_down, 128), *refs, 256)


def att_1_slots(refs):
    own, far, by_x_1, by_y_1, by_x, by_y, both = refs
    return eight_slots(own, View(far, 0), View(by_x_1, 256), View(by_y_1, 256), by_x, by_y, both, 128)


def mlp_1_slots(refs):
    own, own_down, far, far_down, near_x, near_y, by_x, by_y, across_x, across_y, both = refs
    own, far = Joined(View(own, 128), own_down, 128), Joined(View(far, 128), far_down, 128)
    across = Joined(across_y, across_x, 128)
    return own, far, near_x, by_x, near_y, by_y, across, both


def second_message(far, near_x, near_y, to_x, to_y, rows):
    cut = 128 if rows == 256 else 64
    to_x[0:rows, :] = far[0:rows, :]
    to_y[0:rows, :] = far[0:rows, :]
    to_y[rows : rows + cut, :] = near_x[0:cut, :]
    to_x[rows : 2 * rows - cut, :] = near_y[cut:rows, :]


def att_0_message(far, near_x, near_y, to_x, to_y):
    second_message(far, near_x, near_y, to_x, to_y, 144)


def mlp_0_message(far_up, far_down, near_x, near_y, to_x, to_y, to_both):
    far = Joined(far_up, far_down, 128)
    to_both[...] = far[0:256, :]
    second_message(far, near_x, near_y, to_x, to_y, 256)


def att_1_message(far, near_x, near_y, own, own_down, to_x, to_y, to_both, mine):
    to_both[...] = far[0:128, :]
    second_message(far, View(near_x, 256), View(near_y, 256), to_x, to_y, 128)
    mine[0:128, :] = own[128:256, :]
    mine[128:256, :] = own_down[...]


def mlp_1_message(far, far_down, to_all):
    to_all[...] = Joined(View(far, 128), far_down, 128)[0:256, :]


def mlp_1_across(near_x, near_y, to_x, to_y):
    to_y[...] = near_x[0:128, :]
    to_x[...] = near_y[128:256, :]


def slot_blocks():
    return [(r, (y * 2 + x) * 2 + zh) for r, y, x, zh in slot_places()]


def at(block, size):
    return pl.ds(pl.multiple_of(block * size, size), size)


def run(kernel, outs, *ins, after=(), us=1.0, anywhere=False, limit=16):
    smem = pl.BlockSpec(memory_space=pltpu.SMEM)
    vmem = pl.BlockSpec(memory_space=pltpu.VMEM)
    free = pl.BlockSpec(memory_space=pl.ANY)
    skip = len(after)

    def body(*refs):
        kernel(*refs[skip:])

    return pl.pallas_call(
        body,
        out_shape=tuple(outs),
        in_specs=[free] * skip
        + [smem if v.size == 4 else free if anywhere else vmem for v in ins],
        out_specs=tuple(vmem for _ in outs),
        scratch_shapes=getattr(kernel, "scratch", []),
        compiler_params=pltpu.CompilerParams(vmem_limit_bytes=limit << 20),
        cost_estimate=pl.CostEstimate(flops=int(us * 1e7), bytes_accessed=0, transcendentals=0),
    )(*after, *ins)


def gate(after, *values):
    skip = len(after)

    def body(*refs):
        refs[-1][...] = jnp.zeros_like(refs[-1])

    free = pl.BlockSpec(memory_space=pl.ANY)
    return pl.pallas_call(
        body,
        out_shape=tuple(shape(*v.shape, dtype=v.dtype) for v in values) + (shape(8, 128, dtype=F32),),
        in_specs=[free] * (skip + len(values)),
        out_specs=tuple(free for _ in values) + (pl.BlockSpec(memory_space=pltpu.VMEM),),
        input_output_aliases={skip + i: i for i in range(len(values))},
        compiler_params=pltpu.CompilerParams(vmem_limit_bytes=16 << 20),
        cost_estimate=pl.CostEstimate(flops=10**4, bytes_accessed=0, transcendentals=0),
    )(*after, *values)


def shape(*sizes, dtype=BF):
    return jax.ShapeDtypeStruct(sizes, dtype)


def with_scratch(kernel, *scratch):
    kernel.scratch = list(scratch)
    return kernel


def inner_columns(value):
    low = lax.broadcasted_iota(jnp.int32, (value.shape[0], 128), 1) < 64
    parts = []
    for i in range(0, value.shape[1], 256):
        a, b = value[:, i : i + 128], value[:, i + 128 : i + 256]
        parts.append(jnp.where(low, a, pltpu.roll(b, 64, 1)))
        parts.append(jnp.where(low, pltpu.roll(a, 64, 1), b))
    return jnp.concatenate(parts, axis=1)


def spread(value):
    n = value.shape[1]
    if n == 128:
        return value.astype(F32)
    hit = lax.broadcasted_iota(jnp.int32, (n, 128), 1) % n == lax.broadcasted_iota(
        jnp.int32, (n, 128), 0
    )
    return dot(value.astype(F32), hit.astype(F32))


RANKS = ((0, 0), (1, 0), (0, 1), (1, 1))


def qkv_blocks(core, zl):
    return [
        (s * 8 + zl * 4 + x * 2 + core, s * 2 + x) for s in range(3) for x in range(2)
    ]


def up_blocks(core, zl):
    return [
        (chip * 8 + core * 4 + zh * 2 + zl, chip * 2 + zh)
        for chip in range(4)
        for zh in range(2)
    ]


def fetch(sources, held, sems):
    copies = [pltpu.make_async_copy(*pair, sems.at[i]) for i, pair in enumerate(zip(sources, held))]
    for copy in copies:
        copy.start()
    for copy in copies:
        copy.wait()


def prepare_first(*refs):
    sources, refs = refs[:11], refs[11:]
    first, (out_a, out_b, down), (held, sems) = refs[0:4], refs[4:7], (refs[7:18], refs[18])
    fetch(sources[:9] + (sources[9].at[0], sources[10].at[0]), held, sems)
    rows = [spread(v[...]) for v in held[:8]]
    w_out, w_qkv, w_down = held[8:]
    small = jnp.concatenate([v[l : l + 1] for l in range(2) for v in rows], axis=0)
    for i, (dc, dl) in enumerate(RANKS):
        for src, dst in qkv_blocks(bit("core", dc), bit("zl", dl)):
            first[i][0:32, dst * 128 : dst * 128 + 128] = w_qkv[:, at(src, 128)]
        first[i][32:48, 0:128] = small.astype(BF)
        first[i][32:48, 128:768] = jnp.zeros((16, 640), BF)
    low_zl = lax.axis_index("zl") == 0
    for l in range(2):
        w = inner_columns(w_out[l].astype(F32)).astype(BF)
        out_a[l * 32 : l * 32 + 32] = jnp.where(low_zl, w[:, :512], w[:, 512:])
        out_b[l * 32 : l * 32 + 32] = jnp.where(low_zl, w[:, 512:], w[:, :512])
    down[...] = inner_columns(w_down[...].astype(F32)).astype(BF)


def prepare_rest(*refs):
    sources, refs = refs[:4], refs[4:]
    rest, (down, cot), (held, sems) = refs[0:4], refs[4:6], (refs[6:10], refs[10])
    fetch((sources[0].at[1], sources[1], sources[2].at[1], sources[3].at[0]), held, sems)
    w_qkv, w_up, w_down, cot_in = held
    for i, (dc, dl) in enumerate(RANKS):
        core, zl = bit("core", dc), bit("zl", dl)
        for src, dst in qkv_blocks(core, zl):
            rest[i][:, 1024 + dst * 128 : 1152 + dst * 128] = w_qkv[:, at(src, 128)]
        for src, dst in up_blocks(core, zl):
            rest[i][:, dst * 128 : dst * 128 + 128] = w_up[0, :, at(src, 128)]
            rest[i][:, 1792 + dst * 128 : 1920 + dst * 128] = w_up[1, :, at(src, 128)]
    down[...] = inner_columns(w_down[...].astype(F32)).astype(BF)
    cot[...] = inner_columns(cot_in[...].astype(F32)).astype(BF)


def put_out(piece, layer, out_a, out_b):
    for ref, flip in ((out_a, 0), (out_b, 1)):
        zl_from = bit("y", flip)
        for h in range(2):
            piece[pl.ds(pl.multiple_of(h * 64 + zl_from * 32, 32), 32), 768:1024] = ref[
                layer * 32 : layer * 32 + 32, h * 256 : h * 256 + 256
            ]


def pack_first(m0, m1, m2, m3, out_a, out_b, piece):
    lane = lax.broadcasted_iota(jnp.int32, (16, 128), 1)
    kind = lax.broadcasted_iota(jnp.int32, (16, 128), 0) % 8
    one = jnp.zeros((16, 128), F32)
    two = jnp.zeros((16, 128), F32)
    for i, m in enumerate((m0, m1, m2, m3)):
        core, zl = bit("core", RANKS[i][0]), bit("zl", RANKS[i][1])
        piece[at(core * 2 + zl, 32), 0:768] = m[0:32, :]
        s = m[32:48, 0:128].astype(F32)
        mine = (kind < 6) & (lane // 32 == core * 2 + zl)
        pair = (kind == 6) & (lane // 64 == zl)
        if i == 0:
            mine = mine | (kind == 7)
        one = one + jnp.where(mine | (pair & (core == 0)), s, 0.0)
        two = two + jnp.where(pair & (core == 1), s, 0.0)
    put_out(piece, 0, out_a, out_b)
    piece[128:144, 0:128] = one.astype(BF)
    piece[128:144, 128:256] = two.astype(BF)
    piece[128:144, 256:1024] = jnp.zeros((16, 768), BF)


def pack_rest(m0, m1, m2, m3, out_a, out_b, down_0, mlp_0, up_0, deep, pair):
    for i, m in enumerate((m0, m1, m2, m3)):
        spot = at(bit("core", RANKS[i][0]) * 2 + bit("zl", RANKS[i][1]), 32)
        up_0[spot, :] = m[:, 0:1024]
        deep[spot, 0:768] = m[:, 1024:1792]
        deep[at(4 + bit("core", RANKS[i][0]) * 2 + bit("zl", RANKS[i][1]), 32), :] = m[:, 1792:2816]
    put_out(deep, 1, out_a, out_b)
    mlp_0[0:128, :] = up_0[...]
    mlp_0[128:256, :] = down_0[...]
    pair[0:256, :] = mlp_0[...]
    pair[256:384, :] = deep[0:128, :]


def both_ways(value):
    return lax.ppermute(value, ("y", "x"), [(0, 3), (3, 0), (1, 2), (2, 1)])


def first_hops(piece):
    return swap(piece, "zh"), swap(piece, "x"), swap(piece, "y")


def load_rows(pieces, scratch, row, columns):
    for r, block in slot_blocks():
        scratch[at(block, 128), :] = pieces[r][row : row + 128, 0:columns]


def load_out(pieces, scratch):
    for r, y, x, zh in slot_places():
        for h in range(2):
            scratch[at(x * 2 + zh, 64), at(y * 2 + h, 256)] = pieces[r][
                h * 64 : h * 64 + 64, 768:1024
            ]


def normal(x):
    centred = x - jnp.mean(x, axis=-1, keepdims=True)
    inv = lax.rsqrt(jnp.mean(centred * centred, axis=-1, keepdims=True) + EPSILON)
    return centred * inv, inv


def load_stream(blocks, scratch):
    for i, (dc, dl) in enumerate(RANKS):
        spot = at(bit("core", dc) * 2 + bit("zl", dl), 128)
        scratch[spot, :] = inner_columns(blocks[i][0].astype(F32)).astype(scratch.dtype)


def load_blocks(blocks, scratch):
    for i, (dc, dl) in enumerate(RANKS):
        scratch[at(bit("core", dc) * 2 + bit("zl", dl), 128), :] = blocks[i][...]


def load_cores(mine, other, scratch):
    scratch[at(bit("core", 0), 256), :] = Rows(mine)[...]
    scratch[at(bit("core", 1), 256), :] = Rows(other)[...]


def split_product(left, right, keep, send):
    mine, other = at(bit("core", 0), 256), at(bit("core", 1), 256)
    Rows(send)[...] = right(left[other, :]).astype(BF)
    keep[...] = right(left[mine, :])


def row_positions(order, dim):
    shape_ = (512, 1) if dim == 0 else (1, 512)
    row = lax.broadcasted_iota(jnp.int32, shape_, dim)
    start = jnp.zeros(shape_, jnp.int32)
    for c in range(4):
        lead = order[c]
        start = jnp.where(row // 64 == 2 * c, lead, start)
        start = jnp.where(row // 64 == 2 * c + 1, 7 - lead, start)
    return start * 64 + row % 64


def masked_distance(seg_a, seg_b, order, dist):
    same = lax.axis_index("core") == lax.axis_index("zh")
    seg = jnp.where(same, seg_a[...], seg_b[...])
    ends = [jnp.sum((seg < d).astype(jnp.int32), axis=1, keepdims=True) for d in (1, 2)]

    def doc(pos):
        return (pos >= ends[0]).astype(jnp.int32) + (pos >= ends[1]).astype(jnp.int32)

    rows, cols = row_positions(order, 0), row_positions(order, 1)
    gap = rows - cols
    fine = (gap >= 0) & (doc(rows) == doc(cols))
    dist[...] = jnp.where(fine, gap.astype(F32), 1e32)


def slope_of(pair, half):
    core, zl = lax.axis_index("core"), lax.axis_index("zl")
    value = jnp.float32(0.0)
    for c in range(2):
        for z in range(2):
            head = 8 * z + 4 * pair + 2 * c + half
            value = jnp.where((core == c) & (zl == z), jnp.float32(2.0 ** (-8.0 * (head + 1) / HEADS)), value)
    return value


def attend(qkv, dist, probs, o):
    low = lax.broadcasted_iota(jnp.int32, (512, 128), 1) < 64

    def heads(pair, carry):
        q = qkv[:, at(pair, 128)]
        k = qkv[:, at(2 + pair, 128)]
        v = qkv[:, at(4 + pair, 128)]
        found = []
        for half in range(2):
            qh = jnp.where(low == (half == 0), q, jnp.zeros_like(q))
            slope = jnp.where(pair == 0, slope_of(0, half), slope_of(1, half))
            s = dot_t(qh, k) * 0.125 - slope * dist[...]
            p = jnp.exp(s - jnp.max(s, axis=1, keepdims=True))
            p = (p / jnp.sum(p, axis=1, keepdims=True)).astype(BF)
            probs[pair * 2 + half] = p
            found.append(dot(p, v))
        o[:, at(pair, 128)] = jnp.where(low, *found).astype(BF)
        return carry

    lax.fori_loop(0, 2, heads, 0)


def attention_part(h1, vec, layer, pieces, seg_a, seg_b, order, outs, scratch):
    qkv, probs, o, keep, *send = outs
    wq, wo, dist = scratch
    load_rows(pieces, wq, 0, 768)
    load_out(pieces, wo)
    masked_distance(seg_a, seg_b, order, dist)
    qkv[...] = (dot(h1[...], wq[...]) + vec[layer * 8 + 6 : layer * 8 + 7, 0:768]).astype(BF)
    attend(qkv, dist, probs, o)
    split_product(o, lambda rows: dot(rows, wo[...]), keep, send)


def first_attention(t0, t1, t2, t3, *refs):
    pieces, (seg_a, seg_b, order), refs = att_0_slots(refs[:7]), refs[7:10], refs[10:]
    vec, h1, outs, scratch = refs[0], refs[1], refs[2:8], refs[8:]
    q_one, q_two, scratch = scratch[0], scratch[1], scratch[2:]
    for r, block in slot_blocks():
        vec[:, at(block, 128)] = pieces[r][128:144, 0:128].astype(F32)
        q_two[:, at(block, 128)] = pieces[r][128:144, 128:256].astype(F32)
    q_one[...] = vec[...]
    core, zl = lax.axis_index("core"), lax.axis_index("zl")
    for l in range(2):
        row = slice(l * 8 + 6, l * 8 + 7)
        for base, y in ((0, 0), (512, 1)):
            block = (y * 2 + zl) * 2 + core
            vec[row, base : base + 128] = q_one[row, at(block, 128)]
            vec[row, base + 128 : base + 256] = q_two[row, at(block, 128)]
        vec[row, 256:512] = jnp.zeros((1, 256), F32)
    load_stream((t0, t1, t2, t3), h1)
    for i in range(4):
        spot = slice(i * 128, i * 128 + 128)
        z, _ = normal(h1[spot, :].astype(F32))
        h1[spot, :] = (z * vec[0:1, :] + vec[1:2, :]).astype(BF)
    attention_part(h1, vec, 0, pieces, seg_a, seg_b, order, outs, scratch)


def next_attention(*refs):
    mine, other, refs = refs[:2], refs[2:4], refs[4:]
    pieces, (vec, seg_a, seg_b, order), refs = att_1_slots(refs[:7]), refs[7:11], refs[11:]
    h1, outs, scratch = refs[0], refs[1:7], refs[7:]
    load_cores(mine, other, h1)
    attention_part(h1, vec, 1, pieces, seg_a, seg_b, order, outs, scratch)


def add_parts(keep, *refs):
    came, out = Rows(refs[:2]), refs[2]
    out[...] = (keep[...] + came[...].astype(F32)).astype(BF)


def norm_stage(bias_row, gain_row):
    def kernel(x, part, came, vec, x_out, *h):
        h = Rows(h)
        for i in range(2):
            spot = slice(i * 128, i * 128 + 128)
            v = x[spot, :] + part[spot, :].astype(F32) + came[spot, :].astype(F32)
            v = v + vec[bias_row : bias_row + 1, :]
            x_out[spot, :] = v
            z, _ = normal(v)
            h[spot, :] = (z * vec[gain_row : gain_row + 1] + vec[gain_row + 1 : gain_row + 2]).astype(BF)

    return kernel


def first_norm_stage(t0, t2, part, came, vec, *refs):
    x_out, h, x0 = refs[0], refs[1:3], refs[3]
    x0[at(bit("zl", 0), 128), :] = inner_columns(t0[0].astype(F32))
    x0[at(bit("zl", 1), 128), :] = inner_columns(t2[0].astype(F32))
    norm_stage(2, 3)(x0, part, came, vec, x_out, *h)


def mlp_weights(refs, layer):
    count = 11 if layer else 8
    return (mlp_1_slots if layer else mlp_0_slots)(refs[:count]), refs[count:]


def mlp_stage(layer):
    def kernel(*refs):
        mine, other, refs = refs[:2], refs[2:4], refs[4:]
        pieces, refs = mlp_weights(refs, layer)
        vec, h2, u, a, keep, *send, w = refs
        load_cores(mine, other, h2)
        load_rows(pieces, w, 0, 1024)
        for i in range(4):
            spot = slice(i * 128, i * 128 + 128)
            z = dot(h2[spot, :], w[...]) + vec[layer * 8 + 7 : layer * 8 + 8, :]
            u[spot, :] = z
            a[spot, :] = gelu_tanh(z).astype(BF)
        load_rows(pieces, w, 128, 1024)
        split_product(a, lambda rows: dot(rows, w[...]), keep, send)

    return with_scratch(kernel, pltpu.VMEM((1024, 1024), BF))


def finish_rows(x, part, came, vec, out):
    v = x[at(bit("zl", 0), 128), :] + part[...].astype(F32) + came[...].astype(F32) + vec[13:14, :]
    out[0] = inner_columns(v).astype(BF)


def add_split(keep, *refs):
    came, mine, other = Rows(refs[:2]), refs[2], refs[3]
    for to, flip in ((mine, 0), (other, 1)):
        which = bit("zl", flip)
        to[...] = (keep[at(which, 128), :] + came.block(which).astype(F32)).astype(BF)


def gelu_slope(u):
    c = 0.7978845608028654
    t = jnp.tanh(c * (u + 0.044715 * u * u * u))
    return 0.5 * (1.0 + t) + 0.5 * u * (1.0 - t * t) * (c * (1.0 + 3 * 0.044715 * u * u))


def mlp_back(layer):
    def kernel(*refs):
        if layer == 1:
            blocks, u, refs = refs[:4], refs[4], refs[5:]
        else:
            blocks, u, refs = refs[:4], refs[4], refs[5:]
        pieces, (gy2, gu, keep, *send, w) = mlp_weights(refs, layer)
        load_blocks(blocks, gy2) if layer == 1 else load_cores(blocks[:2], blocks[2:], gy2)
        load_rows(pieces, w, 128, 1024)
        for i in range(4):
            spot = slice(i * 128, i * 128 + 128)
            gu[spot, :] = (dot_t(gy2[spot, :], w[...]) * gelu_slope(u[spot, :])).astype(BF)
        load_rows(pieces, w, 0, 1024)
        split_product(gu, lambda rows: dot_t(rows, w[...]), keep, send)

    return with_scratch(kernel, pltpu.VMEM((1024, 1024), BF))


def turned_dot(left, right):
    return lax.dot_general(left, right, (((0,), (0,)), ((), ())), preferred_element_type=F32)


def slot_spots(rows, to_y, to_x, near_0, near_1, far_0, far_1):
    return (
        near_0, far_0, near_1, View(to_x, 0), View(to_y, 0), far_1, View(to_y, rows), View(to_x, rows),
    )


def mlp_grads(h2, a, gy2, gu, *outs):
    spots = slot_spots(256, *outs)
    for r, block in slot_blocks():
        spots[r][0:128, :] = turned_dot(h2[:, at(block, 128)], gu[...]).astype(BF)
        spots[r][128:256, :] = turned_dot(a[:, at(block, 128)], gy2[...]).astype(BF)


def second_sums(rows, near_1, near, far_1, far, to_x, to_y):
    to_x[0:rows, :] = (near_1[...].astype(F32) + near[0:rows, :].astype(F32)).astype(BF)
    to_y[0:rows, :] = (far_1[...].astype(F32) + far[0:rows, :].astype(F32)).astype(BF)


def third_sum(rows, far_0, far, far_2, out):
    total = far_0[...].astype(F32) + far[0:rows, :].astype(F32) + far_2[0:rows, :].astype(F32)
    out[...] = total.astype(BF)


def norm_back(gx, part, came, x, gain, gm, gy, sums):
    totals = [jnp.zeros((1, x.shape[1]), F32) for _ in range(4)]
    for i in range(part.shape[0] // 128):
        spot = slice(i * 128, i * 128 + 128)
        dh = part[spot, :].astype(F32) + came[spot, :].astype(F32)
        z, inv = normal(x[spot, :])
        dz = dh * gain
        mean_a = jnp.mean(dz, axis=-1, keepdims=True)
        mean_b = jnp.mean(dz * z, axis=-1, keepdims=True)
        up = gx[spot, :]
        g = up + inv * (dz - mean_a - z * mean_b)
        gm[spot, :] = g
        rounded = g.astype(BF)
        gy[spot, :] = rounded
        new = (dh * z, dh, rounded.astype(F32), up.astype(BF).astype(F32))
        totals = [t + jnp.sum(v, axis=0, keepdims=True) for t, v in zip(totals, new)]
    sums[...] = jnp.concatenate(totals + [jnp.zeros((4, x.shape[1]), F32)], axis=0)


def norm_back_stage(gain_row):
    def kernel(gx, part, came, x, vec, gm, *refs):
        norm_back(gx, part, came, x, vec[gain_row : gain_row + 1, :], gm, Rows(refs[:2]), refs[2])

    return kernel


def first_norm_back(c0, c2, part, came, x, vec, gm, *refs):
    gy, sums, gx = Rows(refs[:2]), refs[2], refs[3]
    gx[at(bit("zl", 0), 128), :] = c0[...].astype(F32)
    gx[at(bit("zl", 1), 128), :] = c2[...].astype(F32)
    norm_back(gx, part, came, x, vec[11:12, :], gm, gy, sums)


def last_norm_back(gx, part, came, t0, vec, grad, up, x, gm, gy, sums):
    x[...] = inner_columns(t0[0].astype(F32))
    up[...] = gx[at(bit("zl", 0), 128), :]
    norm_back(up, part, came, x, vec[0:1, :], gm, gy, sums)
    grad[0] = inner_columns(gm[...]).astype(BF)


def attention_back(layer):
    def kernel(*refs):
        mine, other, (qkv, probs), refs = refs[:2], refs[2:4], refs[4:6], refs[6:]
        pieces = (att_1_slots if layer else att_0_slots)(refs[:7])
        attention_back_part(mine, other, qkv, probs, pieces, *refs[7:])

    return kernel


def attention_back_part(mine, other, qkv, probs, pieces, *refs):
    gy1, gqkv, keep, *send, wq, wo, go, gk, gv = refs
    load_cores(mine, other, gy1)
    load_rows(pieces, wq, 0, 768)
    load_out(pieces, wo)
    go[...] = dot_t(gy1[...], wo[...]).astype(BF)
    low = lax.broadcasted_iota(jnp.int32, (512, 128), 1) < 64

    def heads(pair, carry):
        q = qkv[:, at(pair, 128)]
        k = qkv[:, at(2 + pair, 128)]
        v = qkv[:, at(4 + pair, 128)]
        g = go[:, at(pair, 128)]
        found = []
        for half in range(2):
            lanes = low == (half == 0)
            gh = jnp.where(lanes, g, jnp.zeros_like(g))
            p = probs[pair * 2 + half]
            pf = p.astype(F32)
            dp = dot_t(gh, v)
            ds = (pf * (dp - jnp.sum(dp * pf, axis=1, keepdims=True))).astype(BF)
            found.append((dot(ds, k), turned_dot(ds, q), turned_dot(p, g)))
        for part, scale in ((0, 0.125), (1, 0.125), (2, 1.0)):
            value = scale * jnp.where(low, found[0][part], found[1][part])
            gqkv[:, at(part * 2 + pair, 128)] = value.astype(BF)
        return carry

    lax.fori_loop(0, 2, heads, 0)
    split_product(gqkv, lambda rows: dot_t(rows, wq[...]), keep, send)


def attention_grads(rows, h1, o, gy1, gqkv, outs, d_out):
    spots = slot_spots(rows, *outs)
    d_out[...] = turned_dot(o[...], gy1[...]).astype(BF)
    for (r, block), (_, y, x, zh) in zip(slot_blocks(), slot_places()):
        spots[r][0:128, 0:768] = turned_dot(h1[:, at(block, 128)], gqkv[...]).astype(BF)
        for h in range(2):
            spots[r][h * 64 : h * 64 + 64, 768:1024] = d_out[at(x * 2 + zh, 64), at(y * 2 + h, 256)]
    return spots


def window_1(h2, a, gy2, gu, *outs):
    mlp_grads(h2, a, gy2, gu, *outs)


def window_2(h1, o, gy1, gqkv, near_1, y_1, far_1, x_1, to_y, to_x, *rest):
    attention_grads(128, h1, o, gy1, gqkv, (to_y, to_x) + rest[:4], rest[4])
    second_sums(256, near_1, View(y_1, 256), far_1, View(x_1, 256), View(to_x, 256), View(to_y, 256))


def window_3(h2, a, gy2, gu, near_1, y_2, far_1, x_2, far_0, x_1, to_y, to_x, *rest):
    mlp_grads(h2, a, gy2, gu, to_y, to_x, *rest[:4])
    second_sums(128, near_1, View(y_2, 128), far_1, View(x_2, 128), View(to_x, 512), View(to_y, 512))
    third_sum(256, far_0, x_1, View(y_2, 256), rest[4])


def window_4(near_1, y_3, far_1, x_3, far_0, x_2, to_x, to_y, to_zh):
    second_sums(256, near_1, View(y_3, 256), far_1, View(x_3, 256), to_x, to_y)
    third_sum(128, far_0, x_2, View(y_3, 512), to_zh)


def window_5(*refs):
    grads, (to_y, to_x), rest = refs[:17], refs[17:19], refs[19:]
    last_attention_grads(*grads, (to_y, to_x) + rest[:4], *rest[4:])


def second_only(near_1, y, far_1, x, to_x, to_y):
    second_sums(144, near_1, View(y, 144), far_1, View(x, 144), to_x, to_y)


def third_only(far_0, x, y, to_zh):
    third_sum(256, far_0, x, y, to_zh)


def window_6(far_0, x_4, y_5, to_zh):
    third_sum(144, far_0, x_4, y_5, to_zh)


def last_attention_grads(
    h1, o, gy1, gqkv, g1, e1, e0, gu1, gu0, gq1, keep, s0, s1, t0, t1, t2, t3, outs, d_out, ups, wide
):
    spots = attention_grads(144, h1, o, gy1, gqkv, outs, d_out)
    send = Rows((s0, s1))
    none = jnp.zeros((2, 1024), F32)
    gain = jnp.zeros((1, 1024), F32)
    shift = jnp.zeros((1, 1024), F32)
    for i, block in enumerate((t0, t1, t2, t3)):
        dc, dl = RANKS[i]
        z, _ = normal(inner_columns(block[0].astype(F32)))
        which = bit("zl", dl)
        dh = send.block(which).astype(F32) if dc else keep[at(which, 128), :]
        gain = gain + jnp.sum(dh * z, axis=0, keepdims=True)
        shift = shift + jnp.sum(dh, axis=0, keepdims=True)
    parts = [g1[0:2, :], e1[2:3, :], e1[0:2, :], e1[3:4, :], none, gain, shift]
    wide[...] = jnp.concatenate(parts + [e0[2:3, :], e0[0:2, :], e0[3:4, :], none], axis=0)
    sums = [jnp.sum(v[...].astype(F32), axis=0, keepdims=True) for v in (gu1, gu0)]
    ups[...] = jnp.concatenate(sums + [jnp.zeros((14, 1024), F32)], axis=0)
    q = [jnp.sum(v[...].astype(F32), axis=0, keepdims=True) for v in (gq1, gqkv)]
    q = jnp.concatenate(q + [jnp.zeros((14, 768), F32)], axis=0)
    core, zl = lax.axis_index("core"), lax.axis_index("zl")
    for r, block in slot_blocks():
        rows = slice(128, 144)
        spots[r][rows, 0:128] = wide[:, at(block, 128)].astype(BF)
        spots[r][rows, 128:256] = ups[:, at(block, 128)].astype(BF)
        mine = jnp.where(block == 4 + zl * 2 + core, q[:, 512:768], jnp.zeros((16, 256), F32))
        mine = jnp.where(block == zl * 2 + core, q[:, 0:256], mine)
        spots[r][rows, 256:512] = mine.astype(BF)
        spots[r][rows, 512:1024] = jnp.zeros((16, 512), BF)


def summed(parts, rows, columns):
    value = parts[0][rows, columns].astype(F32)
    for part in parts[1:]:
        value = value + part[rows, columns].astype(F32)
    return value


def own_out(parts, flip):
    row = bit("y", flip) * 32
    halves = []
    for h in range(2):
        spot = pl.ds(pl.multiple_of(h * 64 + row, 32), 32)
        halves.append(summed(parts, spot, slice(768, 1024)))
    return jnp.concatenate(halves, axis=1)


def rank_rows(i):
    return at(bit("core", RANKS[i][0]) * 2 + bit("zl", RANKS[i][1]), 32)


def unpack_first(y_1, y_2, x_2, x_3, m_near, m_far, a_near, a_far, mine, *refs):
    mlp = (m_near, y_1, View(x_2, 256), m_far)
    att = (a_near, y_2, View(x_3, 512), a_far)
    sends, a, b, down = refs[0:3], refs[3], refs[4], refs[5]
    for i in range(4):
        to = mine if i == 0 else sends[i - 1]
        for parts, start, width in ((att, 0, 768), (mlp, 768, 1024)):
            value = summed(parts, rank_rows(i), slice(0, width))
            to[:, start : start + width] = value.astype(to.dtype)
    a[...] = own_out(att, 0).astype(BF)
    b[...] = own_out(att, 1).astype(BF)
    down[...] = inner_columns(summed(mlp, slice(128, 256), slice(0, 1024)))


def unpack_last(y_3, y_5, x_4, x_6, m_near, m_far, a_near, a_far, a1, b1, down_1, mine, *refs):
    mlp = (m_near, y_3, x_4, m_far)
    att = (a_near, y_5, x_6, a_far)
    sends, (a, b), down = refs[0:3], refs[3:5], refs[5]
    for i in range(4):
        to = mine if i == 0 else sends[i - 1]
        to[0:32, 0:768] = summed(att, rank_rows(i), slice(0, 768)).astype(to.dtype)
        to[0:32, 768:1792] = summed(mlp, rank_rows(i), slice(0, 1024)).astype(to.dtype)
        to[32:48, 0:768] = summed(att, slice(128, 144), slice(0, 768)).astype(to.dtype)
        to[32:48, 768:1792] = jnp.zeros((16, 1024), to.dtype)
    a[0:32, :] = own_out(att, 0).astype(BF)
    b[0:32, :] = own_out(att, 1).astype(BF)
    a[32:64, :] = a1[...]
    b[32:64, :] = b1[...]
    down[0] = inner_columns(summed(mlp, slice(128, 256), slice(0, 1024)))
    down[1] = down_1[...]


def finish(rest, r1, r2, r3, last, l1, l2, l3, a, b, *outs):
    g1, b1, w_qkv, qv, w_out, bo, g2, b2, w_up, up, bd = outs
    for i, (rm, lm) in enumerate(((rest, last), (r1, l1), (r2, l2), (r3, l3))):
        core, zl = bit("core", RANKS[i][0]), bit("zl", RANKS[i][1])
        for src, dst in qkv_blocks(core, zl):
            w_qkv[0, :, at(src, 128)] = lm[0:32, dst * 128 : dst * 128 + 128].astype(F32)
            w_qkv[1, :, at(src, 128)] = rm[:, dst * 128 : dst * 128 + 128].astype(F32)
        for src, dst in up_blocks(core, zl):
            w_up[0, :, at(src, 128)] = lm[0:32, 768 + dst * 128 : 896 + dst * 128].astype(F32)
            w_up[1, :, at(src, 128)] = rm[:, 768 + dst * 128 : 896 + dst * 128].astype(F32)
    low_zl = lax.axis_index("zl") == 0
    for l in range(2):
        va, vb = a[l * 32 : l * 32 + 32].astype(F32), b[l * 32 : l * 32 + 32].astype(F32)
        w = jnp.concatenate([jnp.where(low_zl, va, vb), jnp.where(low_zl, vb, va)], axis=1)
        w_out[l] = inner_columns(w)
    spot = lax.axis_index("core") * 2 + lax.axis_index("zl")

    def chunk(value, size):
        found = jnp.zeros((value.shape[0], size), F32)
        for j in range(4):
            found = jnp.where(spot == j, value[:, j * size : j * size + size], found)
        return found

    mine, by_core = last[32:48, 0:128], l1[32:48, 0:128].astype(F32)
    wide = chunk(mine + by_core, 32)
    late = l2[32:48, 0:128].astype(F32) + l3[32:48, 0:128].astype(F32)
    late = chunk(mine + by_core + late, 32)
    for row, ref in ((2, bo), (3, g2), (4, b2), (5, bd)):
        ref[...] = jnp.concatenate([wide[row + 8 : row + 9], wide[row : row + 1]], axis=0)
    g1[...] = jnp.concatenate([late[8:9], wide[0:1]], axis=0)
    b1[...] = jnp.concatenate([late[9:10], wide[1:2]], axis=0)
    up[...] = jnp.concatenate([last[33:34, 128:256], last[32:33, 128:256]], axis=0)
    both = last[32:48, 256:512]
    for m in (l1, l2, l3):
        both = both + m[32:48, 256:512].astype(F32)
    both = chunk(both, 64)
    qv[...] = jnp.concatenate([both[1:2], both[0:1]], axis=0)


def corner(value):
    return lax.ppermute(value, ("core", "zh"), [(0, 0), (1, 2), (2, 1), (3, 3)])


def to_partners(messages):
    one, two, three = messages
    return (
        swap(one, "core"),
        swap(two, "zl"),
        lax.ppermute(three, ("core", "zl"), [(0, 3), (3, 0), (1, 2), (2, 1)]),
    )


def narrow_body(
    tokens, segment_ids, group_order, ln1_gain, ln1_bias, qkv_weight, qv_bias, out_weight, out_bias,
    ln2_gain, ln2_bias, up_weight, up_bias, down_weight, down_bias, cotangent,
):
    small = (ln1_gain, ln1_bias, out_bias, ln2_gain, ln2_bias, down_bias, qv_bias, up_bias)

    def held(*values):
        return [pltpu.VMEM(v, BF) for v in values] + [pltpu.SemaphoreType.DMA((len(values),))]

    row, rowf = shape(256, 1024), shape(256, 1024, dtype=F32)
    halves = [shape(128, 1024)] * 2

    ready = run(
        with_scratch(
            prepare_first, *held(*[v.shape for v in small], (2, 32, 1024), (32, 3072), (128, 1024))
        ),
        [shape(48, 768)] * 4 + [shape(64, 512)] * 2 + [shape(128, 1024)],
        *small, out_weight, qkv_weight, down_weight, anywhere=True, limit=60, us=3,
    )
    out_b = lax.ppermute(ready[5], ("y", "zl"), [(0, 2), (1, 0), (2, 3), (3, 1)])
    out_a = lax.ppermute(ready[4], ("y", "zl"), [(0, 0), (1, 2), (2, 1), (3, 3)])
    first = (ready[0],) + to_partners(ready[1:4])
    (att_0,) = run(pack_first, [shape(144, 1024)], *first, out_a, out_b)
    far, near_x, near_y = first_hops(att_0)
    block = corner(tokens)
    rest = run(
        with_scratch(
            prepare_rest, *held((32, 3072), (2, 32, 4096), (128, 1024), (128, 1024))
        ),
        [shape(32, 2816)] * 4 + [shape(128, 1024)] * 2,
        qkv_weight, up_weight, down_weight, cotangent, after=(ready[0],), anywhere=True, us=2,
    )
    cot = rest[5]
    mlp_0, up_0, deep, pair = run(
        pack_rest, [row, shape(128, 1024), row, shape(384, 1024)],
        rest[0], *to_partners(gate((att_0,), *rest[1:4])[:3]), out_a, out_b, ready[6],
    )
    down_1 = rest[4]
    def second_hops(kernel, rows_x, rows_y, *ins, after=(), rows=0):
        outs = [shape(n, 1024) for n in (rows_x, rows_y, rows) if n]
        to = run(kernel, outs, *ins, after=after)
        return swap(to[0], "x"), swap(to[1], "y"), both_ways(to[2] if rows else ins[0]), to[0]

    by_x, by_y, both, sent = second_hops(
        att_0_message, 224, 208, far, near_x, near_y, after=(pair, block)
    )
    att_0 = (att_0, far, near_x, near_y, by_x, by_y, both)
    up_0, down_0, _ = gate((sent,), up_0, ready[6])
    far_up, far_down = swap(up_0, "zh"), swap(down_0, "zh")
    by_zl = swap(block, "zl")
    pair, deep, token = gate((by_x, by_y, both, far_up, by_zl), pair, deep)
    pair_x, pair_y = swap(pair, "x"), swap(pair, "y")
    blocks = (block, swap(block, "core"), by_zl, swap(by_zl, "core"))
    segments = (segment_ids, swap(segment_ids, "core"), group_order)

    def cores(values):
        return [swap(v, "core") for v in values]

    def summed_core(keep, *send, after=()):
        (part,) = run(add_parts, [row], keep, *cores(send), after=after)
        return part, swap(part, "zl")

    def split_core(keep, *send, after=()):
        part, other = run(add_split, [shape(128, 1024)] * 2, keep, *cores(send), after=after)
        return part, swap(other, "zl")

    def with_other(values):
        return (*values, *cores(values))

    attention_outs = [
        shape(512, 1024), shape(512, 768), shape(4, 512, 512), shape(512, 256), rowf, *halves,
    ]
    weights_scratch = [pltpu.VMEM((1024, 768), BF), pltpu.VMEM((256, 1024), BF)]
    dist = pltpu.VMEM((512, 512), F32)
    vec_scratch = [pltpu.VMEM((16, 1024), F32)] * 2
    mlp_outs = [shape(512, 1024), shape(512, 1024, dtype=F32), shape(512, 1024), rowf, *halves]

    vec, h1_0, qkv_0, probs_0, o_0, keep, *send = run(
        with_scratch(first_attention, *vec_scratch, *weights_scratch, dist),
        [shape(16, 1024, dtype=F32)] + attention_outs, *blocks, *att_0, *segments, after=(token,), us=10,
    )
    far_down, pair_x, pair_y, deep, down_1, *send, _ = gate(
        (keep,), far_down, pair_x, pair_y, deep, down_1, *send
    )
    deep_far = swap(deep, "zh")
    part, came = summed_core(keep, *send)
    by_x, by_y, both, token = second_hops(
        mlp_0_message, 384, 384, far_up, far_down, pair_x, pair_y, after=(part,), rows=256
    )
    mlp_0 = (mlp_0, far_up, far_down, pair_x, pair_y, by_x, by_y, both)
    x1_0, *h = run(
        with_scratch(first_norm_stage, pltpu.VMEM((256, 1024), F32)),
        [rowf, *halves], blocks[0], blocks[2], part, came, vec, after=(token,), us=1.5,
    )
    h2_0, u_0, a_0, keep, *send = run(
        mlp_stage(0), mlp_outs, *with_other(h), *mlp_0, vec, after=(deep_far,), us=4
    )
    down_1_far = swap(down_1, "zh")
    to_x, to_y, to_both, mine = run(
        att_1_message, [shape(192, 1024)] * 2 + [shape(128, 1024), row],
        deep_far, pair_x, pair_y, deep, down_1, after=(keep,),
    )
    one_x, one_y, both = swap(to_x, "x"), swap(to_y, "y"), both_ways(to_both)
    att_1 = (deep, deep_far, pair_x, pair_y, one_x, one_y, both)
    part, came = summed_core(keep, *send)
    mine, token = gate((part, one_x, one_y), mine)
    near_x, near_y = swap(mine, "x"), swap(mine, "y")
    x2_0, *h = run(norm_stage(5, 8), [rowf, *halves], x1_0, part, came, vec, after=(token, down_1_far), us=1)
    (to_all,) = run(mlp_1_message, [row], deep_far, down_1_far, after=(both, near_x, near_y))
    by_x, by_y = swap(to_all, "x"), swap(to_all, "y")
    h1_1, qkv_1, probs_1, o_1, keep, *send = run(
        with_scratch(next_attention, *weights_scratch, dist),
        attention_outs, *with_other(h), *att_1, vec, *segments, after=(to_all,), us=9,
    )
    to_x, to_y = run(mlp_1_across, [shape(128, 1024)] * 2, near_x, near_y, after=(keep,))
    mlp_1 = (
        deep, down_1, deep_far, down_1_far, near_x, near_y, by_x, by_y,
        swap(to_x, "x"), swap(to_y, "y"), both_ways(to_all),
    )
    cot, _ = gate((keep,), cot)
    cot = corner(cot)
    part, came = summed_core(keep, *send, after=(by_x, by_y))
    x1_1, *h = run(norm_stage(10, 11), [rowf, *halves], x2_0, part, came, vec, after=(token,), us=1)
    by_zl = swap(cot, "zl")
    cots = (cot, swap(cot, "core"), by_zl, swap(by_zl, "core"))
    h2_1, u_1, a_1, keep, *send = run(mlp_stage(1), mlp_outs, *with_other(h), *mlp_1, vec, us=4)

    mlp_back_outs = [shape(512, 1024), shape(512, 1024), rowf, *halves]
    norm_outs = [rowf, *halves, shape(8, 1024, dtype=F32)]
    attention_back_outs = [shape(512, 1024), shape(512, 768), rowf, *halves]
    attention_back_scratch = weights_scratch + [
        pltpu.VMEM((512, 256), BF), pltpu.VMEM((512, 128), F32), pltpu.VMEM((512, 128), F32),
    ]

    def grad_outs(sent, rows):
        return [shape(sent, 1024)] * 2 + [shape(rows, 1024)] * 4

    out_scratch = pltpu.VMEM((256, 1024), BF)

    keep_last, send_last = keep, send
    part_last, came_last = split_core(keep_last, *send_last)
    gy2, gu_1, keep, *send = run(mlp_back(1), mlp_back_outs, *cots, u_1, *mlp_1, after=(part_last,), us=6)
    came_last, *send, _ = gate((keep,), came_last, *send)
    part, came = summed_core(keep, *send)
    to_y, to_x, m1_near_0, m1_near_1, m1_far_0, m1_far_1 = run(
        window_1, grad_outs(512, 256), h2_1, a_1, gy2, gu_1, after=(part,), us=4
    )
    y_1, x_1 = swap(to_y, "y"), swap(to_x, "x")
    gm, *gy, e1 = run(
        with_scratch(first_norm_back, pltpu.VMEM((256, 1024), F32)),
        norm_outs, cots[0], cots[2], part, came, x1_1, vec, after=(m1_far_1,), us=1.5,
    )
    gy1, gqkv_1, keep, *send = run(
        with_scratch(attention_back(1), *attention_back_scratch),
        attention_back_outs, *with_other(gy), qkv_1, probs_1, *att_1, us=9,
    )
    part, came = summed_core(keep, *send)
    (final,) = run(finish_rows, [shape(1, 128, 1024)], x1_1, part_last, came_last, vec)
    output = corner(final)
    to_y, to_x, a1_near_0, a1_near_1, a1_far_0, a1_far_1 = run(
        with_scratch(window_2, out_scratch), grad_outs(512, 128), h1_1, o_1, gy1, gqkv_1,
        m1_near_1, y_1, m1_far_1, x_1, after=(part, output), us=3,
    )
    y_2, x_2 = swap(to_y, "y"), swap(to_x, "x")
    gx, *gy, g1 = run(
        norm_back_stage(8), norm_outs, gm, part, came, x2_0, vec, after=(a1_far_1,), us=1.5
    )
    gy2, gu_0, keep, *send = run(
        mlp_back(0), mlp_back_outs, *with_other(gy), u_0, *mlp_0, us=6
    )
    part, came = summed_core(keep, *send)
    to_y, to_x, m0_near_0, m0_near_1, m0_far_0, m0_far_1, to_zh = run(
        window_3, grad_outs(640, 256) + [row], h2_0, a_0, gy2, gu_0,
        a1_near_1, y_2, a1_far_1, x_2, m1_far_0, x_1, after=(part,), us=4,
    )
    y_3, x_3, m1_far_3 = swap(to_y, "y"), swap(to_x, "x"), swap(to_zh, "zh")
    gm, *gy, e0 = run(
        norm_back_stage(3), norm_outs, gx, part, came, x1_0, vec, after=(m0_far_1,), us=1.5
    )
    gy1, gqkv_0, keep, *send = run(
        with_scratch(attention_back(0), *attention_back_scratch),
        attention_back_outs, *with_other(gy), qkv_0, probs_0, *att_0, us=9,
    )
    to_x, to_y, to_zh = run(
        window_4, [row, row, shape(128, 1024)], m0_near_1, y_3, m0_far_1, x_3, a1_far_0, x_2, after=(keep,)
    )
    x_4, y_4, a1_far_3 = swap(to_x, "x"), swap(to_y, "y"), swap(to_zh, "zh")
    part, came = split_core(keep, *send, after=(to_zh, m1_far_3))
    to_y, to_x, a0_near_0, a0_near_1, a0_far_0, a0_far_1 = run(
        with_scratch(window_5, out_scratch, *vec_scratch), grad_outs(288, 144),
        h1_0, o_0, gy1, gqkv_0, g1, e1, e0, gu_1, gu_0, gqkv_1, keep, *send, *blocks,
        after=(part, x_4, y_4), us=3,
    )
    y_5, x_5 = swap(to_y, "y"), swap(to_x, "x")
    (to_zh,) = run(third_only, [row], m0_far_0, x_3, y_4, after=(a0_far_1,))
    m0_far_3 = swap(to_zh, "zh")
    (grad,) = run(
        with_scratch(
            last_norm_back, *[pltpu.VMEM((128, 1024), F32)] * 3, pltpu.VMEM((128, 1024), BF),
            pltpu.VMEM((8, 1024), F32),
        ),
        [shape(1, 128, 1024)], gm, part, came, blocks[0], vec, after=(to_zh,), us=1.5,
    )
    tokens_grad = corner(grad).astype(F32)
    to_x, to_y = run(second_only, [shape(144, 1024)] * 2, a0_near_1, y_5, a0_far_1, x_5, after=(grad,))
    x_6, y_6 = swap(to_x, "x"), swap(to_y, "y")
    rest = run(
        unpack_first,
        [shape(32, 1792, dtype=F32)] + [shape(32, 1792)] * 3 + [shape(32, 512)] * 2
        + [shape(128, 1024, dtype=F32)],
        y_1, y_2, x_2, x_3, m1_near_0, m1_far_3, a1_near_0, a1_far_3, us=2,
    )
    rest_came = to_partners(rest[1:4])
    (to_zh,) = run(window_6, [shape(144, 1024)], a0_far_0, x_5, y_6, after=rest_came)
    a0_far_3 = swap(to_zh, "zh")
    last = run(
        unpack_last,
        [shape(48, 1792, dtype=F32)] + [shape(48, 1792)] * 3 + [shape(64, 512)] * 2
        + [shape(2, 128, 1024, dtype=F32)],
        y_3, y_5, x_4, x_6, m0_near_0, m0_far_3, a0_near_0, a0_far_3, rest[4], rest[5], rest[6],
        after=rest_came,
    )
    back_a = lax.ppermute(last[4], ("y", "zl"), [(0, 0), (1, 2), (2, 1), (3, 3)])
    back_b = lax.ppermute(last[5], ("y", "zl"), [(0, 1), (1, 3), (2, 0), (3, 2)])
    sizes = (
        (2, 32), (2, 32), (2, 32, 3072), (2, 64), (2, 32, 1024), (2, 32), (2, 32), (2, 32),
        (2, 32, 4096), (2, 128), (2, 32),
    )
    g = run(
        finish, [shape(*s, dtype=F32) for s in sizes],
        rest[0], *rest_came, last[0], *to_partners(last[1:4]), back_a, back_b, us=2,
    )
    return (output, tokens_grad) + tuple(g[:10]) + (last[6], g[10])


def solution(mesh):
    fsdp, ctx = mesh.shape["fsdp"], mesh.shape["ctx"]
    fine = Mesh(mesh.devices.reshape(fsdp // 4, 2, 2, 2, ctx // 2), AXES)
    body = narrow_body if fine.devices.shape == (2, 2, 2, 2, 2) else wide_body
    stream, place = ("y", "x", "core"), ("zh", "zl")
    rows = P(stream, place, None)
    flat, deep = P(None, AXES), P(None, AXES, None)
    params = (flat, flat, deep, flat, deep, flat, flat, flat, deep, flat, deep, flat)
    in_specs = (rows, P(stream, None), P()) + params + (rows,)
    out_specs = (rows, rows) + params
    return jax.shard_map(body, mesh=fine, in_specs=in_specs, out_specs=out_specs, check_vma=False)
```
